512 devices in a mesh: slab: 64 (over x, z), pen: 8 (over y, core).
Axes of the slice: x: 4, y: 4, z: 16, core: 2. Of those that a mesh axis runs over, the one named last changes fastest.
Arguments:
- pressure_rhs: float32 [256, 256, 256], P('slab', 'pen'), may hold values from -120 to 120
- permeability: float32 [256, 256, 256], P('slab', 'pen'), may hold values from 0.2 to 5
- accumulation: float32 [256, 256, 256], P('slab', 'pen'), may hold values from 1 to 8
- coarse_perm: float32 [128, 128, 128], P('slab', 'pen'), may hold values from 0.2 to 5
- coarse_accum: float32 [128, 128, 128], P('slab', 'pen'), may hold values from 1 to 8
- run_lengths: int32 [32], replicated, may hold values from 1 to 4, 64 in all
Outputs:
- updated_pressure: float32 [256, 256, 256], P('slab', 'pen')
The draws below stay inside these ranges and needn't reach their ends.
Inputs may be any that keep to these rules, and one draw needn't show every extreme that they name: `run_lengths`: runs are laid end to end over the blocks 0 to 63 in order and sum to 64; some run has exactly 4 blocks.
All inputs are finite; a program needn't handle non-finite values.
Results may differ from the reference program's by a relative error of at most 0.00002.
Values sent between devices are 32-bit elements; how exact they have to be, the bound alone decides.
No kernel may reach another device: no remote copies, remote signals or barrier semaphores. Data moves between devices by JAX's collectives and lax.ppermute only.
A program may use at most 64 MiB of HBM per device.

```python
import math
import jax
import jax.numpy as jnp
import numpy as np
from jax import lax

CZ = 4
NX = 256
PRE = 2
POST = 2
COARSE_SWEEPS = 6
MOST = 4
BLOCKS = 64
OWNERS = 32
NZ = 256
NY = 256


def block_levels(key, extent, pieces, low, high):
    def one(dim, shards_of):
        draws = jax.random.uniform(jax.random.fold_in(jax.random.fold_in(key, 6), dim), (shards_of,), jnp.float32, low / len(pieces), high / len(pieces))
        return jnp.repeat(jnp.exp(draws), extent[dim] // shards_of).reshape((-1,) + (1,) * (len(extent) - dim - 1))

    level = one(*pieces[0])
    for cut in pieces[1:]:
        level = level * one(*cut)
    return level


def profile(amount, total, bound, skew):
    loads = [(1 << 20) // math.isqrt(grade ** skew) + 1 for grade in range(2, amount + 1)]
    spare, given = total - bound - (amount - 1), [1] * (amount - 1)
    while spare > 0:
        candidates = [i for i in range(amount - 1) if given[i] < bound]
        whole, budget = sum([loads[i] for i in candidates]), spare
        for i in candidates:
            more = min(bound - given[i], max(1, budget * loads[i] // whole), spare)
            given[i] = given[i] + more
            spare = spare - more
    return np.array([bound] + given)


def uneven(own_key, number_of, total, most, skew):
    if number_of == 2:
        one = jax.random.randint(own_key, (), max(1, total - most), min(most, total - 1) + 1)
        return jnp.stack([one, total - one])
    tallies = jnp.asarray(profile(number_of, total, most, skew), jnp.int32)
    pairs = (number_of - 1) // 2
    source_of, sink = tallies[1:1 + 2 * pairs:2], tallies[2:2 + 2 * pairs:2]
    slack = jnp.minimum(source_of - 1, most - sink)
    passed = jax.random.randint(jax.random.fold_in(own_key, 1), (pairs,), 0, 1 << 20) % (slack + 1)
    tallies = tallies.at[1:1 + 2 * pairs:2].set(source_of - passed).at[2:2 + 2 * pairs:2].set(sink + passed)
    return tallies[jax.random.permutation(jax.random.fold_in(own_key, 2), number_of)]


def bell_draw(key, shape, width, reach, shards=(), kind=jnp.bfloat16):
    entries = jax.random.normal(key, shape, jnp.float32) * width
    if len(shards) > 0:
        entries = block_levels(key, shape, shards, -0.22, 0.18) * entries
    return jnp.clip(entries, min=-reach, max=reach).astype(kind)


def setup_inputs(seed: int = 0) -> dict:
    streams_of = jax.random.split(jax.random.key(seed), 7)
    pressure_rhs = bell_draw(streams_of[0], (NZ, NY, NX), 20.0, 120.0, ((0, 64), (1, 8)), jnp.float32)
    permeability = jnp.clip(jnp.exp(math.log(5.0) - 3.218876 * jax.random.uniform(streams_of[1], (NZ, NY, NX), jnp.float32) ** block_levels(streams_of[1], (NZ, NY, NX), ((0, 64), (1, 8)), -0.2, 0.2)), 0.2, 5.0)
    accumulation = jnp.clip(jnp.exp(math.log(8.0) - 2.0794415 * jax.random.uniform(streams_of[2], (NZ, NY, NX), jnp.float32) ** block_levels(streams_of[2], (NZ, NY, NX), ((0, 64), (1, 8)), -0.2, 0.2)), 1.0, 8.0)
    coarse_perm = jnp.clip(jnp.exp(math.log(5.0) - 3.218876 * jax.random.uniform(streams_of[3], (NZ // 2, NY // 2, NX // 2), jnp.float32) ** block_levels(streams_of[3], (NZ // 2, NY // 2, NX // 2), ((0, 64), (1, 8)), -0.2, 0.2)), 0.2, 5.0)
    coarse_accum = jnp.clip(jnp.exp(math.log(8.0) - 2.0794415 * jax.random.uniform(streams_of[4], (NZ // 2, NY // 2, NX // 2), jnp.float32) ** block_levels(streams_of[4], (NZ // 2, NY // 2, NX // 2), ((0, 64), (1, 8)), -0.2, 0.2)), 1.0, 8.0)
    run_lengths = uneven(streams_of[5], OWNERS, BLOCKS, MOST, 1).astype(jnp.int32)
    return dict(pressure_rhs=pressure_rhs, permeability=permeability, accumulation=accumulation, coarse_perm=coarse_perm, coarse_accum=coarse_accum, run_lengths=run_lengths)


OMEGA = 0.7

def neighbours(extended, lower_mask, upper_mask):
    plane_count = extended.shape[0] - 2
    row_count = extended.shape[1] - 2
    col_count = extended.shape[2] - 2
    layers = []
    for off_z in (-1, 0, 1):
        summed = jnp.zeros((plane_count, row_count, col_count), jnp.float32)
        for off_y in (-1, 0, 1):
            for off_x in (-1, 0, 1):
                distance = abs(off_z) + abs(off_y) + abs(off_x)
                if distance == 0:
                    continue
                weight = 0.5 ** (distance - 1)
                summed = summed + weight * extended[1 + off_z:1 + off_z + plane_count, 1 + off_y:1 + off_y + row_count, 1 + off_x:1 + off_x + col_count]
        layers.append(summed)
    return lower_mask * layers[0] + layers[1] + upper_mask * layers[2]

def operate(pressure, trans, diag, lower_mask, upper_mask):
    return diag * pressure - trans * neighbours(jnp.pad(trans * pressure, 1), lower_mask, upper_mask)

def reference(pressure_rhs, permeability, accumulation, coarse_perm, coarse_accum, run_lengths):
    trans = jnp.sqrt(permeability)
    diag = trans * neighbours(jnp.pad(trans, 1), 1.0, 1.0) + accumulation
    pressure = OMEGA * pressure_rhs / diag
    for sweep_step in range(PRE - 1):
        pressure = pressure + OMEGA * (pressure_rhs - operate(pressure, trans, diag, 1.0, 1.0)) / diag
    residual = pressure_rhs - operate(pressure, trans, diag, 1.0, 1.0)
    half_depth = NZ // 2
    half_rows = NY // 2
    half_cols = NX // 2
    coarse_res = residual.reshape(half_depth, 2, half_rows, 2, half_cols, 2).sum(axis=(1, 3, 5))
    coarse_trans = jnp.sqrt(coarse_perm)
    coarse_diag = coarse_trans * neighbours(jnp.pad(coarse_trans, 1), 1.0, 1.0) + coarse_accum
    ends = jnp.cumsum(run_lengths).astype(jnp.int32)
    starts = ends - run_lengths
    slab_ids = jnp.arange(BLOCKS, dtype=jnp.int32)
    run_of_slab = lax.optimization_barrier(jnp.sum((starts[None, :] <= slab_ids[:, None]).astype(jnp.int32), axis=1)) - 1
    plane_run = jnp.repeat(run_of_slab, CZ // 2)
    same_run = (plane_run[1:] == plane_run[:-1]).astype(jnp.float32)
    lower_mask = jnp.concatenate([jnp.zeros((1,), jnp.float32), same_run])[:, None, None]
    upper_mask = jnp.concatenate([same_run, jnp.zeros((1,), jnp.float32)])[:, None, None]
    estimate = OMEGA * coarse_res / coarse_diag
    for sweep_step in range(COARSE_SWEEPS - 1):
        estimate = estimate + OMEGA * (coarse_res - operate(estimate, coarse_trans, coarse_diag, lower_mask, upper_mask)) / coarse_diag
    prolonged = jnp.broadcast_to(estimate[:, None, :, None, :, None], (half_depth, 2, half_rows, 2, half_cols, 2)).reshape(NZ, NY, NX)
    pressure = pressure + prolonged
    for sweep_step in range(POST):
        pressure = pressure + OMEGA * (pressure_rhs - operate(pressure, trans, diag, 1.0, 1.0)) / diag
    return pressure
```

```python
import jax
import jax.numpy as jnp
from jax import lax
from jax.experimental import pallas as pl
from jax.experimental.pallas import tpu as pltpu
from jax.sharding import PartitionSpec as P

OMEGA = 0.7
KEEP = 1.0 - OMEGA
COARSE_SWEEPS = 6

FR = 40
ROWS = 32
COLS = 256
CR = 32
CROWS = 16
CCOLS = 128


def shifted(x, axis, by):
    devices = lax.axis_size(axis)
    pairs = [(i, i + by) for i in range(devices) if 0 <= i + by < devices]
    return lax.ppermute(x, axis, pairs)


def rotated(x, axis, by):
    devices = lax.axis_size(axis)
    return lax.ppermute(x, axis, [(i, (i + by) % devices) for i in range(devices)])


def smooth_xy(v):
    rows, cols = v.shape
    col = lax.broadcasted_iota(jnp.int32, v.shape, 1)
    left = jnp.where(col == 0, 0.0, pltpu.roll(v, 1, 1))
    right = jnp.where(col == cols - 1, 0.0, pltpu.roll(v, cols - 1, 1))
    h = v + 0.5 * (left + right)
    return h + 0.5 * (pltpu.roll(h, 1, 0) + pltpu.roll(h, rows - 1, 0))


def to_wide(x):
    return jnp.concatenate([x[0:8], x[8:16]], axis=1)


def from_wide(x):
    return jnp.concatenate([x[:, 0:CCOLS], x[:, CCOLS:COLS]], axis=0)


Z1_RHS = 96
Z1_ACC = 160
Z1_CO = 224
Z1_ROWS = 232


def pack_z1(rhs, perm, acc, cperm, up, down):
    for out, first3, first2, coarse in ((up, 1, 2, 1), (down, 0, 0, 0)):
        for k in range(3):
            out[32 * k : 32 * k + 32, :] = perm[first3 + k]
        for k in range(2):
            out[Z1_RHS + 32 * k : Z1_RHS + 32 * k + 32, :] = rhs[first2 + k]
            out[Z1_ACC + 32 * k : Z1_ACC + 32 * k + 32, :] = acc[first2 + k]
        out[Z1_CO : Z1_CO + 8, :] = to_wide(cperm[coarse])


def fine_rows(own, lo, hi, base, depth, z, first, count):
    if z < 0:
        at = base + 32 * (z + depth)
        return lo[at + first : at + first + count, :]
    if z > 3:
        at = base + 32 * (z - 4)
        return hi[at + first : at + first + count, :]
    return own[z, first : first + count, :]


def coarse_plane(cperm, lo, hi, c):
    if c < 0:
        return from_wide(lo[Z1_CO : Z1_CO + 8, :])
    if c > 1:
        return from_wide(hi[Z1_CO : Z1_CO + 8, :])
    return cperm[c]


Y1_RHS = 30
Y1_ACC = 46
Y1_CO = 62
Y1_ROWS = 64


def pack_y1(rhs, perm, acc, cperm, lo, hi, up, down):
    for out, top in ((up, True), (down, False)):
        r3 = ROWS - 3 if top else 0
        r2 = ROWS - 2 if top else 0
        for k in range(10):
            out[3 * k : 3 * k + 3, :] = fine_rows(perm, lo, hi, 0, 3, k - 3, r3, 3)
        for k in range(8):
            at = Y1_RHS + 2 * k
            out[at : at + 2, :] = fine_rows(rhs, lo, hi, Z1_RHS, 2, k - 2, r2, 2)
            at = Y1_ACC + 2 * k
            out[at : at + 2, :] = fine_rows(acc, lo, hi, Z1_ACC, 2, k - 2, r2, 2)
        rc = CROWS - 1 if top else 0
        for k in range(4):
            plane = coarse_plane(cperm, lo, hi, k - 1)
            at = Y1_CO + k // 2
            lane = CCOLS * (k % 2)
            out[at : at + 1, lane : lane + CCOLS] = plane[rc : rc + 1, :]


def pre_kernel(
    masks, rhs, perm, acc, cperm, cacc, lo, hi, ylo, yhi,
    t_out, a_out, b_out, u_out, ct_out, ab_out, zup, zdn,
    ts, rs, cs, xs, us, ds, fs,
):
    mlo = masks[0]
    mhi = masks[1]
    zeros = jnp.zeros((FR, COLS), jnp.float32)
    for k in range(10):
        z = k - 3
        ts[k] = zeros
        ts[k, 4:36, :] = jnp.sqrt(fine_rows(perm, lo, hi, 0, 3, z, 0, ROWS))
        ts[k, 1:4, :] = jnp.sqrt(ylo[3 * k : 3 * k + 3, :] * mlo)
        ts[k, 36:39, :] = jnp.sqrt(yhi[3 * k : 3 * k + 3, :] * mhi)
    for k in range(8):
        z = k - 2
        for ref, own, base, ybase in ((rs, rhs, Z1_RHS, Y1_RHS), (cs, acc, Z1_ACC, Y1_ACC)):
            ref[k] = zeros
            ref[k, 4:36, :] = fine_rows(own, lo, hi, base, 2, z, 0, ROWS)
            ref[k, 2:4, :] = ylo[ybase + 2 * k : ybase + 2 * k + 2, :] * mlo
            ref[k, 36:38, :] = yhi[ybase + 2 * k : ybase + 2 * k + 2, :] * mhi
    for k in range(10):
        xs[k] = smooth_xy(ts[k])
    for k in range(8):
        t = ts[k + 1]
        w = 2.0 * (xs[k + 1] + 0.5 * (xs[k] + xs[k + 2]) - t)
        d = t * w + cs[k]
        d = jnp.where(d > 0.0, d, 1.0)
        q = OMEGA * t / d
        if 2 <= k < 6:
            ds[k - 2] = d
        t_out[k] = t
        rs_k = rs[k]
        us[k] = q * rs_k
        cs[k] = q * t
    for k in range(8):
        xs[k] = smooth_xy(us[k])
    for k in range(6):
        a = us[k + 1]
        b = cs[k + 1]
        w = 2.0 * (xs[k + 1] + 0.5 * (xs[k] + xs[k + 2]) - a)
        a_out[k] = a
        b_out[k] = b
        u_out[k] = (1.0 + KEEP) * a + b * w
    for k in range(6):
        xs[k] = smooth_xy(u_out[k])
    sums = []
    for k in range(4):
        u = u_out[k + 1]
        t = ts[k + 3]
        w = 2.0 * (xs[k + 1] + 0.5 * (xs[k] + xs[k + 2]) - u)
        r = rs[k + 2] + t * w - ds[k] * (u / t)
        sums.append(r)
    pairs = []
    for k in range(2):
        both = sums[2 * k] + sums[2 * k + 1]
        halves = []
        for half in range(2):
            at = 2 * k + half
            fs[at] = both[:, CCOLS * half : CCOLS * half + CCOLS]
            halves.append(fs[at, pl.ds(4, CROWS, 2), :] + fs[at, pl.ds(5, CROWS, 2), :])
        pairs.append(jnp.concatenate(halves, axis=1))
    stacked = jnp.concatenate(pairs, axis=0)
    src = lax.broadcasted_iota(jnp.int32, (COLS, CCOLS), 0)
    dst = lax.broadcasted_iota(jnp.int32, (COLS, CCOLS), 1)
    fold = jnp.where(src // 2 == dst, 1.0, 0.0)
    res = jnp.dot(
        stacked, fold, precision=lax.Precision.HIGHEST, preferred_element_type=jnp.float32
    )
    for k in range(4):
        ct_out[k] = jnp.zeros((CR, CCOLS), jnp.float32)
        ct_out[k, 8:24, :] = jnp.sqrt(coarse_plane(cperm, lo, hi, k - 1))
        at = Y1_CO + k // 2
        lane = CCOLS * (k % 2)
        ct_out[k, 7:8, :] = jnp.sqrt(ylo[at : at + 1, lane : lane + CCOLS] * mlo)
        ct_out[k, 24:25, :] = jnp.sqrt(yhi[at : at + 1, lane : lane + CCOLS] * mhi)
    cx = [smooth_xy(ct_out[k]) for k in range(4)]
    for k in range(2):
        t = ct_out[k + 1]
        w = 2.0 * (cx[k + 1] + 0.5 * (cx[k] + cx[k + 2]) - t)
        t = t[8:24]
        d = t * w[8:24] + cacc[k]
        q = OMEGA * t / d
        a = q * res[CROWS * k : CROWS * k + CROWS]
        b = q * t
        for out in (ab_out, zup, zdn):
            out[k] = a
            out[2 + k] = b
    for out, plane in ((zup, 3), (zdn, 2)):
        for k in range(4):
            row = 4 + 16 * (k // 2)
            lane = CCOLS * (k % 2)
            out[4 + k] = u_out[plane, row : row + 16, lane : lane + CCOLS]


Y2_B = 112
Y2_U = 208
Y2_ROWS = 240


def coarse_a(ab, r3lo, r3hi, r4lo, r4hi, c):
    if c < -4:
        return r4lo.at[c + 10]
    if c < -2:
        return r4lo.at[c + 4]
    if c < 0:
        return r3lo.at[c + 2]
    if c < 2:
        return ab.at[c]
    if c < 4:
        return r3hi.at[c - 2]
    if c < 6:
        return r4hi.at[c - 4]
    return r4hi.at[c - 2]


def coarse_b(ab, r3lo, r3hi, r4lo, r4hi, c):
    if c == -5:
        return r4lo.at[6]
    if c < -2:
        return r4lo.at[c + 6]
    if c < 0:
        return r3lo.at[c + 4]
    if c < 2:
        return ab.at[c + 2]
    if c < 4:
        return r3hi.at[c]
    if c < 6:
        return r4hi.at[c - 2]
    return r4hi.at[6]


def pack_y2(ab, u, r3lo, r3hi, r4lo, r4hi, up, down):
    for out, top in ((up, True), (down, False)):
        first = 8 if top else 0
        for k in range(14):
            plane = coarse_a(ab, r3lo, r3hi, r4lo, r4hi, k - 6)
            out[8 * k : 8 * k + 8, :] = plane[first : first + 8, :]
        for k in range(12):
            plane = coarse_b(ab, r3lo, r3hi, r4lo, r4hi, k - 5)
            out[Y2_B + 8 * k : Y2_B + 8 * k + 8, :] = plane[first : first + 8, :]
        for k in range(8):
            at = Y2_U + 4 * k
            for half in range(2):
                if 0 < k < 7:
                    row = 34 if top else 4
                    rows = u[k - 1, row : row + 2, CCOLS * half : CCOLS * half + CCOLS]
                else:
                    edge = r3lo if k == 0 else r3hi
                    if top:
                        rows = edge[6 + half, 14:16, :]
                    else:
                        rows = edge[4 + half, 0:2, :]
                out[at + 2 * half : at + 2 * half + 2, :] = rows


def post_kernel(
    masks, t_in, a_in, b_in, u_in, ct, ab, r3lo, r3hi, r4lo, r4hi, ylo, yhi,
    out, uf, cf, xs,
):
    mlo = masks[0]
    mhi = masks[1]
    a = []
    for k in range(14):
        own = coarse_a(ab, r3lo, r3hi, r4lo, r4hi, k - 6)[...]
        lo = ylo[8 * k : 8 * k + 8, :] * mlo
        hi = yhi[8 * k : 8 * k + 8, :] * mhi
        a.append(jnp.concatenate([lo, own, hi], axis=0))
    b = [None]
    for k in range(12):
        own = coarse_b(ab, r3lo, r3hi, r4lo, r4hi, k - 5)[...]
        lo = ylo[Y2_B + 8 * k : Y2_B + 8 * k + 8, :] * mlo
        hi = yhi[Y2_B + 8 * k : Y2_B + 8 * k + 8, :] * mhi
        b.append(jnp.concatenate([lo, own, hi], axis=0))
    link = [0.5] * 13
    for j in range(6):
        link[2 * j + 1] = 0.5 * masks[2 + j]
    u = list(a)
    for sweep in range(1, COARSE_SWEEPS):
        first, last = sweep, 13 - sweep
        smooth = {k: smooth_xy(u[k]) for k in range(first - 1, last + 2)}
        fresh = list(u)
        for k in range(first, last + 1):
            w = 2.0 * (
                smooth[k] + link[k - 1] * smooth[k - 1] + link[k] * smooth[k + 1] - u[k]
            )
            fresh[k] = KEEP * u[k] + a[k] + b[k] * w
        u = fresh
    corr = []
    for k in range(4):
        t = ct[k]
        inside = t > 0.0
        corr.append(jnp.where(inside, u[5 + k] / jnp.where(inside, t, 1.0), 0.0))
    stacked = jnp.concatenate(corr, axis=0)
    dst = lax.broadcasted_iota(jnp.int32, (CCOLS, COLS), 1)
    src = lax.broadcasted_iota(jnp.int32, (CCOLS, COLS), 0)
    spread = jnp.where(dst // 2 == src, 1.0, 0.0)
    wide = jnp.dot(
        stacked, spread, precision=lax.Precision.HIGHEST, preferred_element_type=jnp.float32
    )
    for k in range(4):
        for half in range(2):
            rows = wide[CR * k + 6 : CR * k + 26, CCOLS * half : CCOLS * half + CCOLS]
            cf[2 * k + half, pl.ds(0, 20, 2), :] = rows
            cf[2 * k + half, pl.ds(1, 20, 2), :] = rows
    zeros = jnp.zeros((FR, COLS), jnp.float32)
    for k in range(8):
        if 0 < k < 7:
            uf[k] = u_in[k - 1]
        else:
            uf[k] = zeros
            edge = r3lo if k == 0 else r3hi
            for j in range(4):
                row = 4 + 16 * (j // 2)
                lane = CCOLS * (j % 2)
                uf[k, row : row + 16, lane : lane + CCOLS] = edge[4 + j]
        at = Y2_U + 4 * k
        for half in range(2):
            lane = CCOLS * half
            uf[k, 2:4, lane : lane + CCOLS] = ylo[at + 2 * half : at + 2 * half + 2, :] * mlo
            uf[k, 36:38, lane : lane + CCOLS] = yhi[at + 2 * half : at + 2 * half + 2, :] * mhi
        both = 2 * (k // 2)
        uf[k] = uf[k] + t_in[k] * jnp.concatenate([cf[both], cf[both + 1]], axis=1)
    for k in range(8):
        xs[k] = smooth_xy(uf[k])
    for k in range(6):
        v = uf[k + 1]
        w = 2.0 * (xs[k + 1] + 0.5 * (xs[k] + xs[k + 2]) - v)
        uf[k + 1] = KEEP * v + a_in[k] + b_in[k] * w
    for k in range(6):
        xs[k] = smooth_xy(uf[k + 1])
    for k in range(4):
        v = uf[k + 2]
        w = 2.0 * (xs[k + 1] + 0.5 * (xs[k] + xs[k + 2]) - v)
        new = KEEP * v + a_in[k + 1] + b_in[k + 1] * w
        uf[k + 2] = new / t_in[k + 2]
        out[k] = uf[k + 2, 4:36, :]


VM = pl.BlockSpec(memory_space=pltpu.VMEM)
SM = pl.BlockSpec(memory_space=pltpu.SMEM)


def f32(*shape):
    return jax.ShapeDtypeStruct(shape, jnp.float32)


def call(kernel, specs, outs, scratch=()):
    return pl.pallas_call(
        kernel,
        in_specs=specs,
        out_specs=jax.tree.map(lambda _: VM, outs),
        out_shape=outs,
        scratch_shapes=[pltpu.VMEM(shape, jnp.float32) for shape in scratch],
    )


def on_device(pressure_rhs, permeability, accumulation, coarse_perm, coarse_accum, run_lengths):
    up, down = call(
        pack_z1, [VM] * 4, (f32(Z1_ROWS, COLS), f32(Z1_ROWS, COLS))
    )(pressure_rhs, permeability, accumulation, coarse_perm)
    lo = shifted(up, "slab", 1)
    hi = shifted(down, "slab", -1)

    slab = lax.axis_index("slab")
    pen = lax.axis_index("pen")
    starts = jnp.cumsum(run_lengths) - run_lengths
    blocks = slab - 2 + jnp.arange(6, dtype=jnp.int32)
    begins = jnp.any(starts[None, :] == blocks[:, None], axis=1)
    masks = jnp.concatenate(
        [
            jnp.stack([pen > 0, pen < lax.axis_size("pen") - 1]).astype(jnp.float32),
            1.0 - begins.astype(jnp.float32),
        ]
    )

    up, down = call(
        pack_y1, [VM] * 6, (f32(Y1_ROWS, COLS), f32(Y1_ROWS, COLS))
    )(pressure_rhs, permeability, accumulation, coarse_perm, lo, hi)
    ylo = rotated(up, "pen", 1)
    yhi = rotated(down, "pen", -1)

    t, a, b, u, ct, ab, zup, zdn = call(
        pre_kernel,
        [SM] + [VM] * 9,
        (
            f32(8, FR, COLS), f32(6, FR, COLS), f32(6, FR, COLS), f32(6, FR, COLS),
            f32(4, CR, CCOLS), f32(4, CROWS, CCOLS),
            f32(8, CROWS, CCOLS), f32(8, CROWS, CCOLS),
        ),
        (
            (10, FR, COLS), (8, FR, COLS), (8, FR, COLS),
            (10, FR, COLS), (8, FR, COLS), (4, FR, COLS), (4, FR, CCOLS),
        ),
    )(masks, pressure_rhs, permeability, accumulation, coarse_perm, coarse_accum, lo, hi, ylo, yhi)
    r3lo = shifted(zup, "slab", 1)
    r3hi = shifted(zdn, "slab", -1)

    r4lo = shifted(jnp.concatenate([ab, r3lo[0:2], r3lo[3:4]], axis=0), "slab", 2)
    r4hi = shifted(jnp.concatenate([ab, r3hi[0:3]], axis=0), "slab", -2)

    up, down = call(
        pack_y2, [VM] * 6, (f32(Y2_ROWS, CCOLS), f32(Y2_ROWS, CCOLS))
    )(ab, u, r3lo, r3hi, r4lo, r4hi)
    ylo = rotated(up, "pen", 1)
    yhi = rotated(down, "pen", -1)

    return call(
        post_kernel,
        [SM] + [VM] * 12,
        f32(4, ROWS, COLS),
        ((8, FR, COLS), (8, FR, CCOLS), (8, FR, COLS)),
    )(masks, t, a, b, u, ct, ab, r3lo, r3hi, r4lo, r4hi, ylo, yhi)


def solution(mesh):
    return jax.shard_map(
        on_device,
        mesh=mesh,
        in_specs=(
            P("slab", "pen", None),
            P("slab", "pen", None),
            P("slab", "pen", None),
            P("slab", "pen", None),
            P("slab", "pen", None),
            P(),
        ),
        out_specs=P("slab", "pen", None),
        check_vma=False,
    )
```

```python
import jax
import jax.numpy as jnp
from jax import lax
from jax.experimental import pallas as pl
from jax.experimental.pallas import tpu as pltpu
from jax.sharding import PartitionSpec as P

OMEGA = 0.7
KEEP = 1.0 - OMEGA
COARSE_SWEEPS = 6

FR = 40
ROWS = 32
COLS = 256
CR = 32
CROWS = 16
CCOLS = 128


def shifted(x, axis, by):
    devices = lax.axis_size(axis)
    pairs = [(i, i + by) for i in range(devices) if 0 <= i + by < devices]
    return lax.ppermute(x, axis, pairs)


def rotated(x, axis, by):
    devices = lax.axis_size(axis)
    return lax.ppermute(x, axis, [(i, (i + by) % devices) for i in range(devices)])


def smooth_xy(v):
    rows, cols = v.shape
    col = lax.broadcasted_iota(jnp.int32, v.shape, 1)
    left = jnp.where(col == 0, 0.0, pltpu.roll(v, 1, 1))
    right = jnp.where(col == cols - 1, 0.0, pltpu.roll(v, cols - 1, 1))
    h = v + 0.5 * (left + right)
    return h + 0.5 * (pltpu.roll(h, 1, 0) + pltpu.roll(h, rows - 1, 0))


def to_wide(x):
    return jnp.concatenate([x[0:8], x[8:16]], axis=1)


def from_wide(x):
    return jnp.concatenate([x[:, 0:CCOLS], x[:, CCOLS:COLS]], axis=0)


Z1_RHS = 96
Z1_ACC = 160
Z1_CO = 224
Z1_ROWS = 232


def pack_z1(rhs, perm, acc, cperm, up, down):
    for out, first3, first2, coarse in ((up, 1, 2, 1), (down, 0, 0, 0)):
        for k in range(3):
            out[32 * k : 32 * k + 32, :] = perm[first3 + k]
        for k in range(2):
            out[Z1_RHS + 32 * k : Z1_RHS + 32 * k + 32, :] = rhs[first2 + k]
            out[Z1_ACC + 32 * k : Z1_ACC + 32 * k + 32, :] = acc[first2 + k]
        out[Z1_CO : Z1_CO + 8, :] = to_wide(cperm[coarse])


def fine_rows(own, lo, hi, base, depth, z, first, count):
    if z < 0:
        at = base + 32 * (z + depth)
        return lo[at + first : at + first + count, :]
    if z > 3:
        at = base + 32 * (z - 4)
        return hi[at + first : at + first + count, :]
    return own[z, first : first + count, :]


def coarse_plane(cperm, lo, hi, c):
    if c < 0:
        return from_wide(lo[Z1_CO : Z1_CO + 8, :])
    if c > 1:
        return from_wide(hi[Z1_CO : Z1_CO + 8, :])
    return cperm[c]


Y1_RHS = 30
Y1_ACC = 46
Y1_CO = 62
Y1_ROWS = 64


def pack_y1(rhs, perm, acc, cperm, lo, hi, up, down):
    for out, top in ((up, True), (down, False)):
        r3 = ROWS - 3 if top else 0
        r2 = ROWS - 2 if top else 0
        for k in range(10):
            out[3 * k : 3 * k + 3, :] = fine_rows(perm, lo, hi, 0, 3, k - 3, r3, 3)
        for k in range(8):
            at = Y1_RHS + 2 * k
            out[at : at + 2, :] = fine_rows(rhs, lo, hi, Z1_RHS, 2, k - 2, r2, 2)
            at = Y1_ACC + 2 * k
            out[at : at + 2, :] = fine_rows(acc, lo, hi, Z1_ACC, 2, k - 2, r2, 2)
        rc = CROWS - 1 if top else 0
        for k in range(4):
            plane = coarse_plane(cperm, lo, hi, k - 1)
            at = Y1_CO + k // 2
            lane = CCOLS * (k % 2)
            out[at : at + 1, lane : lane + CCOLS] = plane[rc : rc + 1, :]


def pre_kernel(
    masks, rhs, perm, acc, cperm, cacc, lo, hi, ylo, yhi,
    t_out, a_out, b_out, u_out, ct_out, ab_out, zup, zdn,
    ts, rs, cs, xs, us, ds, fs,
):
    mlo = masks[0]
    mhi = masks[1]
    zeros = jnp.zeros((FR, COLS), jnp.float32)
    for k in range(10):
        z = k - 3
        ts[k] = zeros
        ts[k, 4:36, :] = jnp.sqrt(fine_rows(perm, lo, hi, 0, 3, z, 0, ROWS))
        ts[k, 1:4, :] = jnp.sqrt(ylo[3 * k : 3 * k + 3, :] * mlo)
        ts[k, 36:39, :] = jnp.sqrt(yhi[3 * k : 3 * k + 3, :] * mhi)
    for k in range(8):
        z = k - 2
        for ref, own, base, ybase in ((rs, rhs, Z1_RHS, Y1_RHS), (cs, acc, Z1_ACC, Y1_ACC)):
            ref[k] = zeros
            ref[k, 4:36, :] = fine_rows(own, lo, hi, base, 2, z, 0, ROWS)
            ref[k, 2:4, :] = ylo[ybase + 2 * k : ybase + 2 * k + 2, :] * mlo
            ref[k, 36:38, :] = yhi[ybase + 2 * k : ybase + 2 * k + 2, :] * mhi
    for k in range(10):
        xs[k] = smooth_xy(ts[k])
    for k in range(8):
        t = ts[k + 1]
        w = 2.0 * (xs[k + 1] + 0.5 * (xs[k] + xs[k + 2]) - t)
        d = t * w + cs[k]
        d = jnp.where(d > 0.0, d, 1.0)
        q = OMEGA * t / d
        if 2 <= k < 6:
            ds[k - 2] = d
        t_out[k] = t
        rs_k = rs[k]
        us[k] = q * rs_k
        cs[k] = q * t
    for k in range(8):
        xs[k] = smooth_xy(us[k])
    for k in range(6):
        a = us[k + 1]
        b = cs[k + 1]
        w = 2.0 * (xs[k + 1] + 0.5 * (xs[k] + xs[k + 2]) - a)
        a_out[k] = a
        b_out[k] = b
        u_out[k] = (1.0 + KEEP) * a + b * w
    for k in range(6):
        xs[k] = smooth_xy(u_out[k])
    sums = []
    for k in range(4):
        u = u_out[k + 1]
        t = ts[k + 3]
        w = 2.0 * (xs[k + 1] + 0.5 * (xs[k] + xs[k + 2]) - u)
        r = rs[k + 2] + t * w - ds[k] * (u / t)
        sums.append(r)
    pairs = []
    for k in range(2):
        both = sums[2 * k] + sums[2 * k + 1]
        halves = []
        for half in range(2):
            at = 2 * k + half
            fs[at] = both[:, CCOLS * half : CCOLS * half + CCOLS]
            halves.append(fs[at, pl.ds(4, CROWS, 2), :] + fs[at, pl.ds(5, CROWS, 2), :])
        pairs.append(jnp.concatenate(halves, axis=1))
    stacked = jnp.concatenate(pairs, axis=0)
    src = lax.broadcasted_iota(jnp.int32, (COLS, CCOLS), 0)
    dst = lax.broadcasted_iota(jnp.int32, (COLS, CCOLS), 1)
    fold = jnp.where(src // 2 == dst, 1.0, 0.0)
    res = jnp.dot(
        stacked, fold, precision=lax.Precision.HIGHEST, preferred_element_type=jnp.float32
    )
    for k in range(4):
        ct_out[k] = jnp.zeros((CR, CCOLS), jnp.float32)
        ct_out[k, 8:24, :] = jnp.sqrt(coarse_plane(cperm, lo, hi, k - 1))
        at = Y1_CO + k // 2
        lane = CCOLS * (k % 2)
        ct_out[k, 7:8, :] = jnp.sqrt(ylo[at : at + 1, lane : lane + CCOLS] * mlo)
        ct_out[k, 24:25, :] = jnp.sqrt(yhi[at : at + 1, lane : lane + CCOLS] * mhi)
    cx = [smooth_xy(ct_out[k]) for k in range(4)]
    for k in range(2):
        t = ct_out[k + 1]
        w = 2.0 * (cx[k + 1] + 0.5 * (cx[k] + cx[k + 2]) - t)
        t = t[8:24]
        d = t * w[8:24] + cacc[k]
        q = OMEGA * t / d
        a = q * res[CROWS * k : CROWS * k + CROWS]
        b = q * t
        for out in (ab_out, zup, zdn):
            out[k] = a
            out[2 + k] = b
    for out, plane in ((zup, 3), (zdn, 2)):
        for k in range(4):
            row = 4 + 16 * (k // 2)
            lane = CCOLS * (k % 2)
            out[4 + k] = u_out[plane, row : row + 16, lane : lane + CCOLS]


Y2_B = 112
Y2_U = 208
Y2_ROWS = 240


def coarse_a(ab, r3lo, r3hi, r4lo, r4hi, c):
    if c < -4:
        return r4lo.at[c + 10]
    if c < -2:
        return r4lo.at[c + 4]
    if c < 0:
        return r3lo.at[c + 2]
    if c < 2:
        return ab.at[c]
    if c < 4:
        return r3hi.at[c - 2]
    if c < 6:
        return r4hi.at[c - 4]
    return r4hi.at[c - 2]


def coarse_b(ab, r3lo, r3hi, r4lo, r4hi, c):
    if c == -5:
        return r4lo.at[6]
    if c < -2:
        return r4lo.at[c + 6]
    if c < 0:
        return r3lo.at[c + 4]
    if c < 2:
        return ab.at[c + 2]
    if c < 4:
        return r3hi.at[c]
    if c < 6:
        return r4hi.at[c - 2]
    return r4hi.at[6]


def pack_y2(ab, u, r3lo, r3hi, r4lo, r4hi, up, down):
    for out, top in ((up, True), (down, False)):
        first = 8 if top else 0
        for k in range(14):
            plane = coarse_a(ab, r3lo, r3hi, r4lo, r4hi, k - 6)
            out[8 * k : 8 * k + 8, :] = plane[first : first + 8, :]
        for k in range(12):
            plane = coarse_b(ab, r3lo, r3hi, r4lo, r4hi, k - 5)
            out[Y2_B + 8 * k : Y2_B + 8 * k + 8, :] = plane[first : first + 8, :]
        for k in range(8):
            at = Y2_U + 4 * k
            for half in range(2):
                if 0 < k < 7:
                    row = 34 if top else 4
                    rows = u[k - 1, row : row + 2, CCOLS * half : CCOLS * half + CCOLS]
                else:
                    edge = r3lo if k == 0 else r3hi
                    if top:
                        rows = edge[6 + half, 14:16, :]
                    else:
                        rows = edge[4 + half, 0:2, :]
                out[at + 2 * half : at + 2 * half + 2, :] = rows


def post_kernel(
    masks, t_in, a_in, b_in, u_in, ct, ab, r3lo, r3hi, r4lo, r4hi, ylo, yhi,
    out, uf, cf, xs,
):
    mlo = masks[0]
    mhi = masks[1]
    a = []
    for k in range(14):
        own = coarse_a(ab, r3lo, r3hi, r4lo, r4hi, k - 6)[...]
        lo = ylo[8 * k : 8 * k + 8, :] * mlo
        hi = yhi[8 * k : 8 * k + 8, :] * mhi
        a.append(jnp.concatenate([lo, own, hi], axis=0))
    b = [None]
    for k in range(12):
        own = coarse_b(ab, r3lo, r3hi, r4lo, r4hi, k - 5)[...]
        lo = ylo[Y2_B + 8 * k : Y2_B + 8 * k + 8, :] * mlo
        hi = yhi[Y2_B + 8 * k : Y2_B + 8 * k + 8, :] * mhi
        b.append(jnp.concatenate([lo, own, hi], axis=0))
    link = [0.5] * 13
    for j in range(6):
        link[2 * j + 1] = 0.5 * masks[2 + j]
    u = list(a)
    for sweep in range(1, COARSE_SWEEPS):
        first, last = sweep, 13 - sweep
        smooth = {k: smooth_xy(u[k]) for k in range(first - 1, last + 2)}
        fresh = list(u)
        for k in range(first, last + 1):
            w = 2.0 * (
                smooth[k] + link[k - 1] * smooth[k - 1] + link[k] * smooth[k + 1] - u[k]
            )
            fresh[k] = KEEP * u[k] + a[k] + b[k] * w
        u = fresh
    corr = []
    for k in range(4):
        t = ct[k]
        inside = t > 0.0
        corr.append(jnp.where(inside, u[5 + k] / jnp.where(inside, t, 1.0), 0.0))
    stacked = jnp.concatenate(corr, axis=0)
    dst = lax.broadcasted_iota(jnp.int32, (CCOLS, COLS), 1)
    src = lax.broadcasted_iota(jnp.int32, (CCOLS, COLS), 0)
    spread = jnp.where(dst // 2 == src, 1.0, 0.0)
    wide = jnp.dot(
        stacked, spread, precision=lax.Precision.HIGHEST, preferred_element_type=jnp.float32
    )
    for k in range(4):
        for half in range(2):
            rows = wide[CR * k + 6 : CR * k + 26, CCOLS * half : CCOLS * half + CCOLS]
            cf[2 * k + half, pl.ds(0, 20, 2), :] = rows
            cf[2 * k + half, pl.ds(1, 20, 2), :] = rows
    zeros = jnp.zeros((FR, COLS), jnp.float32)
    for k in range(8):
        if 0 < k < 7:
            uf[k] = u_in[k - 1]
        else:
            uf[k] = zeros
            edge = r3lo if k == 0 else r3hi
            for j in range(4):
                row = 4 + 16 * (j // 2)
                lane = CCOLS * (j % 2)
                uf[k, row : row + 16, lane : lane + CCOLS] = edge[4 + j]
        at = Y2_U + 4 * k
        for half in range(2):
            lane = CCOLS * half
            uf[k, 2:4, lane : lane + CCOLS] = ylo[at + 2 * half : at + 2 * half + 2, :] * mlo
            uf[k, 36:38, lane : lane + CCOLS] = yhi[at + 2 * half : at + 2 * half + 2, :] * mhi
        both = 2 * (k // 2)
        uf[k] = uf[k] + t_in[k] * jnp.concatenate([cf[both], cf[both + 1]], axis=1)
    for k in range(8):
        xs[k] = smooth_xy(uf[k])
    for k in range(6):
        v = uf[k + 1]
        w = 2.0 * (xs[k + 1] + 0.5 * (xs[k] + xs[k + 2]) - v)
        uf[k + 1] = KEEP * v + a_in[k] + b_in[k] * w
    for k in range(6):
        xs[k] = smooth_xy(uf[k + 1])
    for k in range(4):
        v = uf[k + 2]
        w = 2.0 * (xs[k + 1] + 0.5 * (xs[k] + xs[k + 2]) - v)
        new = KEEP * v + a_in[k + 1] + b_in[k + 1] * w
        uf[k + 2] = new / t_in[k + 2]
        out[k] = uf[k + 2, 4:36, :]


VM = pl.BlockSpec(memory_space=pltpu.VMEM)
SM = pl.BlockSpec(memory_space=pltpu.SMEM)


def f32(*shape):
    return jax.ShapeDtypeStruct(shape, jnp.float32)


def call(kernel, specs, outs, scratch=()):
    return pl.pallas_call(
        kernel,
        in_specs=specs,
        out_specs=jax.tree.map(lambda _: VM, outs),
        out_shape=outs,
        scratch_shapes=[pltpu.VMEM(shape, jnp.float32) for shape in scratch],
        compiler_params=pltpu.CompilerParams(vmem_limit_bytes=8 * 1024 * 1024),
    )


def on_device(pressure_rhs, permeability, accumulation, coarse_perm, coarse_accum, run_lengths):
    up, down = call(
        pack_z1, [VM] * 4, (f32(Z1_ROWS, COLS), f32(Z1_ROWS, COLS))
    )(pressure_rhs, permeability, accumulation, coarse_perm)
    lo = shifted(up, "slab", 1)
    hi = shifted(down, "slab", -1)

    slab = lax.axis_index("slab")
    pen = lax.axis_index("pen")
    starts = jnp.cumsum(run_lengths) - run_lengths
    blocks = slab - 2 + jnp.arange(6, dtype=jnp.int32)
    begins = jnp.any(starts[None, :] == blocks[:, None], axis=1)
    masks = jnp.concatenate(
        [
            jnp.stack([pen > 0, pen < lax.axis_size("pen") - 1]).astype(jnp.float32),
            1.0 - begins.astype(jnp.float32),
        ]
    )

    up, down = call(
        pack_y1, [VM] * 6, (f32(Y1_ROWS, COLS), f32(Y1_ROWS, COLS))
    )(pressure_rhs, permeability, accumulation, coarse_perm, lo, hi)
    ylo = rotated(up, "pen", 1)
    yhi = rotated(down, "pen", -1)

    t, a, b, u, ct, ab, zup, zdn = call(
        pre_kernel,
        [SM] + [VM] * 9,
        (
            f32(8, FR, COLS), f32(6, FR, COLS), f32(6, FR, COLS), f32(6, FR, COLS),
            f32(4, CR, CCOLS), f32(4, CROWS, CCOLS),
            f32(8, CROWS, CCOLS), f32(8, CROWS, CCOLS),
        ),
        (
            (10, FR, COLS), (8, FR, COLS), (8, FR, COLS),
            (10, FR, COLS), (8, FR, COLS), (4, FR, COLS), (4, FR, CCOLS),
        ),
    )(masks, pressure_rhs, permeability, accumulation, coarse_perm, coarse_accum, lo, hi, ylo, yhi)
    r3lo = shifted(zup, "slab", 1)
    r3hi = shifted(zdn, "slab", -1)

    r4lo = shifted(jnp.concatenate([ab, r3lo[0:2], r3lo[3:4]], axis=0), "slab", 2)
    r4hi = shifted(jnp.concatenate([ab, r3hi[0:3]], axis=0), "slab", -2)

    up, down = call(
        pack_y2, [VM] * 6, (f32(Y2_ROWS, CCOLS), f32(Y2_ROWS, CCOLS))
    )(ab, u, r3lo, r3hi, r4lo, r4hi)
    ylo = rotated(up, "pen", 1)
    yhi = rotated(down, "pen", -1)

    return call(
        post_kernel,
        [SM] + [VM] * 12,
        f32(4, ROWS, COLS),
        ((8, FR, COLS), (8, FR, CCOLS), (8, FR, COLS)),
    )(masks, t, a, b, u, ct, ab, r3lo, r3hi, r4lo, r4hi, ylo, yhi)


def solution(mesh):
    return jax.shard_map(
        on_device,
        mesh=mesh,
        in_specs=(
            P("slab", "pen", None),
            P("slab", "pen", None),
            P("slab", "pen", None),
            P("slab", "pen", None),
            P("slab", "pen", None),
            P(),
        ),
        out_specs=P("slab", "pen", None),
        check_vma=False,
    )
```

```python
import jax
import jax.numpy as jnp
from jax import lax
from jax.experimental import pallas as pl
from jax.experimental.pallas import tpu as pltpu
from jax.sharding import PartitionSpec as P

OMEGA = 0.7
KEEP = 1.0 - OMEGA
COARSE_SWEEPS = 6

FR = 40
ROWS = 32
COLS = 256
CR = 32
CROWS = 16
CCOLS = 128


def shifted(x, axis, by):
    devices = lax.axis_size(axis)
    pairs = [(i, i + by) for i in range(devices) if 0 <= i + by < devices]
    return lax.ppermute(x, axis, pairs)


def rotated(x, axis, by):
    devices = lax.axis_size(axis)
    return lax.ppermute(x, axis, [(i, (i + by) % devices) for i in range(devices)])


def smooth_xy(v):
    rows, cols = v.shape
    col = lax.broadcasted_iota(jnp.int32, v.shape, 1)
    left = jnp.where(col == 0, 0.0, pltpu.roll(v, 1, 1))
    right = jnp.where(col == cols - 1, 0.0, pltpu.roll(v, cols - 1, 1))
    h = v + 0.5 * (left + right)
    return h + 0.5 * (pltpu.roll(h, 1, 0) + pltpu.roll(h, rows - 1, 0))


def to_wide(x):
    return jnp.concatenate([x[0:8], x[8:16]], axis=1)


def from_wide(x):
    return jnp.concatenate([x[:, 0:CCOLS], x[:, CCOLS:COLS]], axis=0)


Z1_RHS = 96
Z1_ACC = 160
Z1_CO = 224
Z1_ROWS = 232


def pack_z1(rhs, perm, acc, cperm, up, down, held, sems):
    copies = [pltpu.make_async_copy(cperm, held, sems.at[0])]
    for out, first3, first2 in ((up, 1, 2), (down, 0, 0)):
        for base, ref, first, count in (
            (0, perm, first3, 3), (Z1_RHS, rhs, first2, 2), (Z1_ACC, acc, first2, 2)
        ):
            for k in range(count):
                copies.append(
                    pltpu.make_async_copy(
                        ref.at[first + k],
                        out.at[pl.ds(base + ROWS * k, ROWS)],
                        sems.at[len(copies)],
                    )
                )
    for copy in copies:
        copy.start()
    for copy in copies:
        copy.wait()
    up[Z1_CO : Z1_CO + 8, :] = to_wide(held[1])
    down[Z1_CO : Z1_CO + 8, :] = to_wide(held[0])


def fine_rows(own, lo, hi, base, depth, z, first, count):
    if z < 0:
        at = base + 32 * (z + depth)
        return lo[at + first : at + first + count, :]
    if z > 3:
        at = base + 32 * (z - 4)
        return hi[at + first : at + first + count, :]
    return own[z, first : first + count, :]


def coarse_plane(cperm, lo, hi, c):
    if c < 0:
        return from_wide(lo[Z1_CO : Z1_CO + 8, :])
    if c > 1:
        return from_wide(hi[Z1_CO : Z1_CO + 8, :])
    return cperm[c]


Y1_RHS = 30
Y1_ACC = 46
Y1_CO = 62
Y1_ROWS = 64


def pack_y1(rhs, perm, acc, cperm, lo, hi, up, down):
    for out, top in ((up, True), (down, False)):
        r3 = ROWS - 3 if top else 0
        r2 = ROWS - 2 if top else 0
        for k in range(10):
            out[3 * k : 3 * k + 3, :] = fine_rows(perm, lo, hi, 0, 3, k - 3, r3, 3)
        for k in range(8):
            at = Y1_RHS + 2 * k
            out[at : at + 2, :] = fine_rows(rhs, lo, hi, Z1_RHS, 2, k - 2, r2, 2)
            at = Y1_ACC + 2 * k
            out[at : at + 2, :] = fine_rows(acc, lo, hi, Z1_ACC, 2, k - 2, r2, 2)
        rc = CROWS - 1 if top else 0
        for k in range(4):
            plane = coarse_plane(cperm, lo, hi, k - 1)
            at = Y1_CO + k // 2
            lane = CCOLS * (k % 2)
            out[at : at + 1, lane : lane + CCOLS] = plane[rc : rc + 1, :]


def pre_kernel(
    masks, rhs, perm, acc, cperm, cacc, lo, hi, ylo, yhi,
    t_out, a_out, b_out, u_out, ct_out, ab_out, zup, zdn,
    ts, rs, cs, xs, us, ds, fs,
):
    mlo = masks[0]
    mhi = masks[1]
    zeros = jnp.zeros((FR, COLS), jnp.float32)
    for k in range(10):
        z = k - 3
        ts[k] = zeros
        ts[k, 4:36, :] = jnp.sqrt(fine_rows(perm, lo, hi, 0, 3, z, 0, ROWS))
        ts[k, 1:4, :] = jnp.sqrt(ylo[3 * k : 3 * k + 3, :] * mlo)
        ts[k, 36:39, :] = jnp.sqrt(yhi[3 * k : 3 * k + 3, :] * mhi)
    for k in range(8):
        z = k - 2
        for ref, own, base, ybase in ((rs, rhs, Z1_RHS, Y1_RHS), (cs, acc, Z1_ACC, Y1_ACC)):
            ref[k] = zeros
            ref[k, 4:36, :] = fine_rows(own, lo, hi, base, 2, z, 0, ROWS)
            ref[k, 2:4, :] = ylo[ybase + 2 * k : ybase + 2 * k + 2, :] * mlo
            ref[k, 36:38, :] = yhi[ybase + 2 * k : ybase + 2 * k + 2, :] * mhi
    for k in range(10):
        xs[k] = smooth_xy(ts[k])
    for k in range(8):
        t = ts[k + 1]
        w = 2.0 * (xs[k + 1] + 0.5 * (xs[k] + xs[k + 2]) - t)
        d = t * w + cs[k]
        d = jnp.where(d > 0.0, d, 1.0)
        q = OMEGA * t / d
        if 2 <= k < 6:
            ds[k - 2] = d
        t_out[k] = t
        rs_k = rs[k]
        us[k] = q * rs_k
        cs[k] = q * t
    for k in range(8):
        xs[k] = smooth_xy(us[k])
    for k in range(6):
        a = us[k + 1]
        b = cs[k + 1]
        w = 2.0 * (xs[k + 1] + 0.5 * (xs[k] + xs[k + 2]) - a)
        a_out[k] = a
        b_out[k] = b
        u_out[k] = (1.0 + KEEP) * a + b * w
    for k in range(6):
        xs[k] = smooth_xy(u_out[k])
    sums = []
    for k in range(4):
        u = u_out[k + 1]
        t = ts[k + 3]
        w = 2.0 * (xs[k + 1] + 0.5 * (xs[k] + xs[k + 2]) - u)
        r = rs[k + 2] + t * w - ds[k] * (u / t)
        sums.append(r)
    pairs = []
    for k in range(2):
        both = sums[2 * k] + sums[2 * k + 1]
        halves = []
        for half in range(2):
            at = 2 * k + half
            fs[at] = both[:, CCOLS * half : CCOLS * half + CCOLS]
            halves.append(fs[at, pl.ds(4, CROWS, 2), :] + fs[at, pl.ds(5, CROWS, 2), :])
        pairs.append(jnp.concatenate(halves, axis=1))
    stacked = jnp.concatenate(pairs, axis=0)
    src = lax.broadcasted_iota(jnp.int32, (COLS, CCOLS), 0)
    dst = lax.broadcasted_iota(jnp.int32, (COLS, CCOLS), 1)
    fold = jnp.where(src // 2 == dst, 1.0, 0.0)
    res = jnp.dot(
        stacked, fold, precision=lax.Precision.HIGHEST, preferred_element_type=jnp.float32
    )
    for k in range(4):
        ct_out[k] = jnp.zeros((CR, CCOLS), jnp.float32)
        ct_out[k, 8:24, :] = jnp.sqrt(coarse_plane(cperm, lo, hi, k - 1))
        at = Y1_CO + k // 2
        lane = CCOLS * (k % 2)
        ct_out[k, 7:8, :] = jnp.sqrt(ylo[at : at + 1, lane : lane + CCOLS] * mlo)
        ct_out[k, 24:25, :] = jnp.sqrt(yhi[at : at + 1, lane : lane + CCOLS] * mhi)
    cx = [smooth_xy(ct_out[k]) for k in range(4)]
    for k in range(2):
        t = ct_out[k + 1]
        w = 2.0 * (cx[k + 1] + 0.5 * (cx[k] + cx[k + 2]) - t)
        t = t[8:24]
        d = t * w[8:24] + cacc[k]
        q = OMEGA * t / d
        a = q * res[CROWS * k : CROWS * k + CROWS]
        b = q * t
        for out in (ab_out, zup, zdn):
            out[k] = a
            out[2 + k] = b
    for out, plane in ((zup, 3), (zdn, 2)):
        for k in range(4):
            row = 4 + 16 * (k // 2)
            lane = CCOLS * (k % 2)
            out[4 + k] = u_out[plane, row : row + 16, lane : lane + CCOLS]


def pack_up2(ab, r3lo, out):
    out[0:4] = ab[...]
    out[4:6] = r3lo[0:2]
    out[6] = r3lo[3]


def pack_down2(ab, r3hi, out):
    out[0:4] = ab[...]
    out[4:7] = r3hi[0:3]


Y2_B = 84
Y2_U = 156
Y2_ROWS = 192


def coarse_a(ab, r3lo, r3hi, r4lo, r4hi, c):
    if c < -4:
        return r4lo.at[c + 10]
    if c < -2:
        return r4lo.at[c + 4]
    if c < 0:
        return r3lo.at[c + 2]
    if c < 2:
        return ab.at[c]
    if c < 4:
        return r3hi.at[c - 2]
    if c < 6:
        return r4hi.at[c - 4]
    return r4hi.at[c - 2]


def coarse_b(ab, r3lo, r3hi, r4lo, r4hi, c):
    if c == -5:
        return r4lo.at[6]
    if c < -2:
        return r4lo.at[c + 6]
    if c < 0:
        return r3lo.at[c + 4]
    if c < 2:
        return ab.at[c + 2]
    if c < 4:
        return r3hi.at[c]
    if c < 6:
        return r4hi.at[c - 2]
    return r4hi.at[6]


def pack_y2(ab, u, r3lo, r3hi, r4lo, r4hi, up, down):
    for out, top in ((up, True), (down, False)):
        first = CROWS - 6 if top else 0
        for k in range(14):
            plane = coarse_a(ab, r3lo, r3hi, r4lo, r4hi, k - 6)
            out[6 * k : 6 * k + 6, :] = plane[first : first + 6, :]
        for k in range(12):
            plane = coarse_b(ab, r3lo, r3hi, r4lo, r4hi, k - 5)
            out[Y2_B + 6 * k : Y2_B + 6 * k + 6, :] = plane[first : first + 6, :]
        for k in range(8):
            at = Y2_U + 4 * k
            for half in range(2):
                if 0 < k < 7:
                    row = 34 if top else 4
                    rows = u[k - 1, row : row + 2, CCOLS * half : CCOLS * half + CCOLS]
                else:
                    edge = r3lo if k == 0 else r3hi
                    if top:
                        rows = edge[6 + half, 14:16, :]
                    else:
                        rows = edge[4 + half, 0:2, :]
                out[at + 2 * half : at + 2 * half + 2, :] = rows


def post_kernel(
    masks, t_in, a_in, b_in, u_in, ct, ab, r3lo, r3hi, r4lo, r4hi, ylo, yhi,
    out, uf, cf, xs, ff,
):
    mlo = masks[0]
    mhi = masks[1]
    tile = jnp.zeros((8, CCOLS), jnp.float32)
    a = []
    b = [None]
    for k in range(26):
        if k < 14:
            own = coarse_a(ab, r3lo, r3hi, r4lo, r4hi, k - 6)
        else:
            own = coarse_b(ab, r3lo, r3hi, r4lo, r4hi, k - 19)
        ff[k, 0:8, :] = tile
        ff[k, 24:32, :] = tile
        ff[k, 2:8, :] = ylo[6 * k : 6 * k + 6, :] * mlo
        ff[k, 8:24, :] = own[...]
        ff[k, 24:30, :] = yhi[6 * k : 6 * k + 6, :] * mhi
        (a if k < 14 else b).append(ff[k])
    link = [0.5] * 13
    for j in range(6):
        link[2 * j + 1] = 0.5 * masks[2 + j]
    u = list(a)
    for sweep in range(1, COARSE_SWEEPS):
        first, last = sweep, 13 - sweep
        smooth = {k: smooth_xy(u[k]) for k in range(first - 1, last + 2)}
        fresh = list(u)
        for k in range(first, last + 1):
            w = 2.0 * (
                smooth[k] + link[k - 1] * smooth[k - 1] + link[k] * smooth[k + 1] - u[k]
            )
            fresh[k] = KEEP * u[k] + a[k] + b[k] * w
        u = fresh
    corr = []
    for k in range(4):
        t = ct[k]
        inside = t > 0.0
        corr.append(jnp.where(inside, u[5 + k] / jnp.where(inside, t, 1.0), 0.0))
    stacked = jnp.concatenate(corr, axis=0)
    dst = lax.broadcasted_iota(jnp.int32, (CCOLS, COLS), 1)
    src = lax.broadcasted_iota(jnp.int32, (CCOLS, COLS), 0)
    spread = jnp.where(dst // 2 == src, 1.0, 0.0)
    wide = jnp.dot(
        stacked, spread, precision=lax.Precision.HIGHEST, preferred_element_type=jnp.float32
    )
    for k in range(4):
        for half in range(2):
            rows = wide[CR * k + 6 : CR * k + 26, CCOLS * half : CCOLS * half + CCOLS]
            cf[2 * k + half, pl.ds(0, 20, 2), :] = rows
            cf[2 * k + half, pl.ds(1, 20, 2), :] = rows
    zeros = jnp.zeros((FR, COLS), jnp.float32)
    for k in range(8):
        if 0 < k < 7:
            uf[k] = u_in[k - 1]
        else:
            uf[k] = zeros
            edge = r3lo if k == 0 else r3hi
            for j in range(4):
                row = 4 + 16 * (j // 2)
                lane = CCOLS * (j % 2)
                uf[k, row : row + 16, lane : lane + CCOLS] = edge[4 + j]
        at = Y2_U + 4 * k
        for half in range(2):
            lane = CCOLS * half
            uf[k, 2:4, lane : lane + CCOLS] = ylo[at + 2 * half : at + 2 * half + 2, :] * mlo
            uf[k, 36:38, lane : lane + CCOLS] = yhi[at + 2 * half : at + 2 * half + 2, :] * mhi
        both = 2 * (k // 2)
        uf[k] = uf[k] + t_in[k] * jnp.concatenate([cf[both], cf[both + 1]], axis=1)
    for k in range(8):
        xs[k] = smooth_xy(uf[k])
    for k in range(6):
        v = uf[k + 1]
        w = 2.0 * (xs[k + 1] + 0.5 * (xs[k] + xs[k + 2]) - v)
        uf[k + 1] = KEEP * v + a_in[k] + b_in[k] * w
    for k in range(6):
        xs[k] = smooth_xy(uf[k + 1])
    for k in range(4):
        v = uf[k + 2]
        w = 2.0 * (xs[k + 1] + 0.5 * (xs[k] + xs[k + 2]) - v)
        new = KEEP * v + a_in[k + 1] + b_in[k + 1] * w
        uf[k + 2] = new / t_in[k + 2]
        out[k] = uf[k + 2, 4:36, :]


VM = pl.BlockSpec(memory_space=pltpu.VMEM)
SM = pl.BlockSpec(memory_space=pltpu.SMEM)
HBM = pl.BlockSpec(memory_space=pltpu.HBM)


def f32(*shape):
    return jax.ShapeDtypeStruct(shape, jnp.float32)


def call(kernel, specs, outs, scratch=()):
    return pl.pallas_call(
        kernel,
        in_specs=specs,
        out_specs=jax.tree.map(lambda _: VM, outs),
        out_shape=outs,
        scratch_shapes=[
            pltpu.VMEM(shape, jnp.float32) if isinstance(shape, tuple) else shape
            for shape in scratch
        ],
        compiler_params=pltpu.CompilerParams(vmem_limit_bytes=8 * 1024 * 1024),
    )


def on_device(pressure_rhs, permeability, accumulation, coarse_perm, coarse_accum, run_lengths):
    up, down = call(
        pack_z1,
        [HBM] * 4,
        (f32(Z1_ROWS, COLS), f32(Z1_ROWS, COLS)),
        (pltpu.VMEM((2, CROWS, CCOLS), jnp.float32), pltpu.SemaphoreType.DMA((15,))),
    )(
        *(
            pltpu.with_memory_space_constraint(x, pltpu.HBM)
            for x in (pressure_rhs, permeability, accumulation, coarse_perm)
        )
    )
    lo = shifted(up, "slab", 1)
    hi = shifted(down, "slab", -1)

    slab = lax.axis_index("slab")
    pen = lax.axis_index("pen")
    starts = jnp.cumsum(run_lengths) - run_lengths
    blocks = slab - 2 + jnp.arange(6, dtype=jnp.int32)
    begins = jnp.any(starts[None, :] == blocks[:, None], axis=1)
    masks = jnp.concatenate(
        [
            jnp.stack([pen > 0, pen < lax.axis_size("pen") - 1]).astype(jnp.float32),
            1.0 - begins.astype(jnp.float32),
        ]
    )

    up, down = call(
        pack_y1, [VM] * 6, (f32(Y1_ROWS, COLS), f32(Y1_ROWS, COLS))
    )(pressure_rhs, permeability, accumulation, coarse_perm, lo, hi)
    ylo = rotated(up, "pen", 1)
    yhi = rotated(down, "pen", -1)

    t, a, b, u, ct, ab, zup, zdn = call(
        pre_kernel,
        [SM] + [VM] * 9,
        (
            f32(8, FR, COLS), f32(6, FR, COLS), f32(6, FR, COLS), f32(6, FR, COLS),
            f32(4, CR, CCOLS), f32(4, CROWS, CCOLS),
            f32(8, CROWS, CCOLS), f32(8, CROWS, CCOLS),
        ),
        (
            (10, FR, COLS), (8, FR, COLS), (8, FR, COLS),
            (10, FR, COLS), (8, FR, COLS), (4, FR, COLS), (4, FR, CCOLS),
        ),
    )(masks, pressure_rhs, permeability, accumulation, coarse_perm, coarse_accum, lo, hi, ylo, yhi)
    r3lo = shifted(zup, "slab", 1)
    r3hi = shifted(zdn, "slab", -1)

    further = f32(7, CROWS, CCOLS)
    r4lo = shifted(call(pack_up2, [VM] * 2, further)(ab, r3lo), "slab", 2)
    r4hi = shifted(call(pack_down2, [VM] * 2, further)(ab, r3hi), "slab", -2)

    up, down = call(
        pack_y2, [VM] * 6, (f32(Y2_ROWS, CCOLS), f32(Y2_ROWS, CCOLS))
    )(ab, u, r3lo, r3hi, r4lo, r4hi)
    ylo = rotated(up, "pen", 1)
    yhi = rotated(down, "pen", -1)

    return call(
        post_kernel,
        [SM] + [VM] * 12,
        f32(4, ROWS, COLS),
        ((8, FR, COLS), (8, FR, CCOLS), (8, FR, COLS), (26, CR, CCOLS)),
    )(masks, t, a, b, u, ct, ab, r3lo, r3hi, r4lo, r4hi, ylo, yhi)


def solution(mesh):
    return jax.shard_map(
        on_device,
        mesh=mesh,
        in_specs=(
            P("slab", "pen", None),
            P("slab", "pen", None),
            P("slab", "pen", None),
            P("slab", "pen", None),
            P("slab", "pen", None),
            P(),
        ),
        out_specs=P("slab", "pen", None),
        check_vma=False,
    )
```

```python
import jax
import jax.numpy as jnp
from jax import lax
from jax.experimental import pallas as pl
from jax.experimental.pallas import tpu as pltpu
from jax.sharding import PartitionSpec as P

OMEGA = 0.7
KEEP = 1.0 - OMEGA
COARSE_SWEEPS = 6

FR = 40
ROWS = 32
COLS = 256
CR = 32
CROWS = 16
CCOLS = 128


LINE = 16


def along_lines(x, by):
    slabs, pens = lax.axis_size("slab"), lax.axis_size("pen")
    pairs = []
    for slab in range(slabs):
        for pen in range(pens):
            line, z = divmod(slab, LINE)
            core = pen % 2
            step = (2 * LINE - 1 - z if core else z) + by
            step %= 2 * LINE
            core, z = (0, step) if step < LINE else (1, 2 * LINE - 1 - step)
            pairs.append((slab * pens + pen, (line * LINE + z) * pens + pen // 2 * 2 + core))
    return lax.ppermute(x, ("slab", "pen"), pairs)


def between_lines(x, partners):
    slabs, pens = lax.axis_size("slab"), lax.axis_size("pen")
    pairs = []
    for line in range(1, slabs // LINE):
        for j, k in partners:
            for pen in range(pens):
                here = (line * LINE + j) * pens + pen
                there = ((line - 1) * LINE + k) * pens + pen
                pairs += [(here, there), (there, here)]
    return lax.ppermute(x, ("slab", "pen"), pairs)


def place():
    return lax.axis_index("pen") % 2 == 0, lax.axis_index("slab") % LINE


class Picked:
    def __init__(self, first, one, other, end, across):
        self.parts = (first, one, other, end, across)

    def __getitem__(self, index):
        first, one, other, end, across = self.parts
        value = jnp.where(first, one[index], other[index])
        return jnp.where(end, across[index], value)


def below_above(plus, minus, across):
    first, z = place()
    return (
        Picked(first, plus, minus, z == 0, across),
        Picked(first, minus, plus, z == LINE - 1, across),
    )


def rotated(x, axis, by):
    devices = lax.axis_size(axis)
    return lax.ppermute(x, axis, [(i, (i + by) % devices) for i in range(devices)])


def smooth_xy(v):
    rows, cols = v.shape
    col = lax.broadcasted_iota(jnp.int32, v.shape, 1)
    left = jnp.where(col == 0, 0.0, pltpu.roll(v, 1, 1))
    right = jnp.where(col == cols - 1, 0.0, pltpu.roll(v, cols - 1, 1))
    h = v + 0.5 * (left + right)
    return h + 0.5 * (pltpu.roll(h, 1, 0) + pltpu.roll(h, rows - 1, 0))


def to_wide(x):
    return jnp.concatenate([x[0:8], x[8:16]], axis=1)


def from_wide(x):
    return jnp.concatenate([x[:, 0:CCOLS], x[:, CCOLS:COLS]], axis=0)


Z1_RHS = 96
Z1_ACC = 160
Z1_CO = 224
Z1_ROWS = 232


def pack_z1(rhs, perm, acc, cperm, plus, minus, across, held, sems):
    first, z = place()
    upward = (first, jnp.logical_not(first), z == LINE - 1)
    copies = [pltpu.make_async_copy(cperm, held, sems.at[0])]
    for out, up in zip((plus, minus, across), upward):
        for base, ref, start, count in (
            (0, perm, jnp.where(up, 1, 0), 3),
            (Z1_RHS, rhs, jnp.where(up, 2, 0), 2),
            (Z1_ACC, acc, jnp.where(up, 2, 0), 2),
        ):
            for k in range(count):
                copies.append(
                    pltpu.make_async_copy(
                        ref.at[start + k],
                        out.at[pl.ds(base + ROWS * k, ROWS)],
                        sems.at[len(copies)],
                    )
                )
    for copy in copies:
        copy.start()
    for copy in copies:
        copy.wait()
    for out, up in zip((plus, minus, across), upward):
        out[Z1_CO : Z1_CO + 8, :] = to_wide(held[jnp.where(up, 1, 0)])


def fine_rows(own, lo, hi, base, depth, z, first, count):
    if z < 0:
        at = base + 32 * (z + depth)
        return lo[at + first : at + first + count, :]
    if z > 3:
        at = base + 32 * (z - 4)
        return hi[at + first : at + first + count, :]
    return own[z, first : first + count, :]


def coarse_plane(cperm, lo, hi, c):
    if c < 0:
        return from_wide(lo[Z1_CO : Z1_CO + 8, :])
    if c > 1:
        return from_wide(hi[Z1_CO : Z1_CO + 8, :])
    return cperm[c]


Y1_RHS = 30
Y1_ACC = 46
Y1_CO = 62
Y1_ROWS = 64


def pack_y1(rhs, perm, acc, cperm, plus, minus, across, up, down):
    lo, hi = below_above(plus, minus, across)
    for out, top in ((up, True), (down, False)):
        r3 = ROWS - 3 if top else 0
        r2 = ROWS - 2 if top else 0
        for k in range(10):
            out[3 * k : 3 * k + 3, :] = fine_rows(perm, lo, hi, 0, 3, k - 3, r3, 3)
        for k in range(8):
            at = Y1_RHS + 2 * k
            out[at : at + 2, :] = fine_rows(rhs, lo, hi, Z1_RHS, 2, k - 2, r2, 2)
            at = Y1_ACC + 2 * k
            out[at : at + 2, :] = fine_rows(acc, lo, hi, Z1_ACC, 2, k - 2, r2, 2)
        rc = CROWS - 1 if top else 0
        for k in range(4):
            plane = coarse_plane(cperm, lo, hi, k - 1)
            at = Y1_CO + k // 2
            lane = CCOLS * (k % 2)
            out[at : at + 1, lane : lane + CCOLS] = plane[rc : rc + 1, :]


def pre_kernel(
    masks, rhs, perm, acc, cperm, cacc, plus, minus, across, ylo, yhi,
    t_out, a_out, b_out, u_out, ct_out, ab_out, plus_out, minus_out, across_out,
    ts, rs, cs, xs, us, ds, fs,
):
    first, place_z = place()
    lo, hi = below_above(plus, minus, across)
    mlo = masks[0]
    mhi = masks[1]
    zeros = jnp.zeros((FR, COLS), jnp.float32)
    for k in range(10):
        z = k - 3
        ts[k] = zeros
        ts[k, 4:36, :] = jnp.sqrt(fine_rows(perm, lo, hi, 0, 3, z, 0, ROWS))
        ts[k, 1:4, :] = jnp.sqrt(ylo[3 * k : 3 * k + 3, :] * mlo)
        ts[k, 36:39, :] = jnp.sqrt(yhi[3 * k : 3 * k + 3, :] * mhi)
    for k in range(8):
        z = k - 2
        for ref, own, base, ybase in ((rs, rhs, Z1_RHS, Y1_RHS), (cs, acc, Z1_ACC, Y1_ACC)):
            ref[k] = zeros
            ref[k, 4:36, :] = fine_rows(own, lo, hi, base, 2, z, 0, ROWS)
            ref[k, 2:4, :] = ylo[ybase + 2 * k : ybase + 2 * k + 2, :] * mlo
            ref[k, 36:38, :] = yhi[ybase + 2 * k : ybase + 2 * k + 2, :] * mhi
    for k in range(10):
        xs[k] = smooth_xy(ts[k])
    for k in range(8):
        t = ts[k + 1]
        w = 2.0 * (xs[k + 1] + 0.5 * (xs[k] + xs[k + 2]) - t)
        d = t * w + cs[k]
        d = jnp.where(d > 0.0, d, 1.0)
        q = OMEGA * t / d
        if 2 <= k < 6:
            ds[k - 2] = d
        t_out[k] = t
        rs_k = rs[k]
        us[k] = q * rs_k
        cs[k] = q * t
    for k in range(8):
        xs[k] = smooth_xy(us[k])
    for k in range(6):
        a = us[k + 1]
        b = cs[k + 1]
        w = 2.0 * (xs[k + 1] + 0.5 * (xs[k] + xs[k + 2]) - a)
        a_out[k] = a
        b_out[k] = b
        u_out[k] = (1.0 + KEEP) * a + b * w
    for k in range(6):
        xs[k] = smooth_xy(u_out[k])
    sums = []
    for k in range(4):
        u = u_out[k + 1]
        t = ts[k + 3]
        w = 2.0 * (xs[k + 1] + 0.5 * (xs[k] + xs[k + 2]) - u)
        r = rs[k + 2] + t * w - ds[k] * (u / t)
        sums.append(r)
    pairs = []
    for k in range(2):
        both = sums[2 * k] + sums[2 * k + 1]
        halves = []
        for half in range(2):
            at = 2 * k + half
            fs[at] = both[:, CCOLS * half : CCOLS * half + CCOLS]
            halves.append(fs[at, pl.ds(4, CROWS, 2), :] + fs[at, pl.ds(5, CROWS, 2), :])
        pairs.append(jnp.concatenate(halves, axis=1))
    stacked = jnp.concatenate(pairs, axis=0)
    src = lax.broadcasted_iota(jnp.int32, (COLS, CCOLS), 0)
    dst = lax.broadcasted_iota(jnp.int32, (COLS, CCOLS), 1)
    fold = jnp.where(src // 2 == dst, 1.0, 0.0)
    res = jnp.dot(
        stacked, fold, precision=lax.Precision.HIGHEST, preferred_element_type=jnp.float32
    )
    for k in range(4):
        ct_out[k] = jnp.zeros((CR, CCOLS), jnp.float32)
        ct_out[k, 8:24, :] = jnp.sqrt(coarse_plane(cperm, lo, hi, k - 1))
        at = Y1_CO + k // 2
        lane = CCOLS * (k % 2)
        ct_out[k, 7:8, :] = jnp.sqrt(ylo[at : at + 1, lane : lane + CCOLS] * mlo)
        ct_out[k, 24:25, :] = jnp.sqrt(yhi[at : at + 1, lane : lane + CCOLS] * mhi)
    cx = [smooth_xy(ct_out[k]) for k in range(4)]
    for k in range(2):
        t = ct_out[k + 1]
        w = 2.0 * (cx[k + 1] + 0.5 * (cx[k] + cx[k + 2]) - t)
        t = t[8:24]
        d = t * w[8:24] + cacc[k]
        q = OMEGA * t / d
        a = q * res[CROWS * k : CROWS * k + CROWS]
        b = q * t
        for out in (ab_out, plus_out, minus_out, across_out):
            out[k] = a
            out[2 + k] = b
    for out, up in (
        (plus_out, first), (minus_out, jnp.logical_not(first)), (across_out, place_z == LINE - 1)
    ):
        plane = jnp.where(up, 3, 2)
        for k in range(4):
            row = 4 + 16 * (k // 2)
            lane = CCOLS * (k % 2)
            out[4 + k] = u_out[plane, row : row + 16, lane : lane + CCOLS]


def pack_plus3(held, near, far, out):
    pack_third(place()[0], held, near, far, out)


def pack_minus3(held, near, far, out):
    pack_third(jnp.logical_not(place()[0]), held, near, far, out)


def pack_third(up, held, near, far, out):
    out[0:2] = held[0:2]
    out[2] = held[jnp.where(up, 3, 2)]
    out[3:7] = jnp.where(up, near[0:4], far[...])


Y2_B = 84
Y2_U = 156
Y2_ROWS = 192


def pack_y2(
    ab, u, plus1, minus1, plus2, minus2, plus3, minus3, near, far, up, down, dom, edge
):
    first, z = place()

    def below(plus, minus, k):
        return jnp.where(first, plus[k], minus[k])

    def above(plus, minus, k):
        return jnp.where(first, minus[k], plus[k])

    def choose(value, *ends):
        for at, other in ends:
            value = jnp.where(z == at, other, value)
        return value

    top = LINE - 1
    for k in range(4):
        a = k < 2
        dom[6 + k if a else 17 + k] = ab[k]
        dom[4 + k if a else 15 + k] = choose(below(plus1, minus1, k), (0, near[k]))
        dom[8 + k if a else 19 + k] = choose(above(plus1, minus1, k), (top, near[k]))
        dom[2 + k if a else 13 + k] = choose(
            below(plus2, minus2, k), (0, far[k]), (1, below(plus3, minus3, 3 + k))
        )
        dom[10 + k if a else 21 + k] = choose(
            above(plus2, minus2, k), (top, below(plus3, minus3, 3 + k)), (top - 1, far[k])
        )
        edge[k] = choose(below(plus1, minus1, 4 + k), (0, near[4 + k]))
        edge[4 + k] = choose(above(plus1, minus1, 4 + k), (top, near[4 + k]))
    for k in range(3):
        low = 3 if k == 2 else k
        dom[14 if k == 2 else k] = choose(
            below(plus3, minus3, k),
            (0, above(plus3, minus3, 3 + low)), (1, near[low]), (2, far[low]),
        )
        dom[25 if k == 2 else 12 + k] = choose(
            above(plus3, minus3, k),
            (top, far[k]), (top - 1, near[k]), (top - 2, above(plus3, minus3, 3 + k)),
        )
    for out, top_rows in ((up, True), (down, False)):
        row = CROWS - 6 if top_rows else 0
        for k in range(26):
            out[6 * k : 6 * k + 6, :] = dom[k, row : row + 6, :]
        for k in range(8):
            at = Y2_U + 4 * k
            for half in range(2):
                if 0 < k < 7:
                    row = 34 if top_rows else 4
                    rows = u[k - 1, row : row + 2, CCOLS * half : CCOLS * half + CCOLS]
                else:
                    piece = (0 if k == 0 else 4) + half
                    if top_rows:
                        rows = edge[piece + 2, 14:16, :]
                    else:
                        rows = edge[piece, 0:2, :]
                out[at + 2 * half : at + 2 * half + 2, :] = rows


def post_kernel(
    masks, t_in, a_in, b_in, u_in, ct, dom, edge, ylo, yhi,
    out, uf, cf, xs, ff,
):
    mlo = masks[0]
    mhi = masks[1]
    tile = jnp.zeros((8, CCOLS), jnp.float32)
    a = []
    b = [None]
    for k in range(26):
        ff[k, 0:8, :] = tile
        ff[k, 24:32, :] = tile
        ff[k, 2:8, :] = ylo[6 * k : 6 * k + 6, :] * mlo
        ff[k, 8:24, :] = dom[k]
        ff[k, 24:30, :] = yhi[6 * k : 6 * k + 6, :] * mhi
        (a if k < 14 else b).append(ff[k])
    link = [0.5] * 13
    for j in range(6):
        link[2 * j + 1] = 0.5 * masks[2 + j]
    u = list(a)
    for sweep in range(1, COARSE_SWEEPS):
        first, last = sweep, 13 - sweep
        smooth = {k: smooth_xy(u[k]) for k in range(first - 1, last + 2)}
        fresh = list(u)
        for k in range(first, last + 1):
            w = 2.0 * (
                smooth[k] + link[k - 1] * smooth[k - 1] + link[k] * smooth[k + 1] - u[k]
            )
            fresh[k] = KEEP * u[k] + a[k] + b[k] * w
        u = fresh
    corr = []
    for k in range(4):
        t = ct[k]
        inside = t > 0.0
        corr.append(jnp.where(inside, u[5 + k] / jnp.where(inside, t, 1.0), 0.0))
    stacked = jnp.concatenate(corr, axis=0)
    dst = lax.broadcasted_iota(jnp.int32, (CCOLS, COLS), 1)
    src = lax.broadcasted_iota(jnp.int32, (CCOLS, COLS), 0)
    spread = jnp.where(dst // 2 == src, 1.0, 0.0)
    wide = jnp.dot(
        stacked, spread, precision=lax.Precision.HIGHEST, preferred_element_type=jnp.float32
    )
    for k in range(4):
        for half in range(2):
            rows = wide[CR * k + 6 : CR * k + 26, CCOLS * half : CCOLS * half + CCOLS]
            cf[2 * k + half, pl.ds(0, 20, 2), :] = rows
            cf[2 * k + half, pl.ds(1, 20, 2), :] = rows
    zeros = jnp.zeros((FR, COLS), jnp.float32)
    for k in range(8):
        if 0 < k < 7:
            uf[k] = u_in[k - 1]
        else:
            uf[k] = zeros
            piece = 0 if k == 0 else 4
            for j in range(4):
                row = 4 + 16 * (j // 2)
                lane = CCOLS * (j % 2)
                uf[k, row : row + 16, lane : lane + CCOLS] = edge[piece + j]
        at = Y2_U + 4 * k
        for half in range(2):
            lane = CCOLS * half
            uf[k, 2:4, lane : lane + CCOLS] = ylo[at + 2 * half : at + 2 * half + 2, :] * mlo
            uf[k, 36:38, lane : lane + CCOLS] = yhi[at + 2 * half : at + 2 * half + 2, :] * mhi
        both = 2 * (k // 2)
        uf[k] = uf[k] + t_in[k] * jnp.concatenate([cf[both], cf[both + 1]], axis=1)
    for k in range(8):
        xs[k] = smooth_xy(uf[k])
    for k in range(6):
        v = uf[k + 1]
        w = 2.0 * (xs[k + 1] + 0.5 * (xs[k] + xs[k + 2]) - v)
        uf[k + 1] = KEEP * v + a_in[k] + b_in[k] * w
    for k in range(6):
        xs[k] = smooth_xy(uf[k + 1])
    for k in range(4):
        v = uf[k + 2]
        w = 2.0 * (xs[k + 1] + 0.5 * (xs[k] + xs[k + 2]) - v)
        new = KEEP * v + a_in[k + 1] + b_in[k + 1] * w
        uf[k + 2] = new / t_in[k + 2]
        out[k] = uf[k + 2, 4:36, :]


VM = pl.BlockSpec(memory_space=pltpu.VMEM)
SM = pl.BlockSpec(memory_space=pltpu.SMEM)
HBM = pl.BlockSpec(memory_space=pltpu.HBM)


def f32(*shape):
    return jax.ShapeDtypeStruct(shape, jnp.float32)


def call(kernel, specs, outs, scratch=()):
    return pl.pallas_call(
        kernel,
        in_specs=specs,
        out_specs=jax.tree.map(lambda _: VM, outs),
        out_shape=outs,
        scratch_shapes=[
            pltpu.VMEM(shape, jnp.float32) if isinstance(shape, tuple) else shape
            for shape in scratch
        ],
        compiler_params=pltpu.CompilerParams(vmem_limit_bytes=8 * 1024 * 1024),
    )


def pre_call(*operands):
    return call(
        pre_kernel,
        [SM] + [VM] * 10,
        (
            f32(8, FR, COLS), f32(6, FR, COLS), f32(6, FR, COLS), f32(6, FR, COLS),
            f32(4, CR, CCOLS), f32(4, CROWS, CCOLS),
            f32(8, CROWS, CCOLS), f32(8, CROWS, CCOLS), f32(8, CROWS, CCOLS),
        ),
        (
            (10, FR, COLS), (8, FR, COLS), (8, FR, COLS),
            (10, FR, COLS), (8, FR, COLS), (4, FR, COLS), (4, FR, CCOLS),
        ),
    )(*operands)


def post_call(*operands):
    return call(
        post_kernel,
        [SM] + [VM] * 9,
        f32(4, ROWS, COLS),
        ((8, FR, COLS), (8, FR, CCOLS), (8, FR, COLS), (26, CR, CCOLS)),
    )(*operands)


def on_device(pressure_rhs, permeability, accumulation, coarse_perm, coarse_accum, run_lengths):
    message = f32(Z1_ROWS, COLS)
    plus, minus, across = call(
        pack_z1,
        [HBM] * 4,
        (message, message, message),
        (pltpu.VMEM((2, CROWS, CCOLS), jnp.float32), pltpu.SemaphoreType.DMA((22,))),
    )(
        *(
            pltpu.with_memory_space_constraint(x, pltpu.HBM)
            for x in (pressure_rhs, permeability, accumulation, coarse_perm)
        )
    )
    across = between_lines(across, ((0, LINE - 1),))
    plus = along_lines(plus, 1)
    minus = along_lines(minus, -1)

    slab = lax.axis_index("slab")
    pen = lax.axis_index("pen")
    starts = jnp.cumsum(run_lengths) - run_lengths
    blocks = slab - 2 + jnp.arange(6, dtype=jnp.int32)
    begins = jnp.any(starts[None, :] == blocks[:, None], axis=1)
    masks = jnp.concatenate(
        [
            jnp.stack([pen > 0, pen < lax.axis_size("pen") - 1]).astype(jnp.float32),
            1.0 - begins.astype(jnp.float32),
        ]
    )

    rows = f32(Y1_ROWS, COLS)
    up, down = call(pack_y1, [VM] * 7, (rows, rows))(
        pressure_rhs, permeability, accumulation, coarse_perm, plus, minus, across
    )
    ylo = rotated(up, "pen", 1)
    yhi = rotated(down, "pen", -1)

    t, a, b, u, ct, ab, plus, minus, across = pre_call(
        masks, pressure_rhs, permeability, accumulation, coarse_perm, coarse_accum,
        plus, minus, across, ylo, yhi,
    )
    near = between_lines(across, ((0, LINE - 1), (1, LINE - 2)))
    far = between_lines(ab, ((0, LINE - 2), (1, LINE - 3), (2, LINE - 1)))
    plus1 = along_lines(plus, 1)
    minus1 = along_lines(minus, -1)
    plus2 = along_lines(plus1[0:4], 1)
    minus2 = along_lines(minus1[0:4], -1)
    third = f32(7, CROWS, CCOLS)
    plus3 = along_lines(call(pack_plus3, [VM] * 3, third)(plus2, near, far), 1)
    minus3 = along_lines(call(pack_minus3, [VM] * 3, third)(minus2, near, far), -1)

    rows = f32(Y2_ROWS, CCOLS)
    up, down, dom, edge = call(
        pack_y2, [VM] * 10, (rows, rows, f32(26, CROWS, CCOLS), f32(8, CROWS, CCOLS))
    )(ab, u, plus1, minus1, plus2, minus2, plus3, minus3, near, far)
    ylo = rotated(up, "pen", 1)
    yhi = rotated(down, "pen", -1)

    return post_call(masks, t, a, b, u, ct, dom, edge, ylo, yhi)


def solution(mesh):
    return jax.shard_map(
        on_device,
        mesh=mesh,
        in_specs=(
            P("slab", "pen", None),
            P("slab", "pen", None),
            P("slab", "pen", None),
            P("slab", "pen", None),
            P("slab", "pen", None),
            P(),
        ),
        out_specs=P("slab", "pen", None),
        check_vma=False,
    )
```

```python
import jax
import jax.numpy as jnp
from jax import lax
from jax.experimental import pallas as pl
from jax.experimental.pallas import tpu as pltpu
from jax.sharding import PartitionSpec as P

OMEGA = 0.7
KEEP = 1.0 - OMEGA
COARSE_SWEEPS = 6

FR = 40
ROWS = 32
COLS = 256
CR = 32
CROWS = 16
CCOLS = 128


def shifted(x, axis, by):
    devices = lax.axis_size(axis)
    pairs = [(i, i + by) for i in range(devices) if 0 <= i + by < devices]
    return lax.ppermute(x, axis, pairs)


LINE = 16


def along_lines(x, by):
    slabs, pens = lax.axis_size("slab"), lax.axis_size("pen")
    pairs = []
    for slab in range(slabs):
        for pen in range(pens):
            line, z = divmod(slab, LINE)
            core = pen % 2
            step = (2 * LINE - 1 - z if core else z) + by
            step %= 2 * LINE
            core, z = (0, step) if step < LINE else (1, 2 * LINE - 1 - step)
            pairs.append((slab * pens + pen, (line * LINE + z) * pens + pen // 2 * 2 + core))
    return lax.ppermute(x, ("slab", "pen"), pairs)


def between_lines(x, by):
    slabs, pens = lax.axis_size("slab"), lax.axis_size("pen")
    pairs = []
    for source in range(slabs):
        target = source + by
        if 0 <= target < slabs and source // LINE != target // LINE:
            for pen in range(pens):
                here, there = source * pens + pen, target * pens + pen
                pairs += [(here, there), (there, here)]
    return lax.ppermute(x, ("slab", "pen"), pairs)


def place():
    return lax.axis_index("pen") % 2 == 0, lax.axis_index("slab") % LINE


class Picked:
    def __init__(self, first, one, other, end, across):
        self.parts = (first, one, other, end, across)

    def __getitem__(self, index):
        first, one, other, end, across = self.parts
        value = jnp.where(first, one[index], other[index])
        return jnp.where(end, across[index], value)


def below_above(plus, minus, rising, falling):
    first, z = place()
    return (
        Picked(first, plus, minus, z == 0, rising),
        Picked(first, minus, plus, z == LINE - 1, falling),
    )


def rotated(x, axis, by):
    devices = lax.axis_size(axis)
    return lax.ppermute(x, axis, [(i, (i + by) % devices) for i in range(devices)])


def smooth_xy(v):
    rows, cols = v.shape
    col = lax.broadcasted_iota(jnp.int32, v.shape, 1)
    left = jnp.where(col == 0, 0.0, pltpu.roll(v, 1, 1))
    right = jnp.where(col == cols - 1, 0.0, pltpu.roll(v, cols - 1, 1))
    h = v + 0.5 * (left + right)
    return h + 0.5 * (pltpu.roll(h, 1, 0) + pltpu.roll(h, rows - 1, 0))


def to_wide(x):
    return jnp.concatenate([x[0:8], x[8:16]], axis=1)


def from_wide(x):
    return jnp.concatenate([x[:, 0:CCOLS], x[:, CCOLS:COLS]], axis=0)


Z1_RHS = 96
Z1_ACC = 160
Z1_CO = 224
Z1_ROWS = 232


def pack_z1(rhs, perm, acc, cperm, plus, minus, across, held, sems):
    first, z = place()
    upward = (first, jnp.logical_not(first), z == LINE - 1)
    copies = [pltpu.make_async_copy(cperm, held, sems.at[0])]
    for out, up in zip((plus, minus, across), upward):
        for base, ref, start, count in (
            (0, perm, jnp.where(up, 1, 0), 3),
            (Z1_RHS, rhs, jnp.where(up, 2, 0), 2),
            (Z1_ACC, acc, jnp.where(up, 2, 0), 2),
        ):
            for k in range(count):
                copies.append(
                    pltpu.make_async_copy(
                        ref.at[start + k],
                        out.at[pl.ds(base + ROWS * k, ROWS)],
                        sems.at[len(copies)],
                    )
                )
    for copy in copies:
        copy.start()
    for copy in copies:
        copy.wait()
    for out, up in zip((plus, minus, across), upward):
        out[Z1_CO : Z1_CO + 8, :] = to_wide(held[jnp.where(up, 1, 0)])


def fine_rows(own, lo, hi, base, depth, z, first, count):
    if z < 0:
        at = base + 32 * (z + depth)
        return lo[at + first : at + first + count, :]
    if z > 3:
        at = base + 32 * (z - 4)
        return hi[at + first : at + first + count, :]
    return own[z, first : first + count, :]


def coarse_plane(cperm, lo, hi, c):
    if c < 0:
        return from_wide(lo[Z1_CO : Z1_CO + 8, :])
    if c > 1:
        return from_wide(hi[Z1_CO : Z1_CO + 8, :])
    return cperm[c]


Y1_RHS = 30
Y1_ACC = 46
Y1_CO = 62
Y1_ROWS = 64


def pack_y1(rhs, perm, acc, cperm, plus, minus, rising, falling, up, down):
    lo, hi = below_above(plus, minus, rising, falling)
    for out, top in ((up, True), (down, False)):
        r3 = ROWS - 3 if top else 0
        r2 = ROWS - 2 if top else 0
        for k in range(10):
            out[3 * k : 3 * k + 3, :] = fine_rows(perm, lo, hi, 0, 3, k - 3, r3, 3)
        for k in range(8):
            at = Y1_RHS + 2 * k
            out[at : at + 2, :] = fine_rows(rhs, lo, hi, Z1_RHS, 2, k - 2, r2, 2)
            at = Y1_ACC + 2 * k
            out[at : at + 2, :] = fine_rows(acc, lo, hi, Z1_ACC, 2, k - 2, r2, 2)
        rc = CROWS - 1 if top else 0
        for k in range(4):
            plane = coarse_plane(cperm, lo, hi, k - 1)
            at = Y1_CO + k // 2
            lane = CCOLS * (k % 2)
            out[at : at + 1, lane : lane + CCOLS] = plane[rc : rc + 1, :]


def pre_kernel(
    masks, rhs, perm, acc, cperm, cacc, plus, minus, rising, falling, ylo, yhi,
    t_out, a_out, b_out, u_out, ct_out, ab_out, plus_out, minus_out, across_out,
    ts, rs, cs, xs, us, ds, fs,
):
    first, place_z = place()
    lo, hi = below_above(plus, minus, rising, falling)
    mlo = masks[0]
    mhi = masks[1]
    zeros = jnp.zeros((FR, COLS), jnp.float32)
    for k in range(10):
        z = k - 3
        ts[k] = zeros
        ts[k, 4:36, :] = jnp.sqrt(fine_rows(perm, lo, hi, 0, 3, z, 0, ROWS))
        ts[k, 1:4, :] = jnp.sqrt(ylo[3 * k : 3 * k + 3, :] * mlo)
        ts[k, 36:39, :] = jnp.sqrt(yhi[3 * k : 3 * k + 3, :] * mhi)
    for k in range(8):
        z = k - 2
        for ref, own, base, ybase in ((rs, rhs, Z1_RHS, Y1_RHS), (cs, acc, Z1_ACC, Y1_ACC)):
            ref[k] = zeros
            ref[k, 4:36, :] = fine_rows(own, lo, hi, base, 2, z, 0, ROWS)
            ref[k, 2:4, :] = ylo[ybase + 2 * k : ybase + 2 * k + 2, :] * mlo
            ref[k, 36:38, :] = yhi[ybase + 2 * k : ybase + 2 * k + 2, :] * mhi
    for k in range(10):
        xs[k] = smooth_xy(ts[k])
    for k in range(8):
        t = ts[k + 1]
        w = 2.0 * (xs[k + 1] + 0.5 * (xs[k] + xs[k + 2]) - t)
        d = t * w + cs[k]
        d = jnp.where(d > 0.0, d, 1.0)
        q = OMEGA * t / d
        if 2 <= k < 6:
            ds[k - 2] = d
        t_out[k] = t
        rs_k = rs[k]
        us[k] = q * rs_k
        cs[k] = q * t
    for k in range(8):
        xs[k] = smooth_xy(us[k])
    for k in range(6):
        a = us[k + 1]
        b = cs[k + 1]
        w = 2.0 * (xs[k + 1] + 0.5 * (xs[k] + xs[k + 2]) - a)
        a_out[k] = a
        b_out[k] = b
        u_out[k] = (1.0 + KEEP) * a + b * w
    for k in range(6):
        xs[k] = smooth_xy(u_out[k])
    sums = []
    for k in range(4):
        u = u_out[k + 1]
        t = ts[k + 3]
        w = 2.0 * (xs[k + 1] + 0.5 * (xs[k] + xs[k + 2]) - u)
        r = rs[k + 2] + t * w - ds[k] * (u / t)
        sums.append(r)
    pairs = []
    for k in range(2):
        both = sums[2 * k] + sums[2 * k + 1]
        halves = []
        for half in range(2):
            at = 2 * k + half
            fs[at] = both[:, CCOLS * half : CCOLS * half + CCOLS]
            halves.append(fs[at, pl.ds(4, CROWS, 2), :] + fs[at, pl.ds(5, CROWS, 2), :])
        pairs.append(jnp.concatenate(halves, axis=1))
    stacked = jnp.concatenate(pairs, axis=0)
    src = lax.broadcasted_iota(jnp.int32, (COLS, CCOLS), 0)
    dst = lax.broadcasted_iota(jnp.int32, (COLS, CCOLS), 1)
    fold = jnp.where(src // 2 == dst, 1.0, 0.0)
    res = jnp.dot(
        stacked, fold, precision=lax.Precision.HIGHEST, preferred_element_type=jnp.float32
    )
    for k in range(4):
        ct_out[k] = jnp.zeros((CR, CCOLS), jnp.float32)
        ct_out[k, 8:24, :] = jnp.sqrt(coarse_plane(cperm, lo, hi, k - 1))
        at = Y1_CO + k // 2
        lane = CCOLS * (k % 2)
        ct_out[k, 7:8, :] = jnp.sqrt(ylo[at : at + 1, lane : lane + CCOLS] * mlo)
        ct_out[k, 24:25, :] = jnp.sqrt(yhi[at : at + 1, lane : lane + CCOLS] * mhi)
    cx = [smooth_xy(ct_out[k]) for k in range(4)]
    for k in range(2):
        t = ct_out[k + 1]
        w = 2.0 * (cx[k + 1] + 0.5 * (cx[k] + cx[k + 2]) - t)
        t = t[8:24]
        d = t * w[8:24] + cacc[k]
        q = OMEGA * t / d
        a = q * res[CROWS * k : CROWS * k + CROWS]
        b = q * t
        for out in (ab_out, plus_out, minus_out, across_out):
            out[k] = a
            out[2 + k] = b
    for out, up in (
        (plus_out, first), (minus_out, jnp.logical_not(first)), (across_out, place_z == LINE - 1)
    ):
        plane = jnp.where(up, 3, 2)
        for k in range(4):
            row = 4 + 16 * (k // 2)
            lane = CCOLS * (k % 2)
            out[4 + k] = u_out[plane, row : row + 16, lane : lane + CCOLS]


def pack_second(ab, plus1, minus1, rising1, falling1, up, down):
    lo, hi = below_above(plus1, minus1, rising1, falling1)
    up[0:4] = ab[...]
    up[4:6] = lo[0:2]
    up[6] = lo[3]
    down[0:4] = ab[...]
    down[4:7] = hi[0:3]


Y2_B = 84
Y2_U = 156
Y2_ROWS = 192


def pack_y2(
    ab, u, plus1, minus1, rising1, falling1, lo2, hi2, up, down, dom, edge
):
    lo, hi = below_above(plus1, minus1, rising1, falling1)
    for k in range(4):
        a = k < 2
        dom[6 + k if a else 17 + k] = ab[k]
        dom[4 + k if a else 15 + k] = lo[k]
        dom[8 + k if a else 19 + k] = hi[k]
        dom[2 + k if a else 13 + k] = lo2[k]
        dom[10 + k if a else 21 + k] = hi2[k]
        edge[k] = lo[4 + k]
        edge[4 + k] = hi[4 + k]
    for k in range(3):
        dom[14 if k == 2 else k] = lo2[4 + k]
        dom[25 if k == 2 else 12 + k] = hi2[4 + k]
    for out, top_rows in ((up, True), (down, False)):
        row = CROWS - 6 if top_rows else 0
        for k in range(26):
            out[6 * k : 6 * k + 6, :] = dom[k, row : row + 6, :]
        for k in range(8):
            at = Y2_U + 4 * k
            for half in range(2):
                if 0 < k < 7:
                    row = 34 if top_rows else 4
                    rows = u[k - 1, row : row + 2, CCOLS * half : CCOLS * half + CCOLS]
                else:
                    piece = (0 if k == 0 else 4) + half
                    if top_rows:
                        rows = edge[piece + 2, 14:16, :]
                    else:
                        rows = edge[piece, 0:2, :]
                out[at + 2 * half : at + 2 * half + 2, :] = rows


def post_kernel(
    masks, t_in, a_in, b_in, u_in, ct, dom, edge, ylo, yhi,
    out, uf, cf, xs, ff,
):
    mlo = masks[0]
    mhi = masks[1]
    tile = jnp.zeros((8, CCOLS), jnp.float32)
    a = []
    b = [None]
    for k in range(26):
        ff[k, 0:8, :] = tile
        ff[k, 24:32, :] = tile
        ff[k, 2:8, :] = ylo[6 * k : 6 * k + 6, :] * mlo
        ff[k, 8:24, :] = dom[k]
        ff[k, 24:30, :] = yhi[6 * k : 6 * k + 6, :] * mhi
        (a if k < 14 else b).append(ff[k])
    link = [0.5] * 13
    for j in range(6):
        link[2 * j + 1] = 0.5 * masks[2 + j]
    u = list(a)
    for sweep in range(1, COARSE_SWEEPS):
        first, last = sweep, 13 - sweep
        smooth = {k: smooth_xy(u[k]) for k in range(first - 1, last + 2)}
        fresh = list(u)
        for k in range(first, last + 1):
            w = 2.0 * (
                smooth[k] + link[k - 1] * smooth[k - 1] + link[k] * smooth[k + 1] - u[k]
            )
            fresh[k] = KEEP * u[k] + a[k] + b[k] * w
        u = fresh
    corr = []
    for k in range(4):
        t = ct[k]
        inside = t > 0.0
        corr.append(jnp.where(inside, u[5 + k] / jnp.where(inside, t, 1.0), 0.0))
    stacked = jnp.concatenate(corr, axis=0)
    dst = lax.broadcasted_iota(jnp.int32, (CCOLS, COLS), 1)
    src = lax.broadcasted_iota(jnp.int32, (CCOLS, COLS), 0)
    spread = jnp.where(dst // 2 == src, 1.0, 0.0)
    wide = jnp.dot(
        stacked, spread, precision=lax.Precision.HIGHEST, preferred_element_type=jnp.float32
    )
    for k in range(4):
        for half in range(2):
            rows = wide[CR * k + 6 : CR * k + 26, CCOLS * half : CCOLS * half + CCOLS]
            cf[2 * k + half, pl.ds(0, 20, 2), :] = rows
            cf[2 * k + half, pl.ds(1, 20, 2), :] = rows
    zeros = jnp.zeros((FR, COLS), jnp.float32)
    for k in range(8):
        if 0 < k < 7:
            uf[k] = u_in[k - 1]
        else:
            uf[k] = zeros
            piece = 0 if k == 0 else 4
            for j in range(4):
                row = 4 + 16 * (j // 2)
                lane = CCOLS * (j % 2)
                uf[k, row : row + 16, lane : lane + CCOLS] = edge[piece + j]
        at = Y2_U + 4 * k
        for half in range(2):
            lane = CCOLS * half
            uf[k, 2:4, lane : lane + CCOLS] = ylo[at + 2 * half : at + 2 * half + 2, :] * mlo
            uf[k, 36:38, lane : lane + CCOLS] = yhi[at + 2 * half : at + 2 * half + 2, :] * mhi
        both = 2 * (k // 2)
        uf[k] = uf[k] + t_in[k] * jnp.concatenate([cf[both], cf[both + 1]], axis=1)
    for k in range(8):
        xs[k] = smooth_xy(uf[k])
    for k in range(6):
        v = uf[k + 1]
        w = 2.0 * (xs[k + 1] + 0.5 * (xs[k] + xs[k + 2]) - v)
        uf[k + 1] = KEEP * v + a_in[k] + b_in[k] * w
    for k in range(6):
        xs[k] = smooth_xy(uf[k + 1])
    for k in range(4):
        v = uf[k + 2]
        w = 2.0 * (xs[k + 1] + 0.5 * (xs[k] + xs[k + 2]) - v)
        new = KEEP * v + a_in[k + 1] + b_in[k + 1] * w
        uf[k + 2] = new / t_in[k + 2]
        out[k] = uf[k + 2, 4:36, :]


VM = pl.BlockSpec(memory_space=pltpu.VMEM)
SM = pl.BlockSpec(memory_space=pltpu.SMEM)
HBM = pl.BlockSpec(memory_space=pltpu.HBM)


def f32(*shape):
    return jax.ShapeDtypeStruct(shape, jnp.float32)


def call(kernel, specs, outs, scratch=()):
    return pl.pallas_call(
        kernel,
        in_specs=specs,
        out_specs=jax.tree.map(lambda _: VM, outs),
        out_shape=outs,
        scratch_shapes=[
            pltpu.VMEM(shape, jnp.float32) if isinstance(shape, tuple) else shape
            for shape in scratch
        ],
        compiler_params=pltpu.CompilerParams(vmem_limit_bytes=8 * 1024 * 1024),
    )


def pre_call(*operands):
    return call(
        pre_kernel,
        [SM] + [VM] * 11,
        (
            f32(8, FR, COLS), f32(6, FR, COLS), f32(6, FR, COLS), f32(6, FR, COLS),
            f32(4, CR, CCOLS), f32(4, CROWS, CCOLS),
            f32(8, CROWS, CCOLS), f32(8, CROWS, CCOLS), f32(8, CROWS, CCOLS),
        ),
        (
            (10, FR, COLS), (8, FR, COLS), (8, FR, COLS),
            (10, FR, COLS), (8, FR, COLS), (4, FR, COLS), (4, FR, CCOLS),
        ),
    )(*operands)


def post_call(*operands):
    return call(
        post_kernel,
        [SM] + [VM] * 9,
        f32(4, ROWS, COLS),
        ((8, FR, COLS), (8, FR, CCOLS), (8, FR, COLS), (26, CR, CCOLS)),
    )(*operands)


def on_device(pressure_rhs, permeability, accumulation, coarse_perm, coarse_accum, run_lengths):
    message = f32(Z1_ROWS, COLS)
    plus, minus, across = call(
        pack_z1,
        [HBM] * 4,
        (message, message, message),
        (pltpu.VMEM((2, CROWS, CCOLS), jnp.float32), pltpu.SemaphoreType.DMA((22,))),
    )(
        *(
            pltpu.with_memory_space_constraint(x, pltpu.HBM)
            for x in (pressure_rhs, permeability, accumulation, coarse_perm)
        )
    )
    falling = rising = between_lines(across, 1)
    plus = along_lines(plus, 1)
    minus = along_lines(minus, -1)

    slab = lax.axis_index("slab")
    pen = lax.axis_index("pen")
    starts = jnp.cumsum(run_lengths) - run_lengths
    blocks = slab - 2 + jnp.arange(6, dtype=jnp.int32)
    begins = jnp.any(starts[None, :] == blocks[:, None], axis=1)
    masks = jnp.concatenate(
        [
            jnp.stack([pen > 0, pen < lax.axis_size("pen") - 1]).astype(jnp.float32),
            1.0 - begins.astype(jnp.float32),
        ]
    )

    rows = f32(Y1_ROWS, COLS)
    up, down = call(pack_y1, [VM] * 8, (rows, rows))(
        pressure_rhs, permeability, accumulation, coarse_perm, plus, minus, rising, falling
    )
    ylo = rotated(up, "pen", 1)
    yhi = rotated(down, "pen", -1)

    t, a, b, u, ct, ab, plus, minus, across = pre_call(
        masks, pressure_rhs, permeability, accumulation, coarse_perm, coarse_accum,
        plus, minus, rising, falling, ylo, yhi,
    )
    falling = rising = between_lines(across, 1)
    plus = along_lines(plus, 1)
    minus = along_lines(minus, -1)
    second = f32(7, CROWS, CCOLS)
    up, down = call(pack_second, [VM] * 5, (second, second))(ab, plus, minus, rising, falling)
    lo2 = shifted(up, "slab", 2)
    hi2 = shifted(down, "slab", -2)

    rows = f32(Y2_ROWS, CCOLS)
    up, down, dom, edge = call(
        pack_y2, [VM] * 8, (rows, rows, f32(26, CROWS, CCOLS), f32(8, CROWS, CCOLS))
    )(ab, u, plus, minus, rising, falling, lo2, hi2)
    ylo = rotated(up, "pen", 1)
    yhi = rotated(down, "pen", -1)

    return post_call(masks, t, a, b, u, ct, dom, edge, ylo, yhi)


def solution(mesh):
    return jax.shard_map(
        on_device,
        mesh=mesh,
        in_specs=(
            P("slab", "pen", None),
            P("slab", "pen", None),
            P("slab", "pen", None),
            P("slab", "pen", None),
            P("slab", "pen", None),
            P(),
        ),
        out_specs=P("slab", "pen", None),
        check_vma=False,
    )
```

```python
import jax
import jax.numpy as jnp
from jax import lax
from jax.experimental import pallas as pl
from jax.experimental.pallas import tpu as pltpu
from jax.sharding import PartitionSpec as P

OMEGA = 0.7
KEEP = 1.0 - OMEGA
COARSE_SWEEPS = 6

FR = 40
ROWS = 32
COLS = 256
CR = 32
CROWS = 16
CCOLS = 128


LINE = 16


def along_lines(x, by):
    slabs, pens = lax.axis_size("slab"), lax.axis_size("pen")
    pairs = []
    for slab in range(slabs):
        for pen in range(pens):
            line, z = divmod(slab, LINE)
            core = pen % 2
            step = (2 * LINE - 1 - z if core else z) + by
            step %= 2 * LINE
            core, z = (0, step) if step < LINE else (1, 2 * LINE - 1 - step)
            pairs.append((slab * pens + pen, (line * LINE + z) * pens + pen // 2 * 2 + core))
    return lax.ppermute(x, ("slab", "pen"), pairs)


def between_lines(x, apart):
    slabs, pens = lax.axis_size("slab"), lax.axis_size("pen")
    pairs = []
    for low in range(slabs - apart):
        if low // LINE != (low + apart) // LINE:
            for pen in range(pens):
                here, there = low * pens + pen, (low + apart) * pens + pen
                pairs += [(here, there), (there, here)]
    return lax.ppermute(x, ("slab", "pen"), pairs)


def place():
    return lax.axis_index("pen") % 2 == 0, lax.axis_index("slab") % LINE


class Picked:
    def __init__(self, first, one, other, end, across):
        self.parts = (first, one, other, end, across)

    def __getitem__(self, index):
        first, one, other, end, across = self.parts
        value = jnp.where(first, one[index], other[index])
        return jnp.where(end, across[index], value)


def below_above(plus, minus, across):
    first, z = place()
    return (
        Picked(first, plus, minus, z == 0, across),
        Picked(first, minus, plus, z == LINE - 1, across),
    )


def rotated(x, axis, by):
    devices = lax.axis_size(axis)
    return lax.ppermute(x, axis, [(i, (i + by) % devices) for i in range(devices)])


def smooth_xy(v):
    rows, cols = v.shape
    col = lax.broadcasted_iota(jnp.int32, v.shape, 1)
    left = jnp.where(col == 0, 0.0, pltpu.roll(v, 1, 1))
    right = jnp.where(col == cols - 1, 0.0, pltpu.roll(v, cols - 1, 1))
    h = v + 0.5 * (left + right)
    return h + 0.5 * (pltpu.roll(h, 1, 0) + pltpu.roll(h, rows - 1, 0))


def to_wide(x):
    return jnp.concatenate([x[0:8], x[8:16]], axis=1)


def from_wide(x):
    return jnp.concatenate([x[:, 0:CCOLS], x[:, CCOLS:COLS]], axis=0)


Z1_RHS = 96
Z1_ACC = 160
Z1_CO = 224
Z1_ROWS = 232


def pack_z1(rhs, perm, acc, cperm, plus, minus, across, held, sems):
    first, z = place()
    upward = (first, jnp.logical_not(first), z == LINE - 1)
    copies = [pltpu.make_async_copy(cperm, held, sems.at[0])]
    for out, up in zip((plus, minus, across), upward):
        for base, ref, start, count in (
            (0, perm, jnp.where(up, 1, 0), 3),
            (Z1_RHS, rhs, jnp.where(up, 2, 0), 2),
            (Z1_ACC, acc, jnp.where(up, 2, 0), 2),
        ):
            for k in range(count):
                copies.append(
                    pltpu.make_async_copy(
                        ref.at[start + k],
                        out.at[pl.ds(base + ROWS * k, ROWS)],
                        sems.at[len(copies)],
                    )
                )
    for copy in copies:
        copy.start()
    for copy in copies:
        copy.wait()
    for out, up in zip((plus, minus, across), upward):
        out[Z1_CO : Z1_CO + 8, :] = to_wide(held[jnp.where(up, 1, 0)])


def fine_rows(own, lo, hi, base, depth, z, first, count):
    if z < 0:
        at = base + 32 * (z + depth)
        return lo[at + first : at + first + count, :]
    if z > 3:
        at = base + 32 * (z - 4)
        return hi[at + first : at + first + count, :]
    return own[z, first : first + count, :]


def coarse_plane(cperm, lo, hi, c):
    if c < 0:
        return from_wide(lo[Z1_CO : Z1_CO + 8, :])
    if c > 1:
        return from_wide(hi[Z1_CO : Z1_CO + 8, :])
    return cperm[c]


Y1_RHS = 30
Y1_ACC = 46
Y1_CO = 62
Y1_ROWS = 64


def pack_y1(rhs, perm, acc, cperm, plus, minus, across, up, down):
    lo, hi = below_above(plus, minus, across)
    for out, top in ((up, True), (down, False)):
        r3 = ROWS - 3 if top else 0
        r2 = ROWS - 2 if top else 0
        for k in range(10):
            out[3 * k : 3 * k + 3, :] = fine_rows(perm, lo, hi, 0, 3, k - 3, r3, 3)
        for k in range(8):
            at = Y1_RHS + 2 * k
            out[at : at + 2, :] = fine_rows(rhs, lo, hi, Z1_RHS, 2, k - 2, r2, 2)
            at = Y1_ACC + 2 * k
            out[at : at + 2, :] = fine_rows(acc, lo, hi, Z1_ACC, 2, k - 2, r2, 2)
        rc = CROWS - 1 if top else 0
        for k in range(4):
            plane = coarse_plane(cperm, lo, hi, k - 1)
            at = Y1_CO + k // 2
            lane = CCOLS * (k % 2)
            out[at : at + 1, lane : lane + CCOLS] = plane[rc : rc + 1, :]


def pre_kernel(
    masks, rhs, perm, acc, cperm, cacc, plus, minus, across, ylo, yhi,
    t_out, a_out, b_out, u_out, ct_out, ab_out, plus_out, minus_out, across_out,
    ts, rs, cs, xs, us, ds, fs,
):
    first, place_z = place()
    lo, hi = below_above(plus, minus, across)
    mlo = masks[0]
    mhi = masks[1]
    zeros = jnp.zeros((FR, COLS), jnp.float32)
    for k in range(10):
        z = k - 3
        ts[k] = zeros
        ts[k, 4:36, :] = jnp.sqrt(fine_rows(perm, lo, hi, 0, 3, z, 0, ROWS))
        ts[k, 1:4, :] = jnp.sqrt(ylo[3 * k : 3 * k + 3, :] * mlo)
        ts[k, 36:39, :] = jnp.sqrt(yhi[3 * k : 3 * k + 3, :] * mhi)
    for k in range(8):
        z = k - 2
        for ref, own, base, ybase in ((rs, rhs, Z1_RHS, Y1_RHS), (cs, acc, Z1_ACC, Y1_ACC)):
            ref[k] = zeros
            ref[k, 4:36, :] = fine_rows(own, lo, hi, base, 2, z, 0, ROWS)
            ref[k, 2:4, :] = ylo[ybase + 2 * k : ybase + 2 * k + 2, :] * mlo
            ref[k, 36:38, :] = yhi[ybase + 2 * k : ybase + 2 * k + 2, :] * mhi
    for k in range(10):
        xs[k] = smooth_xy(ts[k])
    for k in range(8):
        t = ts[k + 1]
        w = 2.0 * (xs[k + 1] + 0.5 * (xs[k] + xs[k + 2]) - t)
        d = t * w + cs[k]
        d = jnp.where(d > 0.0, d, 1.0)
        q = OMEGA * t / d
        if 2 <= k < 6:
            ds[k - 2] = d
        t_out[k] = t
        rs_k = rs[k]
        us[k] = q * rs_k
        cs[k] = q * t
    for k in range(8):
        xs[k] = smooth_xy(us[k])
    for k in range(6):
        a = us[k + 1]
        b = cs[k + 1]
        w = 2.0 * (xs[k + 1] + 0.5 * (xs[k] + xs[k + 2]) - a)
        a_out[k] = a
        b_out[k] = b
        u_out[k] = (1.0 + KEEP) * a + b * w
    for k in range(6):
        xs[k] = smooth_xy(u_out[k])
    sums = []
    for k in range(4):
        u = u_out[k + 1]
        t = ts[k + 3]
        w = 2.0 * (xs[k + 1] + 0.5 * (xs[k] + xs[k + 2]) - u)
        r = rs[k + 2] + t * w - ds[k] * (u / t)
        sums.append(r)
    pairs = []
    for k in range(2):
        both = sums[2 * k] + sums[2 * k + 1]
        halves = []
        for half in range(2):
            at = 2 * k + half
            fs[at] = both[:, CCOLS * half : CCOLS * half + CCOLS]
            halves.append(fs[at, pl.ds(4, CROWS, 2), :] + fs[at, pl.ds(5, CROWS, 2), :])
        pairs.append(jnp.concatenate(halves, axis=1))
    stacked = jnp.concatenate(pairs, axis=0)
    src = lax.broadcasted_iota(jnp.int32, (COLS, CCOLS), 0)
    dst = lax.broadcasted_iota(jnp.int32, (COLS, CCOLS), 1)
    fold = jnp.where(src // 2 == dst, 1.0, 0.0)
    res = jnp.dot(
        stacked, fold, precision=lax.Precision.HIGHEST, preferred_element_type=jnp.float32
    )
    for k in range(4):
        ct_out[k] = jnp.zeros((CR, CCOLS), jnp.float32)
        ct_out[k, 8:24, :] = jnp.sqrt(coarse_plane(cperm, lo, hi, k - 1))
        at = Y1_CO + k // 2
        lane = CCOLS * (k % 2)
        ct_out[k, 7:8, :] = jnp.sqrt(ylo[at : at + 1, lane : lane + CCOLS] * mlo)
        ct_out[k, 24:25, :] = jnp.sqrt(yhi[at : at + 1, lane : lane + CCOLS] * mhi)
    cx = [smooth_xy(ct_out[k]) for k in range(4)]
    for k in range(2):
        t = ct_out[k + 1]
        w = 2.0 * (cx[k + 1] + 0.5 * (cx[k] + cx[k + 2]) - t)
        t = t[8:24]
        d = t * w[8:24] + cacc[k]
        q = OMEGA * t / d
        a = q * res[CROWS * k : CROWS * k + CROWS]
        b = q * t
        for out in (ab_out, plus_out, minus_out, across_out):
            out[k] = a
            out[2 + k] = b
    for out, up in (
        (plus_out, first), (minus_out, jnp.logical_not(first)), (across_out, place_z == LINE - 1)
    ):
        plane = jnp.where(up, 3, 2)
        for k in range(4):
            row = 4 + 16 * (k // 2)
            lane = CCOLS * (k % 2)
            out[4 + k] = u_out[plane, row : row + 16, lane : lane + CCOLS]


def pack_far(ab, plus1, minus1, out):
    first, z = place()
    near_start = z < LINE // 2
    out[0:4] = ab[...]
    out[4:8] = jnp.where(first == near_start, plus1[0:4], minus1[0:4])


Y2_B = 84
Y2_U = 156
Y2_ROWS = 192


def pack_y2(
    ab, u, plus1, minus1, across, plus2, minus2, plus3, minus3, far, up, down, dom, edge
):
    first, z = place()

    def below(plus, minus, k, places, other):
        return jnp.where(z < places, other, jnp.where(first, plus[k], minus[k]))

    def above(plus, minus, k, places, other):
        return jnp.where(z >= LINE - places, other, jnp.where(first, minus[k], plus[k]))

    for k in range(4):
        a = k < 2
        dom[6 + k if a else 17 + k] = ab[k]
        dom[4 + k if a else 15 + k] = below(plus1, minus1, k, 1, across[k])
        dom[8 + k if a else 19 + k] = above(plus1, minus1, k, 1, across[k])
        dom[2 + k if a else 13 + k] = below(plus2, minus2, k, 2, far[4 + k])
        dom[10 + k if a else 21 + k] = above(plus2, minus2, k, 2, far[4 + k])
        edge[k] = below(plus1, minus1, 4 + k, 1, across[4 + k])
        edge[4 + k] = above(plus1, minus1, 4 + k, 1, across[4 + k])
    for k in range(3):
        low = 3 if k == 2 else k
        dom[14 if k == 2 else k] = below(plus3, minus3, low, 3, far[low])
        dom[25 if k == 2 else 12 + k] = above(plus3, minus3, k, 3, far[k])
    for out, top_rows in ((up, True), (down, False)):
        row = CROWS - 6 if top_rows else 0
        for k in range(26):
            out[6 * k : 6 * k + 6, :] = dom[k, row : row + 6, :]
        for k in range(8):
            at = Y2_U + 4 * k
            for half in range(2):
                if 0 < k < 7:
                    row = 34 if top_rows else 4
                    rows = u[k - 1, row : row + 2, CCOLS * half : CCOLS * half + CCOLS]
                else:
                    piece = (0 if k == 0 else 4) + half
                    if top_rows:
                        rows = edge[piece + 2, 14:16, :]
                    else:
                        rows = edge[piece, 0:2, :]
                out[at + 2 * half : at + 2 * half + 2, :] = rows


def post_kernel(
    masks, t_in, a_in, b_in, u_in, ct, dom, edge, ylo, yhi,
    out, uf, cf, xs, ff,
):
    mlo = masks[0]
    mhi = masks[1]
    tile = jnp.zeros((8, CCOLS), jnp.float32)
    a = []
    b = [None]
    for k in range(26):
        ff[k, 0:8, :] = tile
        ff[k, 24:32, :] = tile
        ff[k, 2:8, :] = ylo[6 * k : 6 * k + 6, :] * mlo
        ff[k, 8:24, :] = dom[k]
        ff[k, 24:30, :] = yhi[6 * k : 6 * k + 6, :] * mhi
        (a if k < 14 else b).append(ff[k])
    link = [0.5] * 13
    for j in range(6):
        link[2 * j + 1] = 0.5 * masks[2 + j]
    u = list(a)
    for sweep in range(1, COARSE_SWEEPS):
        first, last = sweep, 13 - sweep
        smooth = {k: smooth_xy(u[k]) for k in range(first - 1, last + 2)}
        fresh = list(u)
        for k in range(first, last + 1):
            w = 2.0 * (
                smooth[k] + link[k - 1] * smooth[k - 1] + link[k] * smooth[k + 1] - u[k]
            )
            fresh[k] = KEEP * u[k] + a[k] + b[k] * w
        u = fresh
    corr = []
    for k in range(4):
        t = ct[k]
        inside = t > 0.0
        corr.append(jnp.where(inside, u[5 + k] / jnp.where(inside, t, 1.0), 0.0))
    stacked = jnp.concatenate(corr, axis=0)
    dst = lax.broadcasted_iota(jnp.int32, (CCOLS, COLS), 1)
    src = lax.broadcasted_iota(jnp.int32, (CCOLS, COLS), 0)
    spread = jnp.where(dst // 2 == src, 1.0, 0.0)
    wide = jnp.dot(
        stacked, spread, precision=lax.Precision.HIGHEST, preferred_element_type=jnp.float32
    )
    for k in range(4):
        for half in range(2):
            rows = wide[CR * k + 6 : CR * k + 26, CCOLS * half : CCOLS * half + CCOLS]
            cf[2 * k + half, pl.ds(0, 20, 2), :] = rows
            cf[2 * k + half, pl.ds(1, 20, 2), :] = rows
    zeros = jnp.zeros((FR, COLS), jnp.float32)
    for k in range(8):
        if 0 < k < 7:
            uf[k] = u_in[k - 1]
        else:
            uf[k] = zeros
            piece = 0 if k == 0 else 4
            for j in range(4):
                row = 4 + 16 * (j // 2)
                lane = CCOLS * (j % 2)
                uf[k, row : row + 16, lane : lane + CCOLS] = edge[piece + j]
        at = Y2_U + 4 * k
        for half in range(2):
            lane = CCOLS * half
            uf[k, 2:4, lane : lane + CCOLS] = ylo[at + 2 * half : at + 2 * half + 2, :] * mlo
            uf[k, 36:38, lane : lane + CCOLS] = yhi[at + 2 * half : at + 2 * half + 2, :] * mhi
        both = 2 * (k // 2)
        uf[k] = uf[k] + t_in[k] * jnp.concatenate([cf[both], cf[both + 1]], axis=1)
    for k in range(8):
        xs[k] = smooth_xy(uf[k])
    for k in range(6):
        v = uf[k + 1]
        w = 2.0 * (xs[k + 1] + 0.5 * (xs[k] + xs[k + 2]) - v)
        uf[k + 1] = KEEP * v + a_in[k] + b_in[k] * w
    for k in range(6):
        xs[k] = smooth_xy(uf[k + 1])
    for k in range(4):
        v = uf[k + 2]
        w = 2.0 * (xs[k + 1] + 0.5 * (xs[k] + xs[k + 2]) - v)
        new = KEEP * v + a_in[k + 1] + b_in[k + 1] * w
        uf[k + 2] = new / t_in[k + 2]
        out[k] = uf[k + 2, 4:36, :]


VM = pl.BlockSpec(memory_space=pltpu.VMEM)
SM = pl.BlockSpec(memory_space=pltpu.SMEM)
HBM = pl.BlockSpec(memory_space=pltpu.HBM)


def f32(*shape):
    return jax.ShapeDtypeStruct(shape, jnp.float32)


def call(kernel, specs, outs, scratch=()):
    return pl.pallas_call(
        kernel,
        in_specs=specs,
        out_specs=jax.tree.map(lambda _: VM, outs),
        out_shape=outs,
        scratch_shapes=[
            pltpu.VMEM(shape, jnp.float32) if isinstance(shape, tuple) else shape
            for shape in scratch
        ],
        compiler_params=pltpu.CompilerParams(vmem_limit_bytes=8 * 1024 * 1024),
    )


def pre_call(*operands):
    return call(
        pre_kernel,
        [SM] + [VM] * 10,
        (
            f32(8, FR, COLS), f32(6, FR, COLS), f32(6, FR, COLS), f32(6, FR, COLS),
            f32(4, CR, CCOLS), f32(4, CROWS, CCOLS),
            f32(8, CROWS, CCOLS), f32(8, CROWS, CCOLS), f32(8, CROWS, CCOLS),
        ),
        (
            (10, FR, COLS), (8, FR, COLS), (8, FR, COLS),
            (10, FR, COLS), (8, FR, COLS), (4, FR, COLS), (4, FR, CCOLS),
        ),
    )(*operands)


def post_call(*operands):
    return call(
        post_kernel,
        [SM] + [VM] * 9,
        f32(4, ROWS, COLS),
        ((8, FR, COLS), (8, FR, CCOLS), (8, FR, COLS), (26, CR, CCOLS)),
    )(*operands)


def on_device(pressure_rhs, permeability, accumulation, coarse_perm, coarse_accum, run_lengths):
    message = f32(Z1_ROWS, COLS)
    plus, minus, across = call(
        pack_z1,
        [HBM] * 4,
        (message, message, message),
        (pltpu.VMEM((2, CROWS, CCOLS), jnp.float32), pltpu.SemaphoreType.DMA((22,))),
    )(
        *(
            pltpu.with_memory_space_constraint(x, pltpu.HBM)
            for x in (pressure_rhs, permeability, accumulation, coarse_perm)
        )
    )
    across = between_lines(across, 1)
    plus = along_lines(plus, 1)
    minus = along_lines(minus, -1)

    slab = lax.axis_index("slab")
    pen = lax.axis_index("pen")
    starts = jnp.cumsum(run_lengths) - run_lengths
    blocks = slab - 2 + jnp.arange(6, dtype=jnp.int32)
    begins = jnp.any(starts[None, :] == blocks[:, None], axis=1)
    masks = jnp.concatenate(
        [
            jnp.stack([pen > 0, pen < lax.axis_size("pen") - 1]).astype(jnp.float32),
            1.0 - begins.astype(jnp.float32),
        ]
    )

    rows = f32(Y1_ROWS, COLS)
    up, down = call(pack_y1, [VM] * 7, (rows, rows))(
        pressure_rhs, permeability, accumulation, coarse_perm, plus, minus, across
    )
    ylo = rotated(up, "pen", 1)
    yhi = rotated(down, "pen", -1)

    t, a, b, u, ct, ab, plus, minus, across = pre_call(
        masks, pressure_rhs, permeability, accumulation, coarse_perm, coarse_accum,
        plus, minus, across, ylo, yhi,
    )
    across = between_lines(across, 1)
    plus1 = along_lines(plus, 1)
    minus1 = along_lines(minus, -1)
    far = between_lines(
        call(pack_far, [VM] * 3, f32(8, CROWS, CCOLS))(ab, plus1, minus1), 3
    )
    plus2 = along_lines(plus1[0:4], 1)
    minus2 = along_lines(minus1[0:4], -1)
    plus3 = along_lines(plus2, 1)
    minus3 = along_lines(minus2, -1)

    rows = f32(Y2_ROWS, CCOLS)
    up, down, dom, edge = call(
        pack_y2, [VM] * 10, (rows, rows, f32(26, CROWS, CCOLS), f32(8, CROWS, CCOLS))
    )(ab, u, plus1, minus1, across, plus2, minus2, plus3, minus3, far)
    ylo = rotated(up, "pen", 1)
    yhi = rotated(down, "pen", -1)

    return post_call(masks, t, a, b, u, ct, dom, edge, ylo, yhi)


def solution(mesh):
    return jax.shard_map(
        on_device,
        mesh=mesh,
        in_specs=(
            P("slab", "pen", None),
            P("slab", "pen", None),
            P("slab", "pen", None),
            P("slab", "pen", None),
            P("slab", "pen", None),
            P(),
        ),
        out_specs=P("slab", "pen", None),
        check_vma=False,
    )
```

```python
import jax
import jax.numpy as jnp
from jax import lax
from jax.experimental import pallas as pl
from jax.experimental.pallas import tpu as pltpu
from jax.sharding import PartitionSpec as P

OMEGA = 0.7
KEEP = 1.0 - OMEGA
COARSE_SWEEPS = 6

FR = 40
ROWS = 32
COLS = 256
CR = 32
CROWS = 16
CCOLS = 128


LINE = 16


def along_lines(x, by):
    slabs, pens = lax.axis_size("slab"), lax.axis_size("pen")
    pairs = []
    for slab in range(slabs):
        for pen in range(pens):
            line, z = divmod(slab, LINE)
            core = pen % 2
            step = (2 * LINE - 1 - z if core else z) + by
            step %= 2 * LINE
            core, z = (0, step) if step < LINE else (1, 2 * LINE - 1 - step)
            pairs.append((slab * pens + pen, (line * LINE + z) * pens + pen // 2 * 2 + core))
    return lax.ppermute(x, ("slab", "pen"), pairs)


def between_lines(x, apart):
    slabs, pens = lax.axis_size("slab"), lax.axis_size("pen")
    pairs = []
    for low in range(slabs - apart):
        if low // LINE != (low + apart) // LINE:
            for pen in range(pens):
                here, there = low * pens + pen, (low + apart) * pens + pen
                pairs += [(here, there), (there, here)]
    return lax.ppermute(x, ("slab", "pen"), pairs)


def place():
    return lax.axis_index("pen") % 2 == 0, lax.axis_index("slab") % LINE


class Picked:
    def __init__(self, first, one, other, end, across):
        self.parts = (first, one, other, end, across)

    def __getitem__(self, index):
        first, one, other, end, across = self.parts
        value = jnp.where(first, one[index], other[index])
        return jnp.where(end, across[index], value)


def below_above(plus, minus, across):
    first, z = place()
    return (
        Picked(first, plus, minus, z == 0, across),
        Picked(first, minus, plus, z == LINE - 1, across),
    )


def rotated(x, axis, by):
    devices = lax.axis_size(axis)
    return lax.ppermute(x, axis, [(i, (i + by) % devices) for i in range(devices)])


def smooth_xy(v):
    rows, cols = v.shape
    col = lax.broadcasted_iota(jnp.int32, v.shape, 1)
    left = jnp.where(col == 0, 0.0, pltpu.roll(v, 1, 1))
    right = jnp.where(col == cols - 1, 0.0, pltpu.roll(v, cols - 1, 1))
    h = v + 0.5 * (left + right)
    return h + 0.5 * (pltpu.roll(h, 1, 0) + pltpu.roll(h, rows - 1, 0))


def to_wide(x):
    return jnp.concatenate([x[0:8], x[8:16]], axis=1)


def from_wide(x):
    return jnp.concatenate([x[:, 0:CCOLS], x[:, CCOLS:COLS]], axis=0)


Z1_RHS = 96
Z1_ACC = 160
Z1_CO = 224
Z1_ROWS = 232


def pack_z1(rhs, perm, acc, cperm, plus, minus, across, held, sems):
    first, z = place()
    upward = (first, jnp.logical_not(first), z == LINE - 1)
    copies = [pltpu.make_async_copy(cperm, held, sems.at[0])]
    for out, up in zip((plus, minus, across), upward):
        for base, ref, start, count in (
            (0, perm, jnp.where(up, ROWS, 0), 3),
            (Z1_RHS, rhs, jnp.where(up, 2 * ROWS, 0), 2),
            (Z1_ACC, acc, jnp.where(up, 2 * ROWS, 0), 2),
        ):
            copies.append(
                pltpu.make_async_copy(
                    ref.at[pl.ds(pl.multiple_of(start, ROWS), ROWS * count)],
                    out.at[pl.ds(base, ROWS * count)],
                    sems.at[len(copies)],
                )
            )
    for copy in copies:
        copy.start()
    for copy in copies:
        copy.wait()
    for out, up in zip((plus, minus, across), upward):
        out[Z1_CO : Z1_CO + 8, :] = to_wide(held[jnp.where(up, 1, 0)])


def fine_rows(own, lo, hi, base, depth, z, first, count):
    if z < 0:
        at = base + 32 * (z + depth)
        return lo[at + first : at + first + count, :]
    if z > 3:
        at = base + 32 * (z - 4)
        return hi[at + first : at + first + count, :]
    return own[z, first : first + count, :]


def coarse_plane(cperm, lo, hi, c):
    if c < 0:
        return from_wide(lo[Z1_CO : Z1_CO + 8, :])
    if c > 1:
        return from_wide(hi[Z1_CO : Z1_CO + 8, :])
    return cperm[c]


Y1_RHS = 30
Y1_ACC = 46
Y1_CO = 62
Y1_ROWS = 64


def pack_y1(rhs, perm, acc, cperm, plus, minus, across, up, down):
    lo, hi = below_above(plus, minus, across)
    for out, top in ((up, True), (down, False)):
        r3 = ROWS - 3 if top else 0
        r2 = ROWS - 2 if top else 0
        for k in range(10):
            out[3 * k : 3 * k + 3, :] = fine_rows(perm, lo, hi, 0, 3, k - 3, r3, 3)
        for k in range(8):
            at = Y1_RHS + 2 * k
            out[at : at + 2, :] = fine_rows(rhs, lo, hi, Z1_RHS, 2, k - 2, r2, 2)
            at = Y1_ACC + 2 * k
            out[at : at + 2, :] = fine_rows(acc, lo, hi, Z1_ACC, 2, k - 2, r2, 2)
        rc = CROWS - 1 if top else 0
        for k in range(4):
            plane = coarse_plane(cperm, lo, hi, k - 1)
            at = Y1_CO + k // 2
            lane = CCOLS * (k % 2)
            out[at : at + 1, lane : lane + CCOLS] = plane[rc : rc + 1, :]


def pre_kernel(
    masks, rhs, perm, acc, cperm, cacc, plus, minus, across, ylo, yhi,
    t_out, a_out, b_out, u_out, ct_out, ab_out, plus_out, minus_out, across_out,
    ts, rs, cs, xs, us, ds, fs,
):
    first, place_z = place()
    lo, hi = below_above(plus, minus, across)
    mlo = masks[0]
    mhi = masks[1]
    zeros = jnp.zeros((FR, COLS), jnp.float32)
    for k in range(10):
        z = k - 3
        ts[k] = zeros
        ts[k, 4:36, :] = jnp.sqrt(fine_rows(perm, lo, hi, 0, 3, z, 0, ROWS))
        ts[k, 1:4, :] = jnp.sqrt(ylo[3 * k : 3 * k + 3, :] * mlo)
        ts[k, 36:39, :] = jnp.sqrt(yhi[3 * k : 3 * k + 3, :] * mhi)
    for k in range(8):
        z = k - 2
        for ref, own, base, ybase in ((rs, rhs, Z1_RHS, Y1_RHS), (cs, acc, Z1_ACC, Y1_ACC)):
            ref[k] = zeros
            ref[k, 4:36, :] = fine_rows(own, lo, hi, base, 2, z, 0, ROWS)
            ref[k, 2:4, :] = ylo[ybase + 2 * k : ybase + 2 * k + 2, :] * mlo
            ref[k, 36:38, :] = yhi[ybase + 2 * k : ybase + 2 * k + 2, :] * mhi
    for k in range(10):
        xs[k] = smooth_xy(ts[k])
    for k in range(8):
        t = ts[k + 1]
        w = 2.0 * (xs[k + 1] + 0.5 * (xs[k] + xs[k + 2]) - t)
        d = t * w + cs[k]
        d = jnp.where(d > 0.0, d, 1.0)
        q = OMEGA * t / d
        if 2 <= k < 6:
            ds[k - 2] = d
        t_out[k] = t
        rs_k = rs[k]
        us[k] = q * rs_k
        cs[k] = q * t
    for k in range(8):
        xs[k] = smooth_xy(us[k])
    for k in range(6):
        a = us[k + 1]
        b = cs[k + 1]
        w = 2.0 * (xs[k + 1] + 0.5 * (xs[k] + xs[k + 2]) - a)
        a_out[k] = a
        b_out[k] = b
        u_out[k] = (1.0 + KEEP) * a + b * w
    for k in range(6):
        xs[k] = smooth_xy(u_out[k])
    sums = []
    for k in range(4):
        u = u_out[k + 1]
        t = ts[k + 3]
        w = 2.0 * (xs[k + 1] + 0.5 * (xs[k] + xs[k + 2]) - u)
        r = rs[k + 2] + t * w - ds[k] * (u / t)
        sums.append(r)
    pairs = []
    for k in range(2):
        both = sums[2 * k] + sums[2 * k + 1]
        halves = []
        for half in range(2):
            at = 2 * k + half
            fs[at] = both[:, CCOLS * half : CCOLS * half + CCOLS]
            halves.append(fs[at, pl.ds(4, CROWS, 2), :] + fs[at, pl.ds(5, CROWS, 2), :])
        pairs.append(jnp.concatenate(halves, axis=1))
    stacked = jnp.concatenate(pairs, axis=0)
    src = lax.broadcasted_iota(jnp.int32, (COLS, CCOLS), 0)
    dst = lax.broadcasted_iota(jnp.int32, (COLS, CCOLS), 1)
    fold = jnp.where(src // 2 == dst, 1.0, 0.0)
    res = jnp.dot(
        stacked, fold, precision=lax.Precision.HIGHEST, preferred_element_type=jnp.float32
    )
    for k in range(4):
        ct_out[k] = jnp.zeros((CR, CCOLS), jnp.float32)
        ct_out[k, 8:24, :] = jnp.sqrt(coarse_plane(cperm, lo, hi, k - 1))
        at = Y1_CO + k // 2
        lane = CCOLS * (k % 2)
        ct_out[k, 7:8, :] = jnp.sqrt(ylo[at : at + 1, lane : lane + CCOLS] * mlo)
        ct_out[k, 24:25, :] = jnp.sqrt(yhi[at : at + 1, lane : lane + CCOLS] * mhi)
    cx = [smooth_xy(ct_out[k]) for k in range(4)]
    for k in range(2):
        t = ct_out[k + 1]
        w = 2.0 * (cx[k + 1] + 0.5 * (cx[k] + cx[k + 2]) - t)
        t = t[8:24]
        d = t * w[8:24] + cacc[k]
        q = OMEGA * t / d
        a = q * res[CROWS * k : CROWS * k + CROWS]
        b = q * t
        for out in (ab_out, plus_out, minus_out, across_out):
            out[k] = a
            out[2 + k] = b
    for out, up in (
        (plus_out, first), (minus_out, jnp.logical_not(first)), (across_out, place_z == LINE - 1)
    ):
        plane = jnp.where(up, 3, 2)
        for k in range(4):
            row = 4 + 16 * (k // 2)
            lane = CCOLS * (k % 2)
            out[4 + k] = u_out[plane, row : row + 16, lane : lane + CCOLS]


def pack_far(ab, plus1, minus1, out):
    first, z = place()
    near_start = z < LINE // 2
    out[0:2] = ab[0:2]
    out[2] = ab[jnp.where(near_start, 2, 3)]
    out[3:7] = jnp.where(first == near_start, plus1[0:4], minus1[0:4])


Y2_B = 84
Y2_U = 156
Y2_ROWS = 192


def pack_y2(
    ab, u, plus1, minus1, across, plus2, minus2, plus3, minus3, far, up, down, dom, edge
):
    first, z = place()

    def below(plus, minus, k, places, other):
        return jnp.where(z < places, other, jnp.where(first, plus[k], minus[k]))

    def above(plus, minus, k, places, other):
        return jnp.where(z >= LINE - places, other, jnp.where(first, minus[k], plus[k]))

    for k in range(4):
        a = k < 2
        dom[6 + k if a else 17 + k] = ab[k]
        dom[4 + k if a else 15 + k] = below(plus1, minus1, k, 1, across[k])
        dom[8 + k if a else 19 + k] = above(plus1, minus1, k, 1, across[k])
        dom[2 + k if a else 13 + k] = below(plus2, minus2, k, 2, far[3 + k])
        dom[10 + k if a else 21 + k] = above(plus2, minus2, k, 2, far[3 + k])
        edge[k] = below(plus1, minus1, 4 + k, 1, across[4 + k])
        edge[4 + k] = above(plus1, minus1, 4 + k, 1, across[4 + k])
    for k in range(3):
        low = 3 if k == 2 else k
        dom[14 if k == 2 else k] = below(plus3, minus3, low, 3, far[k])
        dom[25 if k == 2 else 12 + k] = above(plus3, minus3, k, 3, far[k])
    for out, top_rows in ((up, True), (down, False)):
        row = CROWS - 6 if top_rows else 0
        for k in range(26):
            out[6 * k : 6 * k + 6, :] = dom[k, row : row + 6, :]
        for k in range(8):
            at = Y2_U + 4 * k
            for half in range(2):
                if 0 < k < 7:
                    row = 34 if top_rows else 4
                    rows = u[k - 1, row : row + 2, CCOLS * half : CCOLS * half + CCOLS]
                else:
                    piece = (0 if k == 0 else 4) + half
                    if top_rows:
                        rows = edge[piece + 2, 14:16, :]
                    else:
                        rows = edge[piece, 0:2, :]
                out[at + 2 * half : at + 2 * half + 2, :] = rows


def post_kernel(
    masks, t_in, a_in, b_in, u_in, ct, dom, edge, ylo, yhi,
    out, uf, cf, xs, ff,
):
    mlo = masks[0]
    mhi = masks[1]
    tile = jnp.zeros((8, CCOLS), jnp.float32)
    a = []
    b = [None]
    for k in range(26):
        ff[k, 0:8, :] = tile
        ff[k, 24:32, :] = tile
        ff[k, 2:8, :] = ylo[6 * k : 6 * k + 6, :] * mlo
        ff[k, 8:24, :] = dom[k]
        ff[k, 24:30, :] = yhi[6 * k : 6 * k + 6, :] * mhi
        (a if k < 14 else b).append(ff[k])
    link = [0.5] * 13
    for j in range(6):
        link[2 * j + 1] = 0.5 * masks[2 + j]
    u = list(a)
    for sweep in range(1, COARSE_SWEEPS):
        first, last = sweep, 13 - sweep
        smooth = {k: smooth_xy(u[k]) for k in range(first - 1, last + 2)}
        fresh = list(u)
        for k in range(first, last + 1):
            w = 2.0 * (
                smooth[k] + link[k - 1] * smooth[k - 1] + link[k] * smooth[k + 1] - u[k]
            )
            fresh[k] = KEEP * u[k] + a[k] + b[k] * w
        u = fresh
    corr = []
    for k in range(4):
        t = ct[k]
        inside = t > 0.0
        corr.append(jnp.where(inside, u[5 + k] / jnp.where(inside, t, 1.0), 0.0))
    stacked = jnp.concatenate(corr, axis=0)
    dst = lax.broadcasted_iota(jnp.int32, (CCOLS, COLS), 1)
    src = lax.broadcasted_iota(jnp.int32, (CCOLS, COLS), 0)
    spread = jnp.where(dst // 2 == src, 1.0, 0.0)
    wide = jnp.dot(
        stacked, spread, precision=lax.Precision.HIGHEST, preferred_element_type=jnp.float32
    )
    for k in range(4):
        for half in range(2):
            rows = wide[CR * k + 6 : CR * k + 26, CCOLS * half : CCOLS * half + CCOLS]
            cf[2 * k + half, pl.ds(0, 20, 2), :] = rows
            cf[2 * k + half, pl.ds(1, 20, 2), :] = rows
    zeros = jnp.zeros((FR, COLS), jnp.float32)
    for k in range(8):
        if 0 < k < 7:
            uf[k] = u_in[k - 1]
        else:
            uf[k] = zeros
            piece = 0 if k == 0 else 4
            for j in range(4):
                row = 4 + 16 * (j // 2)
                lane = CCOLS * (j % 2)
                uf[k, row : row + 16, lane : lane + CCOLS] = edge[piece + j]
        at = Y2_U + 4 * k
        for half in range(2):
            lane = CCOLS * half
            uf[k, 2:4, lane : lane + CCOLS] = ylo[at + 2 * half : at + 2 * half + 2, :] * mlo
            uf[k, 36:38, lane : lane + CCOLS] = yhi[at + 2 * half : at + 2 * half + 2, :] * mhi
        both = 2 * (k // 2)
        uf[k] = uf[k] + t_in[k] * jnp.concatenate([cf[both], cf[both + 1]], axis=1)
    for k in range(8):
        xs[k] = smooth_xy(uf[k])
    for k in range(6):
        v = uf[k + 1]
        w = 2.0 * (xs[k + 1] + 0.5 * (xs[k] + xs[k + 2]) - v)
        uf[k + 1] = KEEP * v + a_in[k] + b_in[k] * w
    for k in range(6):
        xs[k] = smooth_xy(uf[k + 1])
    for k in range(4):
        v = uf[k + 2]
        w = 2.0 * (xs[k + 1] + 0.5 * (xs[k] + xs[k + 2]) - v)
        new = KEEP * v + a_in[k + 1] + b_in[k + 1] * w
        uf[k + 2] = new / t_in[k + 2]
        out[k] = uf[k + 2, 4:36, :]


VM = pl.BlockSpec(memory_space=pltpu.VMEM)
SM = pl.BlockSpec(memory_space=pltpu.SMEM)
HBM = pl.BlockSpec(memory_space=pltpu.HBM)


def f32(*shape):
    return jax.ShapeDtypeStruct(shape, jnp.float32)


def call(kernel, specs, outs, scratch=()):
    return pl.pallas_call(
        kernel,
        in_specs=specs,
        out_specs=jax.tree.map(lambda _: VM, outs),
        out_shape=outs,
        scratch_shapes=[
            pltpu.VMEM(shape, jnp.float32) if isinstance(shape, tuple) else shape
            for shape in scratch
        ],
        compiler_params=pltpu.CompilerParams(vmem_limit_bytes=8 * 1024 * 1024),
    )


def pre_call(*operands):
    return call(
        pre_kernel,
        [SM] + [VM] * 10,
        (
            f32(8, FR, COLS), f32(6, FR, COLS), f32(6, FR, COLS), f32(6, FR, COLS),
            f32(4, CR, CCOLS), f32(4, CROWS, CCOLS),
            f32(8, CROWS, CCOLS), f32(8, CROWS, CCOLS), f32(8, CROWS, CCOLS),
        ),
        (
            (10, FR, COLS), (8, FR, COLS), (8, FR, COLS),
            (10, FR, COLS), (8, FR, COLS), (4, FR, COLS), (4, FR, CCOLS),
        ),
    )(*operands)


def post_call(*operands):
    return call(
        post_kernel,
        [SM] + [VM] * 9,
        f32(4, ROWS, COLS),
        ((8, FR, COLS), (8, FR, CCOLS), (8, FR, COLS), (26, CR, CCOLS)),
    )(*operands)


def on_device(pressure_rhs, permeability, accumulation, coarse_perm, coarse_accum, run_lengths):
    message = f32(Z1_ROWS, COLS)
    plus, minus, across = call(
        pack_z1,
        [HBM] * 4,
        (message, message, message),
        (pltpu.VMEM((2, CROWS, CCOLS), jnp.float32), pltpu.SemaphoreType.DMA((10,))),
    )(
        *(
            pltpu.with_memory_space_constraint(x, pltpu.HBM)
            for x in (
                pressure_rhs.reshape(-1, COLS),
                permeability.reshape(-1, COLS),
                accumulation.reshape(-1, COLS),
                coarse_perm,
            )
        )
    )
    across = between_lines(across, 1)
    plus = along_lines(plus, 1)
    minus = along_lines(minus, -1)

    slab = lax.axis_index("slab")
    pen = lax.axis_index("pen")
    starts = jnp.cumsum(run_lengths) - run_lengths
    blocks = slab - 2 + jnp.arange(6, dtype=jnp.int32)
    begins = jnp.any(starts[None, :] == blocks[:, None], axis=1)
    masks = jnp.concatenate(
        [
            jnp.stack([pen > 0, pen < lax.axis_size("pen") - 1]).astype(jnp.float32),
            1.0 - begins.astype(jnp.float32),
        ]
    )

    rows = f32(Y1_ROWS, COLS)
    up, down = call(pack_y1, [VM] * 7, (rows, rows))(
        pressure_rhs, permeability, accumulation, coarse_perm, plus, minus, across
    )
    ylo = rotated(up, "pen", 1)
    yhi = rotated(down, "pen", -1)

    t, a, b, u, ct, ab, plus, minus, across = pre_call(
        masks, pressure_rhs, permeability, accumulation, coarse_perm, coarse_accum,
        plus, minus, across, ylo, yhi,
    )
    across = between_lines(across, 1)
    plus1 = along_lines(plus, 1)
    minus1 = along_lines(minus, -1)
    far = between_lines(
        call(pack_far, [VM] * 3, f32(7, CROWS, CCOLS))(ab, plus1, minus1), 3
    )
    plus2 = along_lines(plus1[0:4], 1)
    minus2 = along_lines(minus1[0:4], -1)
    plus3 = along_lines(plus2, 1)
    minus3 = along_lines(minus2, -1)

    rows = f32(Y2_ROWS, CCOLS)
    up, down, dom, edge = call(
        pack_y2, [VM] * 10, (rows, rows, f32(26, CROWS, CCOLS), f32(8, CROWS, CCOLS))
    )(ab, u, plus1, minus1, across, plus2, minus2, plus3, minus3, far)
    ylo = rotated(up, "pen", 1)
    yhi = rotated(down, "pen", -1)

    return post_call(masks, t, a, b, u, ct, dom, edge, ylo, yhi)


def solution(mesh):
    return jax.shard_map(
        on_device,
        mesh=mesh,
        in_specs=(
            P("slab", "pen", None),
            P("slab", "pen", None),
            P("slab", "pen", None),
            P("slab", "pen", None),
            P("slab", "pen", None),
            P(),
        ),
        out_specs=P("slab", "pen", None),
        check_vma=False,
    )
```

```python
import jax
import jax.numpy as jnp
from jax import lax
from jax.experimental import pallas as pl
from jax.experimental.pallas import tpu as pltpu
from jax.sharding import PartitionSpec as P

OMEGA = 0.7
KEEP = 1.0 - OMEGA
COARSE_SWEEPS = 6

FR = 40
ROWS = 32
COLS = 256
CR = 32
CROWS = 16
CCOLS = 128


LINE = 16


def along_lines(x, by):
    slabs, pens = lax.axis_size("slab"), lax.axis_size("pen")
    pairs = []
    for slab in range(slabs):
        for pen in range(pens):
            line, z = divmod(slab, LINE)
            core = pen % 2
            step = (2 * LINE - 1 - z if core else z) + by
            step %= 2 * LINE
            core, z = (0, step) if step < LINE else (1, 2 * LINE - 1 - step)
            pairs.append((slab * pens + pen, (line * LINE + z) * pens + pen // 2 * 2 + core))
    return lax.ppermute(x, ("slab", "pen"), pairs)


def between_lines(x, apart):
    slabs, pens = lax.axis_size("slab"), lax.axis_size("pen")
    pairs = []
    for low in range(slabs - apart):
        if low // LINE != (low + apart) // LINE:
            for pen in range(pens):
                here, there = low * pens + pen, (low + apart) * pens + pen
                pairs += [(here, there), (there, here)]
    return lax.ppermute(x, ("slab", "pen"), pairs)


def first_to_first(x):
    slabs, pens = lax.axis_size("slab"), lax.axis_size("pen")
    pairs = [
        (slab * pens + pen, (slab - LINE) * pens + pen)
        for slab in range(LINE, slabs, LINE)
        for pen in range(pens)
    ]
    return lax.ppermute(x, ("slab", "pen"), pairs)


def ends_onward(x):
    slabs, pens = lax.axis_size("slab"), lax.axis_size("pen")
    pairs = []
    for slab in range(0, slabs - LINE, LINE):
        for pen in range(pens):
            first, last, onward = (
                at * pens + pen for at in (slab, slab + LINE - 1, slab + LINE)
            )
            pairs += [(first, last), (last, onward)]
    return lax.ppermute(x, ("slab", "pen"), pairs)


def place():
    return lax.axis_index("pen") % 2 == 0, lax.axis_index("slab") % LINE


class Picked:
    def __init__(self, first, one, other, end, across):
        self.parts = (first, one, other, end, across)

    def __getitem__(self, index):
        first, one, other, end, across = self.parts
        value = jnp.where(first, one[index], other[index])
        return jnp.where(end, across[index], value)


def below_above(plus, minus, across):
    first, z = place()
    return (
        Picked(first, plus, minus, z == 0, across),
        Picked(first, minus, plus, z == LINE - 1, across),
    )


def rotated(x, axis, by):
    devices = lax.axis_size(axis)
    return lax.ppermute(x, axis, [(i, (i + by) % devices) for i in range(devices)])


def smooth_xy(v):
    rows, cols = v.shape
    col = lax.broadcasted_iota(jnp.int32, v.shape, 1)
    left = jnp.where(col == 0, 0.0, pltpu.roll(v, 1, 1))
    right = jnp.where(col == cols - 1, 0.0, pltpu.roll(v, cols - 1, 1))
    h = v + 0.5 * (left + right)
    return h + 0.5 * (pltpu.roll(h, 1, 0) + pltpu.roll(h, rows - 1, 0))


def to_wide(x):
    return jnp.concatenate([x[0:8], x[8:16]], axis=1)


def from_wide(x):
    return jnp.concatenate([x[:, 0:CCOLS], x[:, CCOLS:COLS]], axis=0)


Z1_RHS = 96
Z1_ACC = 160
Z1_CO = 224
Z1_ROWS = 232


def pack_z1(rhs, perm, acc, cperm, plus, minus, across, held, sems):
    first, z = place()
    upward = (first, jnp.logical_not(first), z == LINE - 1)
    copies = [pltpu.make_async_copy(cperm, held, sems.at[0])]
    for out, up in zip((plus, minus, across), upward):
        for base, ref, start, count in (
            (0, perm, jnp.where(up, ROWS, 0), 3),
            (Z1_RHS, rhs, jnp.where(up, 2 * ROWS, 0), 2),
            (Z1_ACC, acc, jnp.where(up, 2 * ROWS, 0), 2),
        ):
            copies.append(
                pltpu.make_async_copy(
                    ref.at[pl.ds(pl.multiple_of(start, ROWS), ROWS * count)],
                    out.at[pl.ds(base, ROWS * count)],
                    sems.at[len(copies)],
                )
            )
    for copy in copies:
        copy.start()
    for copy in copies:
        copy.wait()
    for out, up in zip((plus, minus, across), upward):
        out[Z1_CO : Z1_CO + 8, :] = to_wide(held[jnp.where(up, 1, 0)])


def hand_on(across, handed, out):
    @pl.when(place()[1] == 0)
    def _():
        out[...] = handed[...]


def fine_rows(own, lo, hi, base, depth, z, first, count):
    if z < 0:
        at = base + 32 * (z + depth)
        return lo[at + first : at + first + count, :]
    if z > 3:
        at = base + 32 * (z - 4)
        return hi[at + first : at + first + count, :]
    return own[z, first : first + count, :]


def coarse_plane(cperm, lo, hi, c):
    if c < 0:
        return from_wide(lo[Z1_CO : Z1_CO + 8, :])
    if c > 1:
        return from_wide(hi[Z1_CO : Z1_CO + 8, :])
    return cperm[c]


Y1_RHS = 30
Y1_ACC = 46
Y1_CO = 62
Y1_ROWS = 72


def pack_y1(rhs, perm, acc, cperm, plus, minus, across, up, down):
    lo, hi = below_above(plus, minus, across)
    for out, top in ((up, True), (down, False)):
        r3 = ROWS - 3 if top else 0
        r2 = ROWS - 2 if top else 0
        for k in range(10):
            out[3 * k : 3 * k + 3, :] = fine_rows(perm, lo, hi, 0, 3, k - 3, r3, 3)
        for k in range(8):
            at = Y1_RHS + 2 * k
            out[at : at + 2, :] = fine_rows(rhs, lo, hi, Z1_RHS, 2, k - 2, r2, 2)
            at = Y1_ACC + 2 * k
            out[at : at + 2, :] = fine_rows(acc, lo, hi, Z1_ACC, 2, k - 2, r2, 2)
        rc = CROWS - 1 if top else 0
        for k in range(4):
            plane = coarse_plane(cperm, lo, hi, k - 1)
            at = Y1_CO + k // 2
            lane = CCOLS * (k % 2)
            out[at : at + 1, lane : lane + CCOLS] = plane[rc : rc + 1, :]


def pre_kernel(
    masks, rhs, perm, acc, cperm, cacc, plus, minus, across, ylo, yhi,
    t_out, a_out, b_out, u_out, ct_out, ab_out, plus_out, minus_out, across_out,
    ts, rs, cs, xs, us, ds, fs,
):
    first, place_z = place()
    lo, hi = below_above(plus, minus, across)
    mlo = masks[0]
    mhi = masks[1]
    zeros = jnp.zeros((FR, COLS), jnp.float32)
    for k in range(10):
        z = k - 3
        ts[k] = zeros
        ts[k, 4:36, :] = jnp.sqrt(fine_rows(perm, lo, hi, 0, 3, z, 0, ROWS))
        ts[k, 1:4, :] = jnp.sqrt(ylo[3 * k : 3 * k + 3, :] * mlo)
        ts[k, 36:39, :] = jnp.sqrt(yhi[3 * k : 3 * k + 3, :] * mhi)
    for k in range(8):
        z = k - 2
        for ref, own, base, ybase in ((rs, rhs, Z1_RHS, Y1_RHS), (cs, acc, Z1_ACC, Y1_ACC)):
            ref[k] = zeros
            ref[k, 4:36, :] = fine_rows(own, lo, hi, base, 2, z, 0, ROWS)
            ref[k, 2:4, :] = ylo[ybase + 2 * k : ybase + 2 * k + 2, :] * mlo
            ref[k, 36:38, :] = yhi[ybase + 2 * k : ybase + 2 * k + 2, :] * mhi
    for k in range(10):
        xs[k] = smooth_xy(ts[k])
    for k in range(8):
        t = ts[k + 1]
        w = 2.0 * (xs[k + 1] + 0.5 * (xs[k] + xs[k + 2]) - t)
        d = t * w + cs[k]
        d = jnp.where(d > 0.0, d, 1.0)
        q = OMEGA * t / d
        if 2 <= k < 6:
            ds[k - 2] = d
        t_out[k] = t
        rs_k = rs[k]
        us[k] = q * rs_k
        cs[k] = q * t
    for k in range(8):
        xs[k] = smooth_xy(us[k])
    for k in range(6):
        a = us[k + 1]
        b = cs[k + 1]
        w = 2.0 * (xs[k + 1] + 0.5 * (xs[k] + xs[k + 2]) - a)
        a_out[k] = a
        b_out[k] = b
        u_out[k] = (1.0 + KEEP) * a + b * w
    for k in range(6):
        xs[k] = smooth_xy(u_out[k])
    sums = []
    for k in range(4):
        u = u_out[k + 1]
        t = ts[k + 3]
        w = 2.0 * (xs[k + 1] + 0.5 * (xs[k] + xs[k + 2]) - u)
        r = rs[k + 2] + t * w - ds[k] * (u / t)
        sums.append(r)
    pairs = []
    for k in range(2):
        both = sums[2 * k] + sums[2 * k + 1]
        halves = []
        for half in range(2):
            at = 2 * k + half
            fs[at] = both[:, CCOLS * half : CCOLS * half + CCOLS]
            halves.append(fs[at, pl.ds(4, CROWS, 2), :] + fs[at, pl.ds(5, CROWS, 2), :])
        pairs.append(jnp.concatenate(halves, axis=1))
    stacked = jnp.concatenate(pairs, axis=0)
    src = lax.broadcasted_iota(jnp.int32, (COLS, CCOLS), 0)
    dst = lax.broadcasted_iota(jnp.int32, (COLS, CCOLS), 1)
    fold = jnp.where(src // 2 == dst, 1.0, 0.0)
    res = jnp.dot(
        stacked, fold, precision=lax.Precision.HIGHEST, preferred_element_type=jnp.float32
    )
    for k in range(4):
        ct_out[k] = jnp.zeros((CR, CCOLS), jnp.float32)
        ct_out[k, 8:24, :] = jnp.sqrt(coarse_plane(cperm, lo, hi, k - 1))
        at = Y1_CO + k // 2
        lane = CCOLS * (k % 2)
        ct_out[k, 7:8, :] = jnp.sqrt(ylo[at : at + 1, lane : lane + CCOLS] * mlo)
        ct_out[k, 24:25, :] = jnp.sqrt(yhi[at : at + 1, lane : lane + CCOLS] * mhi)
    cx = [smooth_xy(ct_out[k]) for k in range(4)]
    for k in range(2):
        t = ct_out[k + 1]
        w = 2.0 * (cx[k + 1] + 0.5 * (cx[k] + cx[k + 2]) - t)
        t = t[8:24]
        d = t * w[8:24] + cacc[k]
        q = OMEGA * t / d
        a = q * res[CROWS * k : CROWS * k + CROWS]
        b = q * t
        for out in (ab_out, plus_out, minus_out, across_out):
            out[k] = a
            out[2 + k] = b
    for out, up in (
        (plus_out, first), (minus_out, jnp.logical_not(first)), (across_out, place_z == LINE - 1)
    ):
        plane = jnp.where(up, 3, 2)
        for k in range(4):
            row = 4 + 16 * (k // 2)
            lane = CCOLS * (k % 2)
            out[4 + k] = u_out[plane, row : row + 16, lane : lane + CCOLS]


def pack_far(ab, plus1, minus1, out):
    first, z = place()
    near_start = z < LINE // 2
    out[0:2] = ab[0:2]
    out[2] = ab[jnp.where(near_start, 2, 3)]
    out[3:7] = jnp.where(first == near_start, plus1[0:4], minus1[0:4])


Y2_B = 84
Y2_U = 156
Y2_ROWS = 200


def pack_y2(
    ab, u, plus1, minus1, across, plus2, minus2, plus3, minus3, far, up, down, dom, edge
):
    first, z = place()

    def below(plus, minus, k, places, other):
        return jnp.where(z < places, other, jnp.where(first, plus[k], minus[k]))

    def above(plus, minus, k, places, other):
        return jnp.where(z >= LINE - places, other, jnp.where(first, minus[k], plus[k]))

    for k in range(4):
        a = k < 2
        dom[6 + k if a else 17 + k] = ab[k]
        dom[4 + k if a else 15 + k] = below(plus1, minus1, k, 1, across[k])
        dom[8 + k if a else 19 + k] = above(plus1, minus1, k, 1, across[k])
        dom[2 + k if a else 13 + k] = below(plus2, minus2, k, 2, far[3 + k])
        dom[10 + k if a else 21 + k] = above(plus2, minus2, k, 2, far[3 + k])
        edge[k] = below(plus1, minus1, 4 + k, 1, across[4 + k])
        edge[4 + k] = above(plus1, minus1, 4 + k, 1, across[4 + k])
    for k in range(3):
        low = 3 if k == 2 else k
        dom[14 if k == 2 else k] = below(plus3, minus3, low, 3, far[k])
        dom[25 if k == 2 else 12 + k] = above(plus3, minus3, k, 3, far[k])
    for out, top_rows in ((up, True), (down, False)):
        row = CROWS - 6 if top_rows else 0
        for k in range(26):
            out[6 * k : 6 * k + 6, :] = dom[k, row : row + 6, :]
        for k in range(8):
            at = Y2_U + 4 * k
            for half in range(2):
                if 0 < k < 7:
                    row = 34 if top_rows else 4
                    rows = u[k - 1, row : row + 2, CCOLS * half : CCOLS * half + CCOLS]
                else:
                    piece = (0 if k == 0 else 4) + half
                    if top_rows:
                        rows = edge[piece + 2, 14:16, :]
                    else:
                        rows = edge[piece, 0:2, :]
                out[at + 2 * half : at + 2 * half + 2, :] = rows


def post_kernel(
    masks, t_in, a_in, b_in, u_in, ct, dom, edge, ylo, yhi,
    out, uf, cf, xs, ff,
):
    mlo = masks[0]
    mhi = masks[1]
    tile = jnp.zeros((8, CCOLS), jnp.float32)
    a = []
    b = [None]
    for k in range(26):
        ff[k, 0:8, :] = tile
        ff[k, 24:32, :] = tile
        ff[k, 2:8, :] = ylo[6 * k : 6 * k + 6, :] * mlo
        ff[k, 8:24, :] = dom[k]
        ff[k, 24:30, :] = yhi[6 * k : 6 * k + 6, :] * mhi
        (a if k < 14 else b).append(ff[k])
    link = [0.5] * 13
    for j in range(6):
        link[2 * j + 1] = 0.5 * masks[2 + j]
    u = list(a)
    for sweep in range(1, COARSE_SWEEPS):
        first, last = sweep, 13 - sweep
        smooth = {k: smooth_xy(u[k]) for k in range(first - 1, last + 2)}
        fresh = list(u)
        for k in range(first, last + 1):
            w = 2.0 * (
                smooth[k] + link[k - 1] * smooth[k - 1] + link[k] * smooth[k + 1] - u[k]
            )
            fresh[k] = KEEP * u[k] + a[k] + b[k] * w
        u = fresh
    corr = []
    for k in range(4):
        t = ct[k]
        inside = t > 0.0
        corr.append(jnp.where(inside, u[5 + k] / jnp.where(inside, t, 1.0), 0.0))
    stacked = jnp.concatenate(corr, axis=0)
    dst = lax.broadcasted_iota(jnp.int32, (CCOLS, COLS), 1)
    src = lax.broadcasted_iota(jnp.int32, (CCOLS, COLS), 0)
    spread = jnp.where(dst // 2 == src, 1.0, 0.0)
    wide = jnp.dot(
        stacked, spread, precision=lax.Precision.HIGHEST, preferred_element_type=jnp.float32
    )
    for k in range(4):
        for half in range(2):
            rows = wide[CR * k + 6 : CR * k + 26, CCOLS * half : CCOLS * half + CCOLS]
            cf[2 * k + half, pl.ds(0, 20, 2), :] = rows
            cf[2 * k + half, pl.ds(1, 20, 2), :] = rows
    zeros = jnp.zeros((FR, COLS), jnp.float32)
    for k in range(8):
        if 0 < k < 7:
            uf[k] = u_in[k - 1]
        else:
            uf[k] = zeros
            piece = 0 if k == 0 else 4
            for j in range(4):
                row = 4 + 16 * (j // 2)
                lane = CCOLS * (j % 2)
                uf[k, row : row + 16, lane : lane + CCOLS] = edge[piece + j]
        at = Y2_U + 4 * k
        for half in range(2):
            lane = CCOLS * half
            uf[k, 2:4, lane : lane + CCOLS] = ylo[at + 2 * half : at + 2 * half + 2, :] * mlo
            uf[k, 36:38, lane : lane + CCOLS] = yhi[at + 2 * half : at + 2 * half + 2, :] * mhi
        both = 2 * (k // 2)
        uf[k] = uf[k] + t_in[k] * jnp.concatenate([cf[both, 0:FR], cf[both + 1, 0:FR]], axis=1)
    for k in range(8):
        xs[k] = smooth_xy(uf[k])
    for k in range(6):
        v = uf[k + 1]
        w = 2.0 * (xs[k + 1] + 0.5 * (xs[k] + xs[k + 2]) - v)
        uf[k + 1] = KEEP * v + a_in[k] + b_in[k] * w
    for k in range(6):
        xs[k] = smooth_xy(uf[k + 1])
    for k in range(4):
        v = uf[k + 2]
        w = 2.0 * (xs[k + 1] + 0.5 * (xs[k] + xs[k + 2]) - v)
        new = KEEP * v + a_in[k + 1] + b_in[k + 1] * w
        uf[k + 2] = new / t_in[k + 2]
        out[k] = uf[k + 2, 4:36, :]


VM = pl.BlockSpec(memory_space=pltpu.VMEM)
SM = pl.BlockSpec(memory_space=pltpu.SMEM)
HBM = pl.BlockSpec(memory_space=pltpu.HBM)


def f32(*shape):
    return jax.ShapeDtypeStruct(shape, jnp.float32)


def call(kernel, specs, outs, scratch=()):
    return pl.pallas_call(
        kernel,
        in_specs=specs,
        out_specs=jax.tree.map(lambda _: VM, outs),
        out_shape=outs,
        scratch_shapes=[
            pltpu.VMEM(shape, jnp.float32) if isinstance(shape, tuple) else shape
            for shape in scratch
        ],
        compiler_params=pltpu.CompilerParams(vmem_limit_bytes=8 * 1024 * 1024),
    )


def pre_call(*operands):
    return call(
        pre_kernel,
        [SM] + [VM] * 10,
        (
            f32(8, FR, COLS), f32(6, FR, COLS), f32(6, FR, COLS), f32(6, FR, COLS),
            f32(4, CR, CCOLS), f32(4, CROWS, CCOLS),
            f32(8, CROWS, CCOLS), f32(8, CROWS, CCOLS), f32(8, CROWS, CCOLS),
        ),
        (
            (10, FR, COLS), (8, FR, COLS), (8, FR, COLS),
            (10, FR, COLS), (8, FR, COLS), (4, FR, COLS), (4, FR, CCOLS),
        ),
    )(*operands)


def post_call(*operands):
    return call(
        post_kernel,
        [SM] + [VM] * 9,
        f32(4, ROWS, COLS),
        ((8, FR, COLS), (8, FR + 8, CCOLS), (8, FR, COLS), (26, CR, CCOLS)),
    )(*operands)


def on_device(pressure_rhs, permeability, accumulation, coarse_perm, coarse_accum, run_lengths):
    message = f32(Z1_ROWS, COLS)
    plus, minus, across = call(
        pack_z1,
        [HBM] * 4,
        (message, message, message),
        (pltpu.VMEM((2, CROWS, CCOLS), jnp.float32), pltpu.SemaphoreType.DMA((10,))),
    )(
        *(
            pltpu.with_memory_space_constraint(x, pltpu.HBM)
            for x in (
                pressure_rhs.reshape(-1, COLS),
                permeability.reshape(-1, COLS),
                accumulation.reshape(-1, COLS),
                coarse_perm,
            )
        )
    )
    across = pl.pallas_call(
        hand_on,
        in_specs=[VM] * 2,
        out_specs=VM,
        out_shape=message,
        input_output_aliases={0: 0},
        compiler_params=pltpu.CompilerParams(vmem_limit_bytes=8 * 1024 * 1024),
    )(across, first_to_first(across))
    across = ends_onward(across)
    plus = along_lines(plus, 1)
    minus = along_lines(minus, -1)

    slab = lax.axis_index("slab")
    pen = lax.axis_index("pen")
    starts = jnp.cumsum(run_lengths) - run_lengths
    blocks = slab - 2 + jnp.arange(6, dtype=jnp.int32)
    begins = jnp.any(starts[None, :] == blocks[:, None], axis=1)
    masks = jnp.concatenate(
        [
            jnp.stack([pen > 0, pen < lax.axis_size("pen") - 1]).astype(jnp.float32),
            1.0 - begins.astype(jnp.float32),
        ]
    )

    rows = f32(Y1_ROWS, COLS)
    up, down = call(pack_y1, [VM] * 7, (rows, rows))(
        pressure_rhs, permeability, accumulation, coarse_perm, plus, minus, across
    )
    ylo = rotated(up, "pen", 1)
    yhi = rotated(down, "pen", -1)

    t, a, b, u, ct, ab, plus, minus, across = pre_call(
        masks, pressure_rhs, permeability, accumulation, coarse_perm, coarse_accum,
        plus, minus, across, ylo, yhi,
    )
    across = between_lines(across, 1)
    plus1 = along_lines(plus, 1)
    minus1 = along_lines(minus, -1)
    far = between_lines(
        call(pack_far, [VM] * 3, f32(7, CROWS, CCOLS))(ab, plus1, minus1), 3
    )
    plus2 = along_lines(plus1[0:4], 1)
    minus2 = along_lines(minus1[0:4], -1)
    plus3 = along_lines(plus2, 1)
    minus3 = along_lines(minus2, -1)

    rows = f32(Y2_ROWS, CCOLS)
    up, down, dom, edge = call(
        pack_y2, [VM] * 10, (rows, rows, f32(26, CROWS, CCOLS), f32(8, CROWS, CCOLS))
    )(ab, u, plus1, minus1, across, plus2, minus2, plus3, minus3, far)
    ylo = rotated(up, "pen", 1)
    yhi = rotated(down, "pen", -1)

    return post_call(masks, t, a, b, u, ct, dom, edge, ylo, yhi)


def solution(mesh):
    return jax.shard_map(
        on_device,
        mesh=mesh,
        in_specs=(
            P("slab", "pen", None),
            P("slab", "pen", None),
            P("slab", "pen", None),
            P("slab", "pen", None),
            P("slab", "pen", None),
            P(),
        ),
        out_specs=P("slab", "pen", None),
        check_vma=False,
    )
```

```python
import jax
import jax.numpy as jnp
from jax import lax
from jax.experimental import pallas as pl
from jax.experimental.pallas import tpu as pltpu
from jax.sharding import PartitionSpec as P

OMEGA = 0.7
KEEP = 1.0 - OMEGA
COARSE_SWEEPS = 6

FR = 40
ROWS = 32
COLS = 256
CR = 32
CROWS = 16
CCOLS = 128


LINE = 16


def along_lines(x, by):
    slabs, pens = lax.axis_size("slab"), lax.axis_size("pen")
    pairs = []
    for slab in range(slabs):
        for pen in range(pens):
            line, z = divmod(slab, LINE)
            core = pen % 2
            step = (2 * LINE - 1 - z if core else z) + by
            step %= 2 * LINE
            core, z = (0, step) if step < LINE else (1, 2 * LINE - 1 - step)
            pairs.append((slab * pens + pen, (line * LINE + z) * pens + pen // 2 * 2 + core))
    return lax.ppermute(x, ("slab", "pen"), pairs)


def between_lines(x, apart):
    slabs, pens = lax.axis_size("slab"), lax.axis_size("pen")
    pairs = []
    for low in range(slabs - apart):
        if low // LINE != (low + apart) // LINE:
            for pen in range(pens):
                here, there = low * pens + pen, (low + apart) * pens + pen
                pairs += [(here, there), (there, here)]
    return lax.ppermute(x, ("slab", "pen"), pairs)


def place():
    return lax.axis_index("pen") % 2 == 0, lax.axis_index("slab") % LINE


class Picked:
    def __init__(self, first, one, other, end, across):
        self.parts = (first, one, other, end, across)

    def __getitem__(self, index):
        first, one, other, end, across = self.parts
        value = jnp.where(first, one[index], other[index])
        return jnp.where(end, across[index], value)


def below_above(plus, minus, across):
    first, z = place()
    return (
        Picked(first, plus, minus, z == 0, across),
        Picked(first, minus, plus, z == LINE - 1, across),
    )


def rotated(x, axis, by):
    devices = lax.axis_size(axis)
    return lax.ppermute(x, axis, [(i, (i + by) % devices) for i in range(devices)])


def smooth_xy(v):
    rows, cols = v.shape
    col = lax.broadcasted_iota(jnp.int32, v.shape, 1)
    left = jnp.where(col == 0, 0.0, pltpu.roll(v, 1, 1))
    right = jnp.where(col == cols - 1, 0.0, pltpu.roll(v, cols - 1, 1))
    h = v + 0.5 * (left + right)
    return h + 0.5 * (pltpu.roll(h, 1, 0) + pltpu.roll(h, rows - 1, 0))


def to_wide(x):
    return jnp.concatenate([x[0:8], x[8:16]], axis=1)


def from_wide(x):
    return jnp.concatenate([x[:, 0:CCOLS], x[:, CCOLS:COLS]], axis=0)


Z1_RHS = 96
Z1_ACC = 160
Z1_CO = 224
Z1_ROWS = 232


def pack_z1(rhs, perm, acc, cperm, plus, minus, across, held, sems):
    first, z = place()
    upward = (first, jnp.logical_not(first), z == LINE - 1)
    copies = [pltpu.make_async_copy(cperm, held, sems.at[0])]
    for out, up in zip((plus, minus, across), upward):
        for base, ref, start, count in (
            (0, perm, jnp.where(up, ROWS, 0), 3),
            (Z1_RHS, rhs, jnp.where(up, 2 * ROWS, 0), 2),
            (Z1_ACC, acc, jnp.where(up, 2 * ROWS, 0), 2),
        ):
            copies.append(
                pltpu.make_async_copy(
                    ref.at[pl.ds(pl.multiple_of(start, ROWS), ROWS * count)],
                    out.at[pl.ds(base, ROWS * count)],
                    sems.at[len(copies)],
                )
            )
    for copy in copies:
        copy.start()
    for copy in copies:
        copy.wait()
    for out, up in zip((plus, minus, across), upward):
        out[Z1_CO : Z1_CO + 8, :] = to_wide(held[jnp.where(up, 1, 0)])


def fine_rows(own, lo, hi, base, depth, z, first, count):
    if z < 0:
        at = base + 32 * (z + depth)
        return lo[at + first : at + first + count, :]
    if z > 3:
        at = base + 32 * (z - 4)
        return hi[at + first : at + first + count, :]
    return own[z, first : first + count, :]


def coarse_plane(cperm, lo, hi, c):
    if c < 0:
        return from_wide(lo[Z1_CO : Z1_CO + 8, :])
    if c > 1:
        return from_wide(hi[Z1_CO : Z1_CO + 8, :])
    return cperm[c]


Y1_RHS = 30
Y1_ACC = 46
Y1_CO = 62
Y1_ROWS = 72


def pack_y1(rhs, perm, acc, cperm, plus, minus, across, up, down):
    lo, hi = below_above(plus, minus, across)
    for out, top in ((up, True), (down, False)):
        r3 = ROWS - 3 if top else 0
        r2 = ROWS - 2 if top else 0
        for k in range(10):
            out[3 * k : 3 * k + 3, :] = fine_rows(perm, lo, hi, 0, 3, k - 3, r3, 3)
        for k in range(8):
            at = Y1_RHS + 2 * k
            out[at : at + 2, :] = fine_rows(rhs, lo, hi, Z1_RHS, 2, k - 2, r2, 2)
            at = Y1_ACC + 2 * k
            out[at : at + 2, :] = fine_rows(acc, lo, hi, Z1_ACC, 2, k - 2, r2, 2)
        rc = CROWS - 1 if top else 0
        for k in range(4):
            plane = coarse_plane(cperm, lo, hi, k - 1)
            at = Y1_CO + k // 2
            lane = CCOLS * (k % 2)
            out[at : at + 1, lane : lane + CCOLS] = plane[rc : rc + 1, :]


def pre_kernel(
    masks, rhs, perm, acc, cperm, cacc, plus, minus, across, ylo, yhi,
    t_out, a_out, b_out, u_out, ct_out, ab_out, plus_out, minus_out, across_out,
    ts, rs, cs, xs, us, ds, fs,
):
    first, place_z = place()
    lo, hi = below_above(plus, minus, across)
    mlo = masks[0]
    mhi = masks[1]
    zeros = jnp.zeros((FR, COLS), jnp.float32)
    for k in range(10):
        z = k - 3
        ts[k] = zeros
        ts[k, 4:36, :] = jnp.sqrt(fine_rows(perm, lo, hi, 0, 3, z, 0, ROWS))
        ts[k, 1:4, :] = jnp.sqrt(ylo[3 * k : 3 * k + 3, :] * mlo)
        ts[k, 36:39, :] = jnp.sqrt(yhi[3 * k : 3 * k + 3, :] * mhi)
    for k in range(8):
        z = k - 2
        for ref, own, base, ybase in ((rs, rhs, Z1_RHS, Y1_RHS), (cs, acc, Z1_ACC, Y1_ACC)):
            ref[k] = zeros
            ref[k, 4:36, :] = fine_rows(own, lo, hi, base, 2, z, 0, ROWS)
            ref[k, 2:4, :] = ylo[ybase + 2 * k : ybase + 2 * k + 2, :] * mlo
            ref[k, 36:38, :] = yhi[ybase + 2 * k : ybase + 2 * k + 2, :] * mhi
    for k in range(10):
        xs[k] = smooth_xy(ts[k])
    for k in range(8):
        t = ts[k + 1]
        w = 2.0 * (xs[k + 1] + 0.5 * (xs[k] + xs[k + 2]) - t)
        d = t * w + cs[k]
        d = jnp.where(d > 0.0, d, 1.0)
        q = OMEGA * t / d
        if 2 <= k < 6:
            ds[k - 2] = d
        t_out[k] = t
        rs_k = rs[k]
        us[k] = q * rs_k
        cs[k] = q * t
    for k in range(8):
        xs[k] = smooth_xy(us[k])
    for k in range(6):
        a = us[k + 1]
        b = cs[k + 1]
        w = 2.0 * (xs[k + 1] + 0.5 * (xs[k] + xs[k + 2]) - a)
        a_out[k] = a
        b_out[k] = b
        u_out[k] = (1.0 + KEEP) * a + b * w
    for k in range(6):
        xs[k] = smooth_xy(u_out[k])
    sums = []
    for k in range(4):
        u = u_out[k + 1]
        t = ts[k + 3]
        w = 2.0 * (xs[k + 1] + 0.5 * (xs[k] + xs[k + 2]) - u)
        r = rs[k + 2] + t * w - ds[k] * (u / t)
        sums.append(r)
    pairs = []
    for k in range(2):
        both = sums[2 * k] + sums[2 * k + 1]
        halves = []
        for half in range(2):
            at = 2 * k + half
            fs[at] = both[:, CCOLS * half : CCOLS * half + CCOLS]
            halves.append(fs[at, pl.ds(4, CROWS, 2), :] + fs[at, pl.ds(5, CROWS, 2), :])
        pairs.append(jnp.concatenate(halves, axis=1))
    stacked = jnp.concatenate(pairs, axis=0)
    src = lax.broadcasted_iota(jnp.int32, (COLS, CCOLS), 0)
    dst = lax.broadcasted_iota(jnp.int32, (COLS, CCOLS), 1)
    fold = jnp.where(src // 2 == dst, 1.0, 0.0)
    res = jnp.dot(
        stacked, fold, precision=lax.Precision.HIGHEST, preferred_element_type=jnp.float32
    )
    for k in range(4):
        ct_out[k] = jnp.zeros((CR, CCOLS), jnp.float32)
        ct_out[k, 8:24, :] = jnp.sqrt(coarse_plane(cperm, lo, hi, k - 1))
        at = Y1_CO + k // 2
        lane = CCOLS * (k % 2)
        ct_out[k, 7:8, :] = jnp.sqrt(ylo[at : at + 1, lane : lane + CCOLS] * mlo)
        ct_out[k, 24:25, :] = jnp.sqrt(yhi[at : at + 1, lane : lane + CCOLS] * mhi)
    cx = [smooth_xy(ct_out[k]) for k in range(4)]
    for k in range(2):
        t = ct_out[k + 1]
        w = 2.0 * (cx[k + 1] + 0.5 * (cx[k] + cx[k + 2]) - t)
        t = t[8:24]
        d = t * w[8:24] + cacc[k]
        q = OMEGA * t / d
        a = q * res[CROWS * k : CROWS * k + CROWS]
        b = q * t
        for out in (ab_out, plus_out, minus_out, across_out):
            out[k] = a
            out[2 + k] = b
    for out, up in (
        (plus_out, first), (minus_out, jnp.logical_not(first)), (across_out, place_z == LINE - 1)
    ):
        plane = jnp.where(up, 3, 2)
        for k in range(4):
            row = 4 + 16 * (k // 2)
            lane = CCOLS * (k % 2)
            out[4 + k] = u_out[plane, row : row + 16, lane : lane + CCOLS]


def pack_far(ab, plus1, minus1, out):
    first, z = place()
    near_start = z < LINE // 2
    out[0:2] = ab[0:2]
    out[2] = ab[jnp.where(near_start, 2, 3)]
    out[3:7] = jnp.where(first == near_start, plus1[0:4], minus1[0:4])


Y2_B = 84
Y2_U = 156
Y2_ROWS = 200


def pack_y2(
    ab, u, plus1, minus1, across, plus2, minus2, plus3, minus3, far, up, down, dom, edge
):
    first, z = place()

    def below(plus, minus, k, places, other):
        return jnp.where(z < places, other, jnp.where(first, plus[k], minus[k]))

    def above(plus, minus, k, places, other):
        return jnp.where(z >= LINE - places, other, jnp.where(first, minus[k], plus[k]))

    for k in range(4):
        a = k < 2
        dom[6 + k if a else 17 + k] = ab[k]
        dom[4 + k if a else 15 + k] = below(plus1, minus1, k, 1, across[k])
        dom[8 + k if a else 19 + k] = above(plus1, minus1, k, 1, across[k])
        dom[2 + k if a else 13 + k] = below(plus2, minus2, k, 2, far[3 + k])
        dom[10 + k if a else 21 + k] = above(plus2, minus2, k, 2, far[3 + k])
        edge[k] = below(plus1, minus1, 4 + k, 1, across[4 + k])
        edge[4 + k] = above(plus1, minus1, 4 + k, 1, across[4 + k])
    for k in range(3):
        low = 3 if k == 2 else k
        dom[14 if k == 2 else k] = below(plus3, minus3, low, 3, far[k])
        dom[25 if k == 2 else 12 + k] = above(plus3, minus3, k, 3, far[k])
    for out, top_rows in ((up, True), (down, False)):
        row = CROWS - 6 if top_rows else 0
        for k in range(26):
            out[6 * k : 6 * k + 6, :] = dom[k, row : row + 6, :]
        for k in range(8):
            at = Y2_U + 4 * k
            for half in range(2):
                if 0 < k < 7:
                    row = 34 if top_rows else 4
                    rows = u[k - 1, row : row + 2, CCOLS * half : CCOLS * half + CCOLS]
                else:
                    piece = (0 if k == 0 else 4) + half
                    if top_rows:
                        rows = edge[piece + 2, 14:16, :]
                    else:
                        rows = edge[piece, 0:2, :]
                out[at + 2 * half : at + 2 * half + 2, :] = rows


def post_kernel(
    masks, t_in, a_in, b_in, u_in, ct, dom, edge, ylo, yhi,
    out, uf, cf, xs, ff,
):
    mlo = masks[0]
    mhi = masks[1]
    tile = jnp.zeros((8, CCOLS), jnp.float32)
    a = []
    b = [None]
    for k in range(26):
        ff[k, 0:8, :] = tile
        ff[k, 24:32, :] = tile
        ff[k, 2:8, :] = ylo[6 * k : 6 * k + 6, :] * mlo
        ff[k, 8:24, :] = dom[k]
        ff[k, 24:30, :] = yhi[6 * k : 6 * k + 6, :] * mhi
        (a if k < 14 else b).append(ff[k])
    link = [0.5] * 13
    for j in range(6):
        link[2 * j + 1] = 0.5 * masks[2 + j]
    u = list(a)
    for sweep in range(1, COARSE_SWEEPS):
        first, last = sweep, 13 - sweep
        smooth = {k: smooth_xy(u[k]) for k in range(first - 1, last + 2)}
        fresh = list(u)
        for k in range(first, last + 1):
            w = 2.0 * (
                smooth[k] + link[k - 1] * smooth[k - 1] + link[k] * smooth[k + 1] - u[k]
            )
            fresh[k] = KEEP * u[k] + a[k] + b[k] * w
        u = fresh
    corr = []
    for k in range(4):
        t = ct[k]
        inside = t > 0.0
        corr.append(jnp.where(inside, u[5 + k] / jnp.where(inside, t, 1.0), 0.0))
    stacked = jnp.concatenate(corr, axis=0)
    dst = lax.broadcasted_iota(jnp.int32, (CCOLS, COLS), 1)
    src = lax.broadcasted_iota(jnp.int32, (CCOLS, COLS), 0)
    spread = jnp.where(dst // 2 == src, 1.0, 0.0)
    wide = jnp.dot(
        stacked, spread, precision=lax.Precision.HIGHEST, preferred_element_type=jnp.float32
    )
    for k in range(4):
        for half in range(2):
            rows = wide[CR * k + 6 : CR * k + 26, CCOLS * half : CCOLS * half + CCOLS]
            cf[2 * k + half, pl.ds(0, 20, 2), :] = rows
            cf[2 * k + half, pl.ds(1, 20, 2), :] = rows
    zeros = jnp.zeros((FR, COLS), jnp.float32)
    for k in range(8):
        if 0 < k < 7:
            uf[k] = u_in[k - 1]
        else:
            uf[k] = zeros
            piece = 0 if k == 0 else 4
            for j in range(4):
                row = 4 + 16 * (j // 2)
                lane = CCOLS * (j % 2)
                uf[k, row : row + 16, lane : lane + CCOLS] = edge[piece + j]
        at = Y2_U + 4 * k
        for half in range(2):
            lane = CCOLS * half
            uf[k, 2:4, lane : lane + CCOLS] = ylo[at + 2 * half : at + 2 * half + 2, :] * mlo
            uf[k, 36:38, lane : lane + CCOLS] = yhi[at + 2 * half : at + 2 * half + 2, :] * mhi
        both = 2 * (k // 2)
        uf[k] = uf[k] + t_in[k] * jnp.concatenate([cf[both, 0:FR], cf[both + 1, 0:FR]], axis=1)
    for k in range(8):
        xs[k] = smooth_xy(uf[k])
    for k in range(6):
        v = uf[k + 1]
        w = 2.0 * (xs[k + 1] + 0.5 * (xs[k] + xs[k + 2]) - v)
        uf[k + 1] = KEEP * v + a_in[k] + b_in[k] * w
    for k in range(6):
        xs[k] = smooth_xy(uf[k + 1])
    for k in range(4):
        v = uf[k + 2]
        w = 2.0 * (xs[k + 1] + 0.5 * (xs[k] + xs[k + 2]) - v)
        new = KEEP * v + a_in[k + 1] + b_in[k + 1] * w
        uf[k + 2] = new / t_in[k + 2]
        out[k] = uf[k + 2, 4:36, :]


VM = pl.BlockSpec(memory_space=pltpu.VMEM)
SM = pl.BlockSpec(memory_space=pltpu.SMEM)
HBM = pl.BlockSpec(memory_space=pltpu.HBM)


def f32(*shape):
    return jax.ShapeDtypeStruct(shape, jnp.float32)


def call(kernel, specs, outs, scratch=()):
    return pl.pallas_call(
        kernel,
        in_specs=specs,
        out_specs=jax.tree.map(lambda _: VM, outs),
        out_shape=outs,
        scratch_shapes=[
            pltpu.VMEM(shape, jnp.float32) if isinstance(shape, tuple) else shape
            for shape in scratch
        ],
        compiler_params=pltpu.CompilerParams(vmem_limit_bytes=8 * 1024 * 1024),
    )


def pre_call(*operands):
    return call(
        pre_kernel,
        [SM] + [VM] * 10,
        (
            f32(8, FR, COLS), f32(6, FR, COLS), f32(6, FR, COLS), f32(6, FR, COLS),
            f32(4, CR, CCOLS), f32(4, CROWS, CCOLS),
            f32(8, CROWS, CCOLS), f32(8, CROWS, CCOLS), f32(8, CROWS, CCOLS),
        ),
        (
            (10, FR, COLS), (8, FR, COLS), (8, FR, COLS),
            (10, FR, COLS), (8, FR, COLS), (4, FR, COLS), (4, FR, CCOLS),
        ),
    )(*operands)


def post_call(*operands):
    return call(
        post_kernel,
        [SM] + [VM] * 9,
        f32(4, ROWS, COLS),
        ((8, FR, COLS), (8, FR + 8, CCOLS), (8, FR, COLS), (26, CR, CCOLS)),
    )(*operands)


def on_device(pressure_rhs, permeability, accumulation, coarse_perm, coarse_accum, run_lengths):
    message = f32(Z1_ROWS, COLS)
    plus, minus, across = call(
        pack_z1,
        [HBM] * 4,
        (message, message, message),
        (pltpu.VMEM((2, CROWS, CCOLS), jnp.float32), pltpu.SemaphoreType.DMA((10,))),
    )(
        *(
            pltpu.with_memory_space_constraint(x, pltpu.HBM)
            for x in (
                pressure_rhs.reshape(-1, COLS),
                permeability.reshape(-1, COLS),
                accumulation.reshape(-1, COLS),
                coarse_perm,
            )
        )
    )
    across = between_lines(across, 1)
    plus = along_lines(plus, 1)
    minus = along_lines(minus, -1)

    slab = lax.axis_index("slab")
    pen = lax.axis_index("pen")
    starts = jnp.cumsum(run_lengths) - run_lengths
    blocks = slab - 2 + jnp.arange(6, dtype=jnp.int32)
    begins = jnp.any(starts[None, :] == blocks[:, None], axis=1)
    masks = jnp.concatenate(
        [
            jnp.stack([pen > 0, pen < lax.axis_size("pen") - 1]).astype(jnp.float32),
            1.0 - begins.astype(jnp.float32),
        ]
    )

    rows = f32(Y1_ROWS, COLS)
    up, down = call(pack_y1, [VM] * 7, (rows, rows))(
        pressure_rhs, permeability, accumulation, coarse_perm, plus, minus, across
    )
    ylo = rotated(up, "pen", 1)
    yhi = rotated(down, "pen", -1)

    t, a, b, u, ct, ab, plus, minus, across = pre_call(
        masks, pressure_rhs, permeability, accumulation, coarse_perm, coarse_accum,
        plus, minus, across, ylo, yhi,
    )
    across = between_lines(across, 1)
    plus1 = along_lines(plus, 1)
    minus1 = along_lines(minus, -1)
    far = between_lines(
        call(pack_far, [VM] * 3, f32(7, CROWS, CCOLS))(ab, plus1, minus1), 3
    )
    plus2 = along_lines(plus1[0:4], 1)
    minus2 = along_lines(minus1[0:4], -1)
    plus3 = along_lines(plus2, 1)
    minus3 = along_lines(minus2, -1)

    rows = f32(Y2_ROWS, CCOLS)
    up, down, dom, edge = call(
        pack_y2, [VM] * 10, (rows, rows, f32(26, CROWS, CCOLS), f32(8, CROWS, CCOLS))
    )(ab, u, plus1, minus1, across, plus2, minus2, plus3, minus3, far)
    ylo = rotated(up, "pen", 1)
    yhi = rotated(down, "pen", -1)

    return post_call(masks, t, a, b, u, ct, dom, edge, ylo, yhi)


def solution(mesh):
    return jax.shard_map(
        on_device,
        mesh=mesh,
        in_specs=(
            P("slab", "pen", None),
            P("slab", "pen", None),
            P("slab", "pen", None),
            P("slab", "pen", None),
            P("slab", "pen", None),
            P(),
        ),
        out_specs=P("slab", "pen", None),
        check_vma=False,
    )
```

```python
import jax
import jax.numpy as jnp
from jax import lax
from jax.experimental import pallas as pl
from jax.experimental.pallas import tpu as pltpu
from jax.sharding import PartitionSpec as P

OMEGA = 0.7
KEEP = 1.0 - OMEGA
COARSE_SWEEPS = 6

FR = 40
ROWS = 32
COLS = 256
CR = 32
CROWS = 16
CCOLS = 128


LINE = 16


def along_lines(x, by):
    slabs, pens = lax.axis_size("slab"), lax.axis_size("pen")
    pairs = []
    for slab in range(slabs):
        for pen in range(pens):
            line, z = divmod(slab, LINE)
            core = pen % 2
            step = (2 * LINE - 1 - z if core else z) + by
            step %= 2 * LINE
            core, z = (0, step) if step < LINE else (1, 2 * LINE - 1 - step)
            pairs.append((slab * pens + pen, (line * LINE + z) * pens + pen // 2 * 2 + core))
    return lax.ppermute(x, ("slab", "pen"), pairs)


def between_lines(x, apart):
    slabs, pens = lax.axis_size("slab"), lax.axis_size("pen")
    pairs = []
    for low in range(slabs - apart):
        if low // LINE != (low + apart) // LINE:
            for pen in range(pens):
                here, there = low * pens + pen, (low + apart) * pens + pen
                pairs += [(here, there), (there, here)]
    return lax.ppermute(x, ("slab", "pen"), pairs)


def place():
    return lax.axis_index("pen") % 2 == 0, lax.axis_index("slab") % LINE


class Picked:
    def __init__(self, first, one, other, end, across):
        self.parts = (first, one, other, end, across)

    def __getitem__(self, index):
        first, one, other, end, across = self.parts
        value = jnp.where(first, one[index], other[index])
        return jnp.where(end, across[index], value)


def below_above(plus, minus, across):
    first, z = place()
    return (
        Picked(first, plus, minus, z == 0, across),
        Picked(first, minus, plus, z == LINE - 1, across),
    )


def rotated(x, axis, by):
    devices = lax.axis_size(axis)
    return lax.ppermute(x, axis, [(i, (i + by) % devices) for i in range(devices)])


def smooth_xy(v):
    rows, cols = v.shape
    col = lax.broadcasted_iota(jnp.int32, v.shape, 1)
    left = jnp.where(col == 0, 0.0, pltpu.roll(v, 1, 1))
    right = jnp.where(col == cols - 1, 0.0, pltpu.roll(v, cols - 1, 1))
    h = v + 0.5 * (left + right)
    return h + 0.5 * (pltpu.roll(h, 1, 0) + pltpu.roll(h, rows - 1, 0))


def to_wide(x):
    return jnp.concatenate([x[0:8], x[8:16]], axis=1)


def from_wide(x):
    return jnp.concatenate([x[:, 0:CCOLS], x[:, CCOLS:COLS]], axis=0)


Z1_RHS = 96
Z1_ACC = 160
Z1_CO = 224
Z1_ROWS = 232


def pack_z1(rhs, perm, acc, cperm, plus, minus, across, held, sems):
    first, z = place()
    upward = (first, jnp.logical_not(first), z == LINE - 1)
    copies = [pltpu.make_async_copy(cperm, held, sems.at[0])]
    for out, up in zip((plus, minus, across), upward):
        for base, ref, start, count in (
            (0, perm, jnp.where(up, ROWS, 0), 3),
            (Z1_RHS, rhs, jnp.where(up, 2 * ROWS, 0), 2),
            (Z1_ACC, acc, jnp.where(up, 2 * ROWS, 0), 2),
        ):
            copies.append(
                pltpu.make_async_copy(
                    ref.at[pl.ds(pl.multiple_of(start, ROWS), ROWS * count)],
                    out.at[pl.ds(base, ROWS * count)],
                    sems.at[len(copies)],
                )
            )
    for copy in copies:
        copy.start()
    for copy in copies:
        copy.wait()
    for out, up in zip((plus, minus, across), upward):
        out[Z1_CO : Z1_CO + 8, :] = to_wide(held[jnp.where(up, 1, 0)])


def fine_rows(own, lo, hi, base, depth, z, first, count):
    if z < 0:
        at = base + 32 * (z + depth)
        return lo[at + first : at + first + count, :]
    if z > 3:
        at = base + 32 * (z - 4)
        return hi[at + first : at + first + count, :]
    return own[z, first : first + count, :]


def coarse_plane(cperm, lo, hi, c):
    if c < 0:
        return from_wide(lo[Z1_CO : Z1_CO + 8, :])
    if c > 1:
        return from_wide(hi[Z1_CO : Z1_CO + 8, :])
    return cperm[c]


Y1_RHS = 30
Y1_ACC = 46
Y1_CO = 62
Y1_ROWS = 72


def pack_y1(rhs, perm, acc, cperm, plus, minus, across, up, down):
    lo, hi = below_above(plus, minus, across)
    for out, top in ((up, True), (down, False)):
        r3 = ROWS - 3 if top else 0
        r2 = ROWS - 2 if top else 0
        for k in range(10):
            out[3 * k : 3 * k + 3, :] = fine_rows(perm, lo, hi, 0, 3, k - 3, r3, 3)
        for k in range(8):
            at = Y1_RHS + 2 * k
            out[at : at + 2, :] = fine_rows(rhs, lo, hi, Z1_RHS, 2, k - 2, r2, 2)
            at = Y1_ACC + 2 * k
            out[at : at + 2, :] = fine_rows(acc, lo, hi, Z1_ACC, 2, k - 2, r2, 2)
        rc = CROWS - 1 if top else 0
        for k in range(4):
            plane = coarse_plane(cperm, lo, hi, k - 1)
            at = Y1_CO + k // 2
            lane = CCOLS * (k % 2)
            out[at : at + 1, lane : lane + CCOLS] = plane[rc : rc + 1, :]


def pre_kernel(
    masks, rhs, perm, acc, cperm, cacc, plus, minus, across, ylo, yhi,
    t_out, a_out, b_out, u_out, ct_out, ab_out, plus_out, minus_out, across_out,
    ts, rs, cs, xs, us, ds, fs,
):
    first, place_z = place()
    lo, hi = below_above(plus, minus, across)
    mlo = masks[0]
    mhi = masks[1]
    zeros = jnp.zeros((FR, COLS), jnp.float32)
    for k in range(10):
        z = k - 3
        ts[k] = zeros
        ts[k, 4:36, :] = jnp.sqrt(fine_rows(perm, lo, hi, 0, 3, z, 0, ROWS))
        ts[k, 1:4, :] = jnp.sqrt(ylo[3 * k : 3 * k + 3, :] * mlo)
        ts[k, 36:39, :] = jnp.sqrt(yhi[3 * k : 3 * k + 3, :] * mhi)
    for k in range(8):
        z = k - 2
        for ref, own, base, ybase in ((rs, rhs, Z1_RHS, Y1_RHS), (cs, acc, Z1_ACC, Y1_ACC)):
            ref[k] = zeros
            ref[k, 4:36, :] = fine_rows(own, lo, hi, base, 2, z, 0, ROWS)
            ref[k, 2:4, :] = ylo[ybase + 2 * k : ybase + 2 * k + 2, :] * mlo
            ref[k, 36:38, :] = yhi[ybase + 2 * k : ybase + 2 * k + 2, :] * mhi
    for k in range(10):
        xs[k] = smooth_xy(ts[k])
    for k in range(8):
        t = ts[k + 1]
        w = 2.0 * (xs[k + 1] + 0.5 * (xs[k] + xs[k + 2]) - t)
        d = t * w + cs[k]
        d = jnp.where(d > 0.0, d, 1.0)
        q = OMEGA * t / d
        if 2 <= k < 6:
            ds[k - 2] = d
        t_out[k] = t
        rs_k = rs[k]
        us[k] = q * rs_k
        cs[k] = q * t
    for k in range(8):
        xs[k] = smooth_xy(us[k])
    for k in range(6):
        a = us[k + 1]
        b = cs[k + 1]
        w = 2.0 * (xs[k + 1] + 0.5 * (xs[k] + xs[k + 2]) - a)
        a_out[k] = a
        b_out[k] = b
        u_out[k] = (1.0 + KEEP) * a + b * w
    for k in range(6):
        xs[k] = smooth_xy(u_out[k])
    sums = []
    for k in range(4):
        u = u_out[k + 1]
        t = ts[k + 3]
        w = 2.0 * (xs[k + 1] + 0.5 * (xs[k] + xs[k + 2]) - u)
        r = rs[k + 2] + t * w - ds[k] * (u / t)
        sums.append(r)
    pairs = []
    for k in range(2):
        both = sums[2 * k] + sums[2 * k + 1]
        halves = []
        for half in range(2):
            at = 2 * k + half
            fs[at] = both[:, CCOLS * half : CCOLS * half + CCOLS]
            halves.append(fs[at, pl.ds(4, CROWS, 2), :] + fs[at, pl.ds(5, CROWS, 2), :])
        pairs.append(jnp.concatenate(halves, axis=1))
    stacked = jnp.concatenate(pairs, axis=0)
    src = lax.broadcasted_iota(jnp.int32, (COLS, CCOLS), 0)
    dst = lax.broadcasted_iota(jnp.int32, (COLS, CCOLS), 1)
    fold = jnp.where(src // 2 == dst, 1.0, 0.0)
    res = jnp.dot(
        stacked, fold, precision=lax.Precision.HIGHEST, preferred_element_type=jnp.float32
    )
    for k in range(4):
        ct_out[k] = jnp.zeros((CR, CCOLS), jnp.float32)
        ct_out[k, 8:24, :] = jnp.sqrt(coarse_plane(cperm, lo, hi, k - 1))
        at = Y1_CO + k // 2
        lane = CCOLS * (k % 2)
        ct_out[k, 7:8, :] = jnp.sqrt(ylo[at : at + 1, lane : lane + CCOLS] * mlo)
        ct_out[k, 24:25, :] = jnp.sqrt(yhi[at : at + 1, lane : lane + CCOLS] * mhi)
    cx = [smooth_xy(ct_out[k]) for k in range(4)]
    for k in range(2):
        t = ct_out[k + 1]
        w = 2.0 * (cx[k + 1] + 0.5 * (cx[k] + cx[k + 2]) - t)
        t = t[8:24]
        d = t * w[8:24] + cacc[k]
        q = OMEGA * t / d
        a = q * res[CROWS * k : CROWS * k + CROWS]
        b = q * t
        for out in (ab_out, across_out):
            out[k] = a
            out[2 + k] = b
    for out, up, at in (
        (plus_out, first, 0),
        (minus_out, jnp.logical_not(first), 0),
        (across_out, place_z == LINE - 1, 4),
    ):
        plane = jnp.where(up, 3, 2)
        for k in range(4):
            row = 4 + 16 * (k // 2)
            lane = CCOLS * (k % 2)
            out[at + k] = u_out[plane, row : row + 16, lane : lane + CCOLS]


def pass_on(plus2, minus2, across, plus_out, minus_out):
    del across
    plus_out[...] = plus2[0:4]
    minus_out[...] = minus2[0:4]


def pack_far(ab, plus1, minus1, out):
    first, z = place()
    near_start = z < LINE // 2
    out[0:2] = ab[0:2]
    out[2] = ab[jnp.where(near_start, 2, 3)]
    out[3:7] = jnp.where(first == near_start, plus1[0:4], minus1[0:4])


Y2_B = 84
Y2_U = 156
Y2_ROWS = 200


def pack_y2(
    ab, u, plus1, minus1, across, plus2, minus2, plus3, minus3, far, up, down, dom, edge
):
    first, z = place()

    def below(plus, minus, k, places, other):
        return jnp.where(z < places, other, jnp.where(first, plus[k], minus[k]))

    def above(plus, minus, k, places, other):
        return jnp.where(z >= LINE - places, other, jnp.where(first, minus[k], plus[k]))

    for k in range(4):
        a = k < 2
        dom[6 + k if a else 17 + k] = ab[k]
        dom[4 + k if a else 15 + k] = below(plus1, minus1, k, 1, across[k])
        dom[8 + k if a else 19 + k] = above(plus1, minus1, k, 1, across[k])
        dom[2 + k if a else 13 + k] = below(plus2, minus2, k, 2, far[3 + k])
        dom[10 + k if a else 21 + k] = above(plus2, minus2, k, 2, far[3 + k])
        edge[k] = below(plus2, minus2, 4 + k, 1, across[4 + k])
        edge[4 + k] = above(plus2, minus2, 4 + k, 1, across[4 + k])
    for k in range(3):
        low = 3 if k == 2 else k
        dom[14 if k == 2 else k] = below(plus3, minus3, low, 3, far[k])
        dom[25 if k == 2 else 12 + k] = above(plus3, minus3, k, 3, far[k])
    for out, top_rows in ((up, True), (down, False)):
        row = CROWS - 6 if top_rows else 0
        for k in range(26):
            out[6 * k : 6 * k + 6, :] = dom[k, row : row + 6, :]
        for k in range(8):
            at = Y2_U + 4 * k
            for half in range(2):
                if 0 < k < 7:
                    row = 34 if top_rows else 4
                    rows = u[k - 1, row : row + 2, CCOLS * half : CCOLS * half + CCOLS]
                else:
                    piece = (0 if k == 0 else 4) + half
                    if top_rows:
                        rows = edge[piece + 2, 14:16, :]
                    else:
                        rows = edge[piece, 0:2, :]
                out[at + 2 * half : at + 2 * half + 2, :] = rows


def post_kernel(
    masks, t_in, a_in, b_in, u_in, ct, dom, edge, ylo, yhi,
    out, uf, cf, xs, ff,
):
    mlo = masks[0]
    mhi = masks[1]
    tile = jnp.zeros((8, CCOLS), jnp.float32)
    a = []
    b = [None]
    for k in range(26):
        ff[k, 0:8, :] = tile
        ff[k, 24:32, :] = tile
        ff[k, 2:8, :] = ylo[6 * k : 6 * k + 6, :] * mlo
        ff[k, 8:24, :] = dom[k]
        ff[k, 24:30, :] = yhi[6 * k : 6 * k + 6, :] * mhi
        (a if k < 14 else b).append(ff[k])
    link = [0.5] * 13
    for j in range(6):
        link[2 * j + 1] = 0.5 * masks[2 + j]
    u = list(a)
    for sweep in range(1, COARSE_SWEEPS):
        first, last = sweep, 13 - sweep
        smooth = {k: smooth_xy(u[k]) for k in range(first - 1, last + 2)}
        fresh = list(u)
        for k in range(first, last + 1):
            w = 2.0 * (
                smooth[k] + link[k - 1] * smooth[k - 1] + link[k] * smooth[k + 1] - u[k]
            )
            fresh[k] = KEEP * u[k] + a[k] + b[k] * w
        u = fresh
    corr = []
    for k in range(4):
        t = ct[k]
        inside = t > 0.0
        corr.append(jnp.where(inside, u[5 + k] / jnp.where(inside, t, 1.0), 0.0))
    stacked = jnp.concatenate(corr, axis=0)
    dst = lax.broadcasted_iota(jnp.int32, (CCOLS, COLS), 1)
    src = lax.broadcasted_iota(jnp.int32, (CCOLS, COLS), 0)
    spread = jnp.where(dst // 2 == src, 1.0, 0.0)
    wide = jnp.dot(
        stacked, spread, precision=lax.Precision.HIGHEST, preferred_element_type=jnp.float32
    )
    for k in range(4):
        for half in range(2):
            rows = wide[CR * k + 6 : CR * k + 26, CCOLS * half : CCOLS * half + CCOLS]
            cf[2 * k + half, pl.ds(0, 20, 2), :] = rows
            cf[2 * k + half, pl.ds(1, 20, 2), :] = rows
    zeros = jnp.zeros((FR, COLS), jnp.float32)
    for k in range(8):
        if 0 < k < 7:
            uf[k] = u_in[k - 1]
        else:
            uf[k] = zeros
            piece = 0 if k == 0 else 4
            for j in range(4):
                row = 4 + 16 * (j // 2)
                lane = CCOLS * (j % 2)
                uf[k, row : row + 16, lane : lane + CCOLS] = edge[piece + j]
        at = Y2_U + 4 * k
        for half in range(2):
            lane = CCOLS * half
            uf[k, 2:4, lane : lane + CCOLS] = ylo[at + 2 * half : at + 2 * half + 2, :] * mlo
            uf[k, 36:38, lane : lane + CCOLS] = yhi[at + 2 * half : at + 2 * half + 2, :] * mhi
        both = 2 * (k // 2)
        uf[k] = uf[k] + t_in[k] * jnp.concatenate([cf[both, 0:FR], cf[both + 1, 0:FR]], axis=1)
    for k in range(8):
        xs[k] = smooth_xy(uf[k])
    for k in range(6):
        v = uf[k + 1]
        w = 2.0 * (xs[k + 1] + 0.5 * (xs[k] + xs[k + 2]) - v)
        uf[k + 1] = KEEP * v + a_in[k] + b_in[k] * w
    for k in range(6):
        xs[k] = smooth_xy(uf[k + 1])
    for k in range(4):
        v = uf[k + 2]
        w = 2.0 * (xs[k + 1] + 0.5 * (xs[k] + xs[k + 2]) - v)
        new = KEEP * v + a_in[k + 1] + b_in[k + 1] * w
        uf[k + 2] = new / t_in[k + 2]
        out[k] = uf[k + 2, 4:36, :]


VM = pl.BlockSpec(memory_space=pltpu.VMEM)
SM = pl.BlockSpec(memory_space=pltpu.SMEM)
HBM = pl.BlockSpec(memory_space=pltpu.HBM)


def f32(*shape):
    return jax.ShapeDtypeStruct(shape, jnp.float32)


def call(kernel, specs, outs, scratch=()):
    return pl.pallas_call(
        kernel,
        in_specs=specs,
        out_specs=jax.tree.map(lambda _: VM, outs),
        out_shape=outs,
        scratch_shapes=[
            pltpu.VMEM(shape, jnp.float32) if isinstance(shape, tuple) else shape
            for shape in scratch
        ],
        compiler_params=pltpu.CompilerParams(vmem_limit_bytes=8 * 1024 * 1024),
    )


def pre_call(*operands):
    return call(
        pre_kernel,
        [SM] + [VM] * 10,
        (
            f32(8, FR, COLS), f32(6, FR, COLS), f32(6, FR, COLS), f32(6, FR, COLS),
            f32(4, CR, CCOLS), f32(4, CROWS, CCOLS),
            f32(4, CROWS, CCOLS), f32(4, CROWS, CCOLS), f32(8, CROWS, CCOLS),
        ),
        (
            (10, FR, COLS), (8, FR, COLS), (8, FR, COLS),
            (10, FR, COLS), (8, FR, COLS), (4, FR, COLS), (4, FR, CCOLS),
        ),
    )(*operands)


def post_call(*operands):
    return call(
        post_kernel,
        [SM] + [VM] * 9,
        f32(4, ROWS, COLS),
        ((8, FR, COLS), (8, FR + 8, CCOLS), (8, FR, COLS), (26, CR, CCOLS)),
    )(*operands)


def on_device(pressure_rhs, permeability, accumulation, coarse_perm, coarse_accum, run_lengths):
    message = f32(Z1_ROWS, COLS)
    plus, minus, across = call(
        pack_z1,
        [HBM] * 4,
        (message, message, message),
        (pltpu.VMEM((2, CROWS, CCOLS), jnp.float32), pltpu.SemaphoreType.DMA((10,))),
    )(
        *(
            pltpu.with_memory_space_constraint(x, pltpu.HBM)
            for x in (
                pressure_rhs.reshape(-1, COLS),
                permeability.reshape(-1, COLS),
                accumulation.reshape(-1, COLS),
                coarse_perm,
            )
        )
    )
    across = between_lines(across, 1)
    plus = along_lines(plus, 1)
    minus = along_lines(minus, -1)

    slab = lax.axis_index("slab")
    pen = lax.axis_index("pen")
    starts = jnp.cumsum(run_lengths) - run_lengths
    blocks = slab - 2 + jnp.arange(6, dtype=jnp.int32)
    begins = jnp.any(starts[None, :] == blocks[:, None], axis=1)
    masks = jnp.concatenate(
        [
            jnp.stack([pen > 0, pen < lax.axis_size("pen") - 1]).astype(jnp.float32),
            1.0 - begins.astype(jnp.float32),
        ]
    )

    rows = f32(Y1_ROWS, COLS)
    up, down = call(pack_y1, [VM] * 7, (rows, rows))(
        pressure_rhs, permeability, accumulation, coarse_perm, plus, minus, across
    )
    ylo = rotated(up, "pen", 1)
    yhi = rotated(down, "pen", -1)

    t, a, b, u, ct, ab, plus, minus, across = pre_call(
        masks, pressure_rhs, permeability, accumulation, coarse_perm, coarse_accum,
        plus, minus, across, ylo, yhi,
    )
    across = between_lines(across, 1)
    plus1 = along_lines(ab, 1)
    minus1 = along_lines(ab, -1)
    far = between_lines(
        call(pack_far, [VM] * 3, f32(7, CROWS, CCOLS))(ab, plus1, minus1), 3
    )
    plus2 = along_lines(jnp.concatenate([plus1, plus], axis=0), 1)
    minus2 = along_lines(jnp.concatenate([minus1, minus], axis=0), -1)
    block = f32(4, CROWS, CCOLS)
    plus, minus = call(pass_on, [VM] * 3, (block, block))(plus2, minus2, across)
    plus3 = along_lines(plus, 1)
    minus3 = along_lines(minus, -1)

    rows = f32(Y2_ROWS, CCOLS)
    up, down, dom, edge = call(
        pack_y2, [VM] * 10, (rows, rows, f32(26, CROWS, CCOLS), f32(8, CROWS, CCOLS))
    )(ab, u, plus1, minus1, across, plus2, minus2, plus3, minus3, far)
    ylo = rotated(up, "pen", 1)
    yhi = rotated(down, "pen", -1)

    return post_call(masks, t, a, b, u, ct, dom, edge, ylo, yhi)


def solution(mesh):
    return jax.shard_map(
        on_device,
        mesh=mesh,
        in_specs=(
            P("slab", "pen", None),
            P("slab", "pen", None),
            P("slab", "pen", None),
            P("slab", "pen", None),
            P("slab", "pen", None),
            P(),
        ),
        out_specs=P("slab", "pen", None),
        check_vma=False,
    )
```

```python
import jax
import jax.numpy as jnp
from jax import lax
from jax.experimental import pallas as pl
from jax.experimental.pallas import tpu as pltpu
from jax.sharding import PartitionSpec as P

OMEGA = 0.7
KEEP = 1.0 - OMEGA
COARSE_SWEEPS = 6

FR = 40
ROWS = 32
COLS = 256
CR = 32
CROWS = 16
CCOLS = 128


LINE = 16


def along_lines(x, by):
    slabs, pens = lax.axis_size("slab"), lax.axis_size("pen")
    pairs = []
    for slab in range(slabs):
        for pen in range(pens):
            line, z = divmod(slab, LINE)
            core = pen % 2
            step = (2 * LINE - 1 - z if core else z) + by
            step %= 2 * LINE
            core, z = (0, step) if step < LINE else (1, 2 * LINE - 1 - step)
            pairs.append((slab * pens + pen, (line * LINE + z) * pens + pen // 2 * 2 + core))
    return lax.ppermute(x, ("slab", "pen"), pairs)


def between_lines(x, apart):
    slabs, pens = lax.axis_size("slab"), lax.axis_size("pen")
    pairs = []
    for low in range(slabs - apart):
        if low // LINE != (low + apart) // LINE:
            for pen in range(pens):
                here, there = low * pens + pen, (low + apart) * pens + pen
                pairs += [(here, there), (there, here)]
    return lax.ppermute(x, ("slab", "pen"), pairs)


def place():
    return lax.axis_index("pen") % 2 == 0, lax.axis_index("slab") % LINE


class Picked:
    def __init__(self, first, one, other, end, across):
        self.parts = (first, one, other, end, across)

    def __getitem__(self, index):
        first, one, other, end, across = self.parts
        value = jnp.where(first, one[index], other[index])
        return jnp.where(end, across[index], value)


def below_above(plus, minus, across):
    first, z = place()
    return (
        Picked(first, plus, minus, z == 0, across),
        Picked(first, minus, plus, z == LINE - 1, across),
    )


def rotated(x, axis, by):
    devices = lax.axis_size(axis)
    return lax.ppermute(x, axis, [(i, (i + by) % devices) for i in range(devices)])


def smooth_xy(v):
    rows, cols = v.shape
    col = lax.broadcasted_iota(jnp.int32, v.shape, 1)
    left = jnp.where(col == 0, 0.0, pltpu.roll(v, 1, 1))
    right = jnp.where(col == cols - 1, 0.0, pltpu.roll(v, cols - 1, 1))
    h = v + 0.5 * (left + right)
    return h + 0.5 * (pltpu.roll(h, 1, 0) + pltpu.roll(h, rows - 1, 0))


def to_wide(x):
    return jnp.concatenate([x[0:8], x[8:16]], axis=1)


def from_wide(x):
    return jnp.concatenate([x[:, 0:CCOLS], x[:, CCOLS:COLS]], axis=0)


Z1_RHS = 96
Z1_ACC = 160
Z1_CO = 224
Z1_ROWS = 232


def pack_z1(rhs, perm, acc, cperm, plus, minus, across, held, sems):
    first, z = place()
    upward = (first, jnp.logical_not(first), z == LINE - 1)
    copies = [pltpu.make_async_copy(cperm, held, sems.at[0])]
    for out, up in zip((plus, minus, across), upward):
        for base, ref, start, count in (
            (0, perm, jnp.where(up, ROWS, 0), 3),
            (Z1_RHS, rhs, jnp.where(up, 2 * ROWS, 0), 2),
            (Z1_ACC, acc, jnp.where(up, 2 * ROWS, 0), 2),
        ):
            copies.append(
                pltpu.make_async_copy(
                    ref.at[pl.ds(pl.multiple_of(start, ROWS), ROWS * count)],
                    out.at[pl.ds(base, ROWS * count)],
                    sems.at[len(copies)],
                )
            )
    for copy in copies:
        copy.start()
    for copy in copies:
        copy.wait()
    for out, up in zip((plus, minus, across), upward):
        out[Z1_CO : Z1_CO + 8, :] = to_wide(held[jnp.where(up, 1, 0)])


def fine_rows(own, lo, hi, base, depth, z, first, count):
    if z < 0:
        at = base + 32 * (z + depth)
        return lo[at + first : at + first + count, :]
    if z > 3:
        at = base + 32 * (z - 4)
        return hi[at + first : at + first + count, :]
    return own[z, first : first + count, :]


def coarse_plane(cperm, lo, hi, c):
    if c < 0:
        return from_wide(lo[Z1_CO : Z1_CO + 8, :])
    if c > 1:
        return from_wide(hi[Z1_CO : Z1_CO + 8, :])
    return cperm[c]


Y1_RHS = 30
Y1_ACC = 46
Y1_CO = 62
Y1_ROWS = 72


def pack_y1(rhs, perm, acc, cperm, plus, minus, across, up, down):
    lo, hi = below_above(plus, minus, across)
    for out, top in ((up, True), (down, False)):
        r3 = ROWS - 3 if top else 0
        r2 = ROWS - 2 if top else 0
        for k in range(10):
            out[3 * k : 3 * k + 3, :] = fine_rows(perm, lo, hi, 0, 3, k - 3, r3, 3)
        for k in range(8):
            at = Y1_RHS + 2 * k
            out[at : at + 2, :] = fine_rows(rhs, lo, hi, Z1_RHS, 2, k - 2, r2, 2)
            at = Y1_ACC + 2 * k
            out[at : at + 2, :] = fine_rows(acc, lo, hi, Z1_ACC, 2, k - 2, r2, 2)
        rc = CROWS - 1 if top else 0
        for k in range(4):
            plane = coarse_plane(cperm, lo, hi, k - 1)
            at = Y1_CO + k // 2
            lane = CCOLS * (k % 2)
            out[at : at + 1, lane : lane + CCOLS] = plane[rc : rc + 1, :]


def frame_kernel(rhs, perm, acc, cperm, plus, minus, across, ts, rs, cs, ct):
    lo, hi = below_above(plus, minus, across)
    zeros = jnp.zeros((FR, COLS), jnp.float32)
    for k in range(10):
        ts[k] = zeros
        ts[k, 4:36, :] = jnp.sqrt(fine_rows(perm, lo, hi, 0, 3, k - 3, 0, ROWS))
    for k in range(8):
        for ref, own, base in ((rs, rhs, Z1_RHS), (cs, acc, Z1_ACC)):
            ref[k] = zeros
            ref[k, 4:36, :] = fine_rows(own, lo, hi, base, 2, k - 2, 0, ROWS)
    for k in range(4):
        ct[k] = jnp.zeros((CR, CCOLS), jnp.float32)
        ct[k, 8:24, :] = jnp.sqrt(coarse_plane(cperm, lo, hi, k - 1))


def pre_kernel(
    masks, ts_in, rs_in, cs_in, ct_in, cacc, ylo, yhi,
    ts, rs, cs, ct_out, a_out, b_out, u_out, ab_out, plus_out, minus_out, across_out,
    xs, us, ds, fs,
):
    del ts_in, rs_in, cs_in, ct_in
    first, place_z = place()
    mlo = masks[0]
    mhi = masks[1]
    for k in range(10):
        ts[k, 1:4, :] = jnp.sqrt(ylo[3 * k : 3 * k + 3, :] * mlo)
        ts[k, 36:39, :] = jnp.sqrt(yhi[3 * k : 3 * k + 3, :] * mhi)
    for k in range(8):
        for ref, ybase in ((rs, Y1_RHS), (cs, Y1_ACC)):
            ref[k, 2:4, :] = ylo[ybase + 2 * k : ybase + 2 * k + 2, :] * mlo
            ref[k, 36:38, :] = yhi[ybase + 2 * k : ybase + 2 * k + 2, :] * mhi
    for k in range(10):
        xs[k] = smooth_xy(ts[k])
    for k in range(8):
        t = ts[k + 1]
        w = 2.0 * (xs[k + 1] + 0.5 * (xs[k] + xs[k + 2]) - t)
        d = t * w + cs[k]
        d = jnp.where(d > 0.0, d, 1.0)
        q = OMEGA * t / d
        if 2 <= k < 6:
            ds[k - 2] = d
        rs_k = rs[k]
        us[k] = q * rs_k
        cs[k] = q * t
    for k in range(8):
        xs[k] = smooth_xy(us[k])
    for k in range(6):
        a = us[k + 1]
        b = cs[k + 1]
        w = 2.0 * (xs[k + 1] + 0.5 * (xs[k] + xs[k + 2]) - a)
        a_out[k] = a
        b_out[k] = b
        u_out[k] = (1.0 + KEEP) * a + b * w
    for k in range(6):
        xs[k] = smooth_xy(u_out[k])
    sums = []
    for k in range(4):
        u = u_out[k + 1]
        t = ts[k + 3]
        w = 2.0 * (xs[k + 1] + 0.5 * (xs[k] + xs[k + 2]) - u)
        r = rs[k + 2] + t * w - ds[k] * (u / t)
        sums.append(r)
    pairs = []
    for k in range(2):
        both = sums[2 * k] + sums[2 * k + 1]
        halves = []
        for half in range(2):
            at = 2 * k + half
            fs[at] = both[:, CCOLS * half : CCOLS * half + CCOLS]
            halves.append(fs[at, pl.ds(4, CROWS, 2), :] + fs[at, pl.ds(5, CROWS, 2), :])
        pairs.append(jnp.concatenate(halves, axis=1))
    stacked = jnp.concatenate(pairs, axis=0)
    src = lax.broadcasted_iota(jnp.int32, (COLS, CCOLS), 0)
    dst = lax.broadcasted_iota(jnp.int32, (COLS, CCOLS), 1)
    fold = jnp.where(src // 2 == dst, 1.0, 0.0)
    res = jnp.dot(
        stacked, fold, precision=lax.Precision.HIGHEST, preferred_element_type=jnp.float32
    )
    for k in range(4):
        at = Y1_CO + k // 2
        lane = CCOLS * (k % 2)
        ct_out[k, 7:8, :] = jnp.sqrt(ylo[at : at + 1, lane : lane + CCOLS] * mlo)
        ct_out[k, 24:25, :] = jnp.sqrt(yhi[at : at + 1, lane : lane + CCOLS] * mhi)
    cx = [smooth_xy(ct_out[k]) for k in range(4)]
    for k in range(2):
        t = ct_out[k + 1]
        w = 2.0 * (cx[k + 1] + 0.5 * (cx[k] + cx[k + 2]) - t)
        t = t[8:24]
        d = t * w[8:24] + cacc[k]
        q = OMEGA * t / d
        a = q * res[CROWS * k : CROWS * k + CROWS]
        b = q * t
        for out in (ab_out, across_out):
            out[k] = a
            out[2 + k] = b
    for out, up, at in (
        (plus_out, first, 0),
        (minus_out, jnp.logical_not(first), 0),
        (across_out, place_z == LINE - 1, 4),
    ):
        plane = jnp.where(up, 3, 2)
        for k in range(4):
            row = 4 + 16 * (k // 2)
            lane = CCOLS * (k % 2)
            out[at + k] = u_out[plane, row : row + 16, lane : lane + CCOLS]


def pass_on(plus2, minus2, across, plus_out, minus_out):
    del across
    plus_out[...] = plus2[0:4]
    minus_out[...] = minus2[0:4]


def pack_far(ab, plus1, minus1, out):
    first, z = place()
    near_start = z < LINE // 2
    out[0:2] = ab[0:2]
    out[2] = ab[jnp.where(near_start, 2, 3)]
    out[3:7] = jnp.where(first == near_start, plus1[0:4], minus1[0:4])


Y2_B = 84
Y2_U = 156
Y2_ROWS = 200


def pack_y2(
    ab, u, plus1, minus1, across, plus2, minus2, plus3, minus3, far, up, down, dom, edge
):
    first, z = place()

    def below(plus, minus, k, places, other):
        return jnp.where(z < places, other, jnp.where(first, plus[k], minus[k]))

    def above(plus, minus, k, places, other):
        return jnp.where(z >= LINE - places, other, jnp.where(first, minus[k], plus[k]))

    for k in range(4):
        a = k < 2
        dom[6 + k if a else 17 + k] = ab[k]
        dom[4 + k if a else 15 + k] = below(plus1, minus1, k, 1, across[k])
        dom[8 + k if a else 19 + k] = above(plus1, minus1, k, 1, across[k])
        dom[2 + k if a else 13 + k] = below(plus2, minus2, k, 2, far[3 + k])
        dom[10 + k if a else 21 + k] = above(plus2, minus2, k, 2, far[3 + k])
        edge[k] = below(plus2, minus2, 4 + k, 1, across[4 + k])
        edge[4 + k] = above(plus2, minus2, 4 + k, 1, across[4 + k])
    for k in range(3):
        low = 3 if k == 2 else k
        dom[14 if k == 2 else k] = below(plus3, minus3, low, 3, far[k])
        dom[25 if k == 2 else 12 + k] = above(plus3, minus3, k, 3, far[k])
    for out, top_rows in ((up, True), (down, False)):
        row = CROWS - 6 if top_rows else 0
        for k in range(26):
            out[6 * k : 6 * k + 6, :] = dom[k, row : row + 6, :]
        for k in range(8):
            at = Y2_U + 4 * k
            for half in range(2):
                if 0 < k < 7:
                    row = 34 if top_rows else 4
                    rows = u[k - 1, row : row + 2, CCOLS * half : CCOLS * half + CCOLS]
                else:
                    piece = (0 if k == 0 else 4) + half
                    if top_rows:
                        rows = edge[piece + 2, 14:16, :]
                    else:
                        rows = edge[piece, 0:2, :]
                out[at + 2 * half : at + 2 * half + 2, :] = rows


def post_kernel(
    masks, t_in, a_in, b_in, u_in, ct, dom, edge, ylo, yhi,
    out, uf, cf, xs, ff,
):
    mlo = masks[0]
    mhi = masks[1]
    tile = jnp.zeros((8, CCOLS), jnp.float32)
    a = []
    b = [None]
    for k in range(26):
        ff[k, 0:8, :] = tile
        ff[k, 24:32, :] = tile
        ff[k, 2:8, :] = ylo[6 * k : 6 * k + 6, :] * mlo
        ff[k, 8:24, :] = dom[k]
        ff[k, 24:30, :] = yhi[6 * k : 6 * k + 6, :] * mhi
        (a if k < 14 else b).append(ff[k])
    link = [0.5] * 13
    for j in range(6):
        link[2 * j + 1] = 0.5 * masks[2 + j]
    u = list(a)
    for sweep in range(1, COARSE_SWEEPS):
        first, last = sweep, 13 - sweep
        smooth = {k: smooth_xy(u[k]) for k in range(first - 1, last + 2)}
        fresh = list(u)
        for k in range(first, last + 1):
            w = 2.0 * (
                smooth[k] + link[k - 1] * smooth[k - 1] + link[k] * smooth[k + 1] - u[k]
            )
            fresh[k] = KEEP * u[k] + a[k] + b[k] * w
        u = fresh
    corr = []
    for k in range(4):
        t = ct[k]
        inside = t > 0.0
        corr.append(jnp.where(inside, u[5 + k] / jnp.where(inside, t, 1.0), 0.0))
    stacked = jnp.concatenate(corr, axis=0)
    dst = lax.broadcasted_iota(jnp.int32, (CCOLS, COLS), 1)
    src = lax.broadcasted_iota(jnp.int32, (CCOLS, COLS), 0)
    spread = jnp.where(dst // 2 == src, 1.0, 0.0)
    wide = jnp.dot(
        stacked, spread, precision=lax.Precision.HIGHEST, preferred_element_type=jnp.float32
    )
    for k in range(4):
        for half in range(2):
            rows = wide[CR * k + 6 : CR * k + 26, CCOLS * half : CCOLS * half + CCOLS]
            cf[2 * k + half, pl.ds(0, 20, 2), :] = rows
            cf[2 * k + half, pl.ds(1, 20, 2), :] = rows
    zeros = jnp.zeros((FR, COLS), jnp.float32)
    for k in range(8):
        if 0 < k < 7:
            uf[k] = u_in[k - 1]
        else:
            uf[k] = zeros
            piece = 0 if k == 0 else 4
            for j in range(4):
                row = 4 + 16 * (j // 2)
                lane = CCOLS * (j % 2)
                uf[k, row : row + 16, lane : lane + CCOLS] = edge[piece + j]
        at = Y2_U + 4 * k
        for half in range(2):
            lane = CCOLS * half
            uf[k, 2:4, lane : lane + CCOLS] = ylo[at + 2 * half : at + 2 * half + 2, :] * mlo
            uf[k, 36:38, lane : lane + CCOLS] = yhi[at + 2 * half : at + 2 * half + 2, :] * mhi
        both = 2 * (k // 2)
        uf[k] = uf[k] + t_in[k + 1] * jnp.concatenate([cf[both, 0:FR], cf[both + 1, 0:FR]], axis=1)
    for k in range(8):
        xs[k] = smooth_xy(uf[k])
    for k in range(6):
        v = uf[k + 1]
        w = 2.0 * (xs[k + 1] + 0.5 * (xs[k] + xs[k + 2]) - v)
        uf[k + 1] = KEEP * v + a_in[k] + b_in[k] * w
    for k in range(6):
        xs[k] = smooth_xy(uf[k + 1])
    for k in range(4):
        v = uf[k + 2]
        w = 2.0 * (xs[k + 1] + 0.5 * (xs[k] + xs[k + 2]) - v)
        new = KEEP * v + a_in[k + 1] + b_in[k + 1] * w
        uf[k + 2] = new / t_in[k + 3]
        out[k] = uf[k + 2, 4:36, :]


VM = pl.BlockSpec(memory_space=pltpu.VMEM)
SM = pl.BlockSpec(memory_space=pltpu.SMEM)
HBM = pl.BlockSpec(memory_space=pltpu.HBM)


def f32(*shape):
    return jax.ShapeDtypeStruct(shape, jnp.float32)


def call(kernel, specs, outs, scratch=(), in_place=0):
    return pl.pallas_call(
        kernel,
        input_output_aliases={k + 1: k for k in range(in_place)},
        in_specs=specs,
        out_specs=jax.tree.map(lambda _: VM, outs),
        out_shape=outs,
        scratch_shapes=[
            pltpu.VMEM(shape, jnp.float32) if isinstance(shape, tuple) else shape
            for shape in scratch
        ],
        compiler_params=pltpu.CompilerParams(vmem_limit_bytes=8 * 1024 * 1024),
    )


def frame_call(*operands):
    return call(
        frame_kernel,
        [VM] * 7,
        (f32(10, FR, COLS), f32(8, FR, COLS), f32(8, FR, COLS), f32(4, CR, CCOLS)),
    )(*operands)


def pre_call(*operands):
    return call(
        pre_kernel,
        [SM] + [VM] * 7,
        (
            f32(10, FR, COLS), f32(8, FR, COLS), f32(8, FR, COLS), f32(4, CR, CCOLS),
            f32(6, FR, COLS), f32(6, FR, COLS), f32(6, FR, COLS), f32(4, CROWS, CCOLS),
            f32(4, CROWS, CCOLS), f32(4, CROWS, CCOLS), f32(8, CROWS, CCOLS),
        ),
        ((10, FR, COLS), (8, FR, COLS), (4, FR, COLS), (4, FR, CCOLS)),
        in_place=4,
    )(*operands)


def post_call(*operands):
    return call(
        post_kernel,
        [SM] + [VM] * 9,
        f32(4, ROWS, COLS),
        ((8, FR, COLS), (8, FR + 8, CCOLS), (8, FR, COLS), (26, CR, CCOLS)),
    )(*operands)


def on_device(pressure_rhs, permeability, accumulation, coarse_perm, coarse_accum, run_lengths):
    message = f32(Z1_ROWS, COLS)
    plus, minus, across = call(
        pack_z1,
        [HBM] * 4,
        (message, message, message),
        (pltpu.VMEM((2, CROWS, CCOLS), jnp.float32), pltpu.SemaphoreType.DMA((10,))),
    )(
        *(
            pltpu.with_memory_space_constraint(x, pltpu.HBM)
            for x in (
                pressure_rhs.reshape(-1, COLS),
                permeability.reshape(-1, COLS),
                accumulation.reshape(-1, COLS),
                coarse_perm,
            )
        )
    )
    across = between_lines(across, 1)
    plus = along_lines(plus, 1)
    minus = along_lines(minus, -1)

    slab = lax.axis_index("slab")
    pen = lax.axis_index("pen")
    starts = jnp.cumsum(run_lengths) - run_lengths
    blocks = slab - 2 + jnp.arange(6, dtype=jnp.int32)
    begins = jnp.any(starts[None, :] == blocks[:, None], axis=1)
    masks = jnp.concatenate(
        [
            jnp.stack([pen > 0, pen < lax.axis_size("pen") - 1]).astype(jnp.float32),
            1.0 - begins.astype(jnp.float32),
        ]
    )

    rows = f32(Y1_ROWS, COLS)
    up, down = call(pack_y1, [VM] * 7, (rows, rows))(
        pressure_rhs, permeability, accumulation, coarse_perm, plus, minus, across
    )
    ylo = rotated(up, "pen", 1)
    yhi = rotated(down, "pen", -1)

    frames = frame_call(
        pressure_rhs, permeability, accumulation, coarse_perm, plus, minus, across
    )
    t, _, _, ct, a, b, u, ab, plus, minus, across = pre_call(
        masks, *frames, coarse_accum, ylo, yhi
    )
    across = between_lines(across, 1)
    plus1 = along_lines(ab, 1)
    minus1 = along_lines(ab, -1)
    far = between_lines(
        call(pack_far, [VM] * 3, f32(7, CROWS, CCOLS))(ab, plus1, minus1), 3
    )
    plus2 = along_lines(jnp.concatenate([plus1, plus], axis=0), 1)
    minus2 = along_lines(jnp.concatenate([minus1, minus], axis=0), -1)
    block = f32(4, CROWS, CCOLS)
    plus, minus = call(pass_on, [VM] * 3, (block, block))(plus2, minus2, across)
    plus3 = along_lines(plus, 1)
    minus3 = along_lines(minus, -1)

    rows = f32(Y2_ROWS, CCOLS)
    up, down, dom, edge = call(
        pack_y2, [VM] * 10, (rows, rows, f32(26, CROWS, CCOLS), f32(8, CROWS, CCOLS))
    )(ab, u, plus1, minus1, across, plus2, minus2, plus3, minus3, far)
    ylo = rotated(up, "pen", 1)
    yhi = rotated(down, "pen", -1)

    return post_call(masks, t, a, b, u, ct, dom, edge, ylo, yhi)


def solution(mesh):
    return jax.shard_map(
        on_device,
        mesh=mesh,
        in_specs=(
            P("slab", "pen", None),
            P("slab", "pen", None),
            P("slab", "pen", None),
            P("slab", "pen", None),
            P("slab", "pen", None),
            P(),
        ),
        out_specs=P("slab", "pen", None),
        check_vma=False,
    )
```

```python
import jax
import jax.numpy as jnp
from jax import lax
from jax.experimental import pallas as pl
from jax.experimental.pallas import tpu as pltpu
from jax.sharding import PartitionSpec as P

OMEGA = 0.7
KEEP = 1.0 - OMEGA
COARSE_SWEEPS = 6

FR = 40
ROWS = 32
COLS = 256
CR = 32
CROWS = 16
CCOLS = 128


LINE = 16


def along_lines(x, by):
    slabs, pens = lax.axis_size("slab"), lax.axis_size("pen")
    pairs = []
    for slab in range(slabs):
        for pen in range(pens):
            line, z = divmod(slab, LINE)
            core = pen % 2
            step = (2 * LINE - 1 - z if core else z) + by
            step %= 2 * LINE
            core, z = (0, step) if step < LINE else (1, 2 * LINE - 1 - step)
            pairs.append((slab * pens + pen, (line * LINE + z) * pens + pen // 2 * 2 + core))
    return lax.ppermute(x, ("slab", "pen"), pairs)


def between_lines(x, apart):
    slabs, pens = lax.axis_size("slab"), lax.axis_size("pen")
    pairs = []
    for low in range(slabs - apart):
        if low // LINE != (low + apart) // LINE:
            for pen in range(pens):
                here, there = low * pens + pen, (low + apart) * pens + pen
                pairs += [(here, there), (there, here)]
    return lax.ppermute(x, ("slab", "pen"), pairs)


def place():
    return lax.axis_index("pen") % 2 == 0, lax.axis_index("slab") % LINE


class Picked:
    def __init__(self, first, one, other, end, across):
        self.parts = (first, one, other, end, across)

    def __getitem__(self, index):
        first, one, other, end, across = self.parts
        value = jnp.where(first, one[index], other[index])
        return jnp.where(end, across[index], value)


def below_above(plus, minus, across):
    first, z = place()
    return (
        Picked(first, plus, minus, z == 0, across),
        Picked(first, minus, plus, z == LINE - 1, across),
    )


def rotated(x, axis, by):
    devices = lax.axis_size(axis)
    return lax.ppermute(x, axis, [(i, (i + by) % devices) for i in range(devices)])


def smooth_xy(v):
    rows, cols = v.shape
    col = lax.broadcasted_iota(jnp.int32, v.shape, 1)
    left = jnp.where(col == 0, 0.0, pltpu.roll(v, 1, 1))
    right = jnp.where(col == cols - 1, 0.0, pltpu.roll(v, cols - 1, 1))
    h = v + 0.5 * (left + right)
    return h + 0.5 * (pltpu.roll(h, 1, 0) + pltpu.roll(h, rows - 1, 0))


def to_wide(x):
    return jnp.concatenate([x[0:8], x[8:16]], axis=1)


def from_wide(x):
    return jnp.concatenate([x[:, 0:CCOLS], x[:, CCOLS:COLS]], axis=0)


Z1_RHS = 96
Z1_ACC = 160
Z1_CO = 224
Z1_ROWS = 232


def pack_z1(rhs, perm, acc, cperm, plus, minus, across, held, sems):
    first, z = place()
    upward = (first, jnp.logical_not(first), z == LINE - 1)
    copies = [pltpu.make_async_copy(cperm, held, sems.at[0])]
    for out, up in zip((plus, minus, across), upward):
        for base, ref, start, count in (
            (0, perm, jnp.where(up, ROWS, 0), 3),
            (Z1_RHS, rhs, jnp.where(up, 2 * ROWS, 0), 2),
            (Z1_ACC, acc, jnp.where(up, 2 * ROWS, 0), 2),
        ):
            copies.append(
                pltpu.make_async_copy(
                    ref.at[pl.ds(pl.multiple_of(start, ROWS), ROWS * count)],
                    out.at[pl.ds(base, ROWS * count)],
                    sems.at[len(copies)],
                )
            )
    for copy in copies:
        copy.start()
    for copy in copies:
        copy.wait()
    for out, up in zip((plus, minus, across), upward):
        out[Z1_CO : Z1_CO + 8, :] = to_wide(held[jnp.where(up, 1, 0)])


def fine_rows(own, lo, hi, base, depth, z, first, count):
    if z < 0:
        at = base + 32 * (z + depth)
        return lo[at + first : at + first + count, :]
    if z > 3:
        at = base + 32 * (z - 4)
        return hi[at + first : at + first + count, :]
    return own[z, first : first + count, :]


def coarse_plane(cperm, lo, hi, c):
    if c < 0:
        return from_wide(lo[Z1_CO : Z1_CO + 8, :])
    if c > 1:
        return from_wide(hi[Z1_CO : Z1_CO + 8, :])
    return cperm[c]


Y1_RHS = 30
Y1_ACC = 46
Y1_CO = 62
Y1_ROWS = 72


def pack_y1(rhs, perm, acc, cperm, plus, minus, across, up, down):
    lo, hi = below_above(plus, minus, across)
    for out, top in ((up, True), (down, False)):
        r3 = ROWS - 3 if top else 0
        r2 = ROWS - 2 if top else 0
        for k in range(10):
            out[3 * k : 3 * k + 3, :] = fine_rows(perm, lo, hi, 0, 3, k - 3, r3, 3)
        for k in range(8):
            at = Y1_RHS + 2 * k
            out[at : at + 2, :] = fine_rows(rhs, lo, hi, Z1_RHS, 2, k - 2, r2, 2)
            at = Y1_ACC + 2 * k
            out[at : at + 2, :] = fine_rows(acc, lo, hi, Z1_ACC, 2, k - 2, r2, 2)
        rc = CROWS - 1 if top else 0
        for k in range(4):
            plane = coarse_plane(cperm, lo, hi, k - 1)
            at = Y1_CO + k // 2
            lane = CCOLS * (k % 2)
            out[at : at + 1, lane : lane + CCOLS] = plane[rc : rc + 1, :]


def frame_kernel(rhs, perm, acc, cperm, plus, minus, across, ts, rs, cs, ct):
    lo, hi = below_above(plus, minus, across)
    zeros = jnp.zeros((FR, COLS), jnp.float32)
    for k in range(10):
        ts[k] = zeros
        ts[k, 4:36, :] = jnp.sqrt(fine_rows(perm, lo, hi, 0, 3, k - 3, 0, ROWS))
    for k in range(8):
        for ref, own, base in ((rs, rhs, Z1_RHS), (cs, acc, Z1_ACC)):
            ref[k] = zeros
            ref[k, 4:36, :] = fine_rows(own, lo, hi, base, 2, k - 2, 0, ROWS)
    for k in range(4):
        ct[k] = jnp.zeros((CR, CCOLS), jnp.float32)
        ct[k, 8:24, :] = jnp.sqrt(coarse_plane(cperm, lo, hi, k - 1))


def pre_kernel(
    masks, ts_in, rs_in, cs_in, ct_in, cacc, ylo, yhi,
    ts, rs, cs, ct_out, a_out, b_out, u_out, ab_out, plus_out, minus_out, across_out,
    xs, us, ds, fs,
):
    del ts_in, rs_in, cs_in, ct_in
    first, place_z = place()
    mlo = masks[0]
    mhi = masks[1]
    for k in range(10):
        ts[k, 1:4, :] = jnp.sqrt(ylo[3 * k : 3 * k + 3, :] * mlo)
        ts[k, 36:39, :] = jnp.sqrt(yhi[3 * k : 3 * k + 3, :] * mhi)
    for k in range(8):
        for ref, ybase in ((rs, Y1_RHS), (cs, Y1_ACC)):
            ref[k, 2:4, :] = ylo[ybase + 2 * k : ybase + 2 * k + 2, :] * mlo
            ref[k, 36:38, :] = yhi[ybase + 2 * k : ybase + 2 * k + 2, :] * mhi
    for k in range(10):
        xs[k] = smooth_xy(ts[k])
    for k in range(8):
        t = ts[k + 1]
        w = 2.0 * (xs[k + 1] + 0.5 * (xs[k] + xs[k + 2]) - t)
        d = t * w + cs[k]
        d = jnp.where(d > 0.0, d, 1.0)
        q = OMEGA * t / d
        if 2 <= k < 6:
            ds[k - 2] = d
        rs_k = rs[k]
        us[k] = q * rs_k
        cs[k] = q * t
    for k in range(8):
        xs[k] = smooth_xy(us[k])
    for k in range(6):
        a = us[k + 1]
        b = cs[k + 1]
        w = 2.0 * (xs[k + 1] + 0.5 * (xs[k] + xs[k + 2]) - a)
        a_out[k] = a
        b_out[k] = b
        u_out[k] = (1.0 + KEEP) * a + b * w
    for k in range(6):
        xs[k] = smooth_xy(u_out[k])
    sums = []
    for k in range(4):
        u = u_out[k + 1]
        t = ts[k + 3]
        w = 2.0 * (xs[k + 1] + 0.5 * (xs[k] + xs[k + 2]) - u)
        r = rs[k + 2] + t * w - ds[k] * (u / t)
        sums.append(r)
    pairs = []
    for k in range(2):
        both = sums[2 * k] + sums[2 * k + 1]
        halves = []
        for half in range(2):
            at = 2 * k + half
            fs[at] = both[:, CCOLS * half : CCOLS * half + CCOLS]
            halves.append(fs[at, pl.ds(4, CROWS, 2), :] + fs[at, pl.ds(5, CROWS, 2), :])
        pairs.append(jnp.concatenate(halves, axis=1))
    stacked = jnp.concatenate(pairs, axis=0)
    src = lax.broadcasted_iota(jnp.int32, (COLS, CCOLS), 0)
    dst = lax.broadcasted_iota(jnp.int32, (COLS, CCOLS), 1)
    fold = jnp.where(src // 2 == dst, 1.0, 0.0)
    res = jnp.dot(
        stacked, fold, precision=lax.Precision.HIGHEST, preferred_element_type=jnp.float32
    )
    for k in range(4):
        at = Y1_CO + k // 2
        lane = CCOLS * (k % 2)
        ct_out[k, 7:8, :] = jnp.sqrt(ylo[at : at + 1, lane : lane + CCOLS] * mlo)
        ct_out[k, 24:25, :] = jnp.sqrt(yhi[at : at + 1, lane : lane + CCOLS] * mhi)
    cx = [smooth_xy(ct_out[k]) for k in range(4)]
    for k in range(2):
        t = ct_out[k + 1]
        w = 2.0 * (cx[k + 1] + 0.5 * (cx[k] + cx[k + 2]) - t)
        t = t[8:24]
        d = t * w[8:24] + cacc[k]
        q = OMEGA * t / d
        a = q * res[CROWS * k : CROWS * k + CROWS]
        b = q * t
        for out in (ab_out, across_out):
            out[k] = a
            out[2 + k] = b
    for out, up, at in (
        (plus_out, first, 0),
        (minus_out, jnp.logical_not(first), 0),
        (across_out, place_z == LINE - 1, 4),
    ):
        plane = jnp.where(up, 3, 2)
        for k in range(4):
            row = 4 + 16 * (k // 2)
            lane = CCOLS * (k % 2)
            out[at + k] = u_out[plane, row : row + 16, lane : lane + CCOLS]


def pass_on(plus2, minus2, across, plus_out, minus_out):
    del across
    plus_out[...] = plus2[0:4]
    minus_out[...] = minus2[0:4]


def pack_far(ab, plus1, minus1, out):
    first, z = place()
    near_start = z < LINE // 2
    out[0:2] = ab[0:2]
    out[2] = ab[jnp.where(near_start, 2, 3)]
    out[3:7] = jnp.where(first == near_start, plus1[0:4], minus1[0:4])


Y2_B = 84
Y2_U = 156
Y2_ROWS = 200


def pack_y2(
    ab, u, plus1, minus1, across, plus2, minus2, plus3, minus3, far, up, down, dom, edge
):
    first, z = place()

    def below(plus, minus, k, places, other):
        return jnp.where(z < places, other, jnp.where(first, plus[k], minus[k]))

    def above(plus, minus, k, places, other):
        return jnp.where(z >= LINE - places, other, jnp.where(first, minus[k], plus[k]))

    for k in range(4):
        a = k < 2
        dom[6 + k if a else 17 + k] = ab[k]
        dom[4 + k if a else 15 + k] = below(plus1, minus1, k, 1, across[k])
        dom[8 + k if a else 19 + k] = above(plus1, minus1, k, 1, across[k])
        dom[2 + k if a else 13 + k] = below(plus2, minus2, k, 2, far[3 + k])
        dom[10 + k if a else 21 + k] = above(plus2, minus2, k, 2, far[3 + k])
        edge[k] = below(plus2, minus2, 4 + k, 1, across[4 + k])
        edge[4 + k] = above(plus2, minus2, 4 + k, 1, across[4 + k])
    for k in range(3):
        low = 3 if k == 2 else k
        dom[14 if k == 2 else k] = below(plus3, minus3, low, 3, far[k])
        dom[25 if k == 2 else 12 + k] = above(plus3, minus3, k, 3, far[k])
    for out, top_rows in ((up, True), (down, False)):
        row = CROWS - 6 if top_rows else 0
        for k in range(26):
            out[6 * k : 6 * k + 6, :] = dom[k, row : row + 6, :]
        for k in range(8):
            at = Y2_U + 4 * k
            for half in range(2):
                if 0 < k < 7:
                    row = 34 if top_rows else 4
                    rows = u[k - 1, row : row + 2, CCOLS * half : CCOLS * half + CCOLS]
                else:
                    piece = (0 if k == 0 else 4) + half
                    if top_rows:
                        rows = edge[piece + 2, 14:16, :]
                    else:
                        rows = edge[piece, 0:2, :]
                out[at + 2 * half : at + 2 * half + 2, :] = rows


def window_kernel(u_in, dom, edge, ff, uf):
    for k in range(26):
        ff[k] = jnp.zeros((CR, CCOLS), jnp.float32)
        ff[k, 8:24, :] = dom[k]
    for k in range(8):
        if 0 < k < 7:
            uf[k] = u_in[k - 1]
        else:
            uf[k] = jnp.zeros((FR, COLS), jnp.float32)
            piece = 0 if k == 0 else 4
            for j in range(4):
                row = 4 + 16 * (j // 2)
                lane = CCOLS * (j % 2)
                uf[k, row : row + 16, lane : lane + CCOLS] = edge[piece + j]


def post_kernel(
    masks, ff_in, uf_in, t_in, a_in, b_in, ct, ylo, yhi,
    ff, uf, out, cf, xs,
):
    del ff_in, uf_in
    mlo = masks[0]
    mhi = masks[1]
    a = []
    b = [None]
    for k in range(26):
        ff[k, 2:8, :] = ylo[6 * k : 6 * k + 6, :] * mlo
        ff[k, 24:30, :] = yhi[6 * k : 6 * k + 6, :] * mhi
        (a if k < 14 else b).append(ff[k])
    link = [0.5] * 13
    for j in range(6):
        link[2 * j + 1] = 0.5 * masks[2 + j]
    u = list(a)
    for sweep in range(1, COARSE_SWEEPS):
        first, last = sweep, 13 - sweep
        smooth = {k: smooth_xy(u[k]) for k in range(first - 1, last + 2)}
        fresh = list(u)
        for k in range(first, last + 1):
            w = 2.0 * (
                smooth[k] + link[k - 1] * smooth[k - 1] + link[k] * smooth[k + 1] - u[k]
            )
            fresh[k] = KEEP * u[k] + a[k] + b[k] * w
        u = fresh
    corr = []
    for k in range(4):
        t = ct[k]
        inside = t > 0.0
        corr.append(jnp.where(inside, u[5 + k] / jnp.where(inside, t, 1.0), 0.0))
    stacked = jnp.concatenate(corr, axis=0)
    dst = lax.broadcasted_iota(jnp.int32, (CCOLS, COLS), 1)
    src = lax.broadcasted_iota(jnp.int32, (CCOLS, COLS), 0)
    spread = jnp.where(dst // 2 == src, 1.0, 0.0)
    wide = jnp.dot(
        stacked, spread, precision=lax.Precision.HIGHEST, preferred_element_type=jnp.float32
    )
    for k in range(4):
        for half in range(2):
            rows = wide[CR * k + 6 : CR * k + 26, CCOLS * half : CCOLS * half + CCOLS]
            cf[2 * k + half, pl.ds(0, 20, 2), :] = rows
            cf[2 * k + half, pl.ds(1, 20, 2), :] = rows
    for k in range(8):
        at = Y2_U + 4 * k
        for half in range(2):
            lane = CCOLS * half
            uf[k, 2:4, lane : lane + CCOLS] = ylo[at + 2 * half : at + 2 * half + 2, :] * mlo
            uf[k, 36:38, lane : lane + CCOLS] = yhi[at + 2 * half : at + 2 * half + 2, :] * mhi
        both = 2 * (k // 2)
        uf[k] = uf[k] + t_in[k + 1] * jnp.concatenate([cf[both, 0:FR], cf[both + 1, 0:FR]], axis=1)
    for k in range(8):
        xs[k] = smooth_xy(uf[k])
    for k in range(6):
        v = uf[k + 1]
        w = 2.0 * (xs[k + 1] + 0.5 * (xs[k] + xs[k + 2]) - v)
        uf[k + 1] = KEEP * v + a_in[k] + b_in[k] * w
    for k in range(6):
        xs[k] = smooth_xy(uf[k + 1])
    for k in range(4):
        v = uf[k + 2]
        w = 2.0 * (xs[k + 1] + 0.5 * (xs[k] + xs[k + 2]) - v)
        new = KEEP * v + a_in[k + 1] + b_in[k + 1] * w
        uf[k + 2] = new / t_in[k + 3]
        out[k] = uf[k + 2, 4:36, :]


VM = pl.BlockSpec(memory_space=pltpu.VMEM)
SM = pl.BlockSpec(memory_space=pltpu.SMEM)
HBM = pl.BlockSpec(memory_space=pltpu.HBM)


def f32(*shape):
    return jax.ShapeDtypeStruct(shape, jnp.float32)


def call(kernel, specs, outs, scratch=(), in_place=0):
    return pl.pallas_call(
        kernel,
        input_output_aliases={k + 1: k for k in range(in_place)},
        in_specs=specs,
        out_specs=jax.tree.map(lambda _: VM, outs),
        out_shape=outs,
        scratch_shapes=[
            pltpu.VMEM(shape, jnp.float32) if isinstance(shape, tuple) else shape
            for shape in scratch
        ],
        compiler_params=pltpu.CompilerParams(vmem_limit_bytes=8 * 1024 * 1024),
    )


def frame_call(*operands):
    return call(
        frame_kernel,
        [VM] * 7,
        (f32(10, FR, COLS), f32(8, FR, COLS), f32(8, FR, COLS), f32(4, CR, CCOLS)),
    )(*operands)


def pre_call(*operands):
    return call(
        pre_kernel,
        [SM] + [VM] * 7,
        (
            f32(10, FR, COLS), f32(8, FR, COLS), f32(8, FR, COLS), f32(4, CR, CCOLS),
            f32(6, FR, COLS), f32(6, FR, COLS), f32(6, FR, COLS), f32(4, CROWS, CCOLS),
            f32(4, CROWS, CCOLS), f32(4, CROWS, CCOLS), f32(8, CROWS, CCOLS),
        ),
        ((10, FR, COLS), (8, FR, COLS), (4, FR, COLS), (4, FR, CCOLS)),
        in_place=4,
    )(*operands)


def window_call(*operands):
    return call(
        window_kernel, [VM] * 3, (f32(26, CR, CCOLS), f32(8, FR, COLS))
    )(*operands)


def post_call(*operands):
    return call(
        post_kernel,
        [SM] + [VM] * 8,
        (f32(26, CR, CCOLS), f32(8, FR, COLS), f32(4, ROWS, COLS)),
        ((8, FR + 8, CCOLS), (8, FR, COLS)),
        in_place=2,
    )(*operands)


def on_device(pressure_rhs, permeability, accumulation, coarse_perm, coarse_accum, run_lengths):
    message = f32(Z1_ROWS, COLS)
    plus, minus, across = call(
        pack_z1,
        [HBM] * 4,
        (message, message, message),
        (pltpu.VMEM((2, CROWS, CCOLS), jnp.float32), pltpu.SemaphoreType.DMA((10,))),
    )(
        *(
            pltpu.with_memory_space_constraint(x, pltpu.HBM)
            for x in (
                pressure_rhs.reshape(-1, COLS),
                permeability.reshape(-1, COLS),
                accumulation.reshape(-1, COLS),
                coarse_perm,
            )
        )
    )
    across = between_lines(across, 1)
    plus = along_lines(plus, 1)
    minus = along_lines(minus, -1)

    slab = lax.axis_index("slab")
    pen = lax.axis_index("pen")
    starts = jnp.cumsum(run_lengths) - run_lengths
    blocks = slab - 2 + jnp.arange(6, dtype=jnp.int32)
    begins = jnp.any(starts[None, :] == blocks[:, None], axis=1)
    masks = jnp.concatenate(
        [
            jnp.stack([pen > 0, pen < lax.axis_size("pen") - 1]).astype(jnp.float32),
            1.0 - begins.astype(jnp.float32),
        ]
    )

    rows = f32(Y1_ROWS, COLS)
    up, down = call(pack_y1, [VM] * 7, (rows, rows))(
        pressure_rhs, permeability, accumulation, coarse_perm, plus, minus, across
    )
    ylo = rotated(up, "pen", 1)
    yhi = rotated(down, "pen", -1)

    frames = frame_call(
        pressure_rhs, permeability, accumulation, coarse_perm, plus, minus, across
    )
    t, _, _, ct, a, b, u, ab, plus, minus, across = pre_call(
        masks, *frames, coarse_accum, ylo, yhi
    )
    across = between_lines(across, 1)
    plus1 = along_lines(ab, 1)
    minus1 = along_lines(ab, -1)
    far = between_lines(
        call(pack_far, [VM] * 3, f32(7, CROWS, CCOLS))(ab, plus1, minus1), 3
    )
    plus2 = along_lines(jnp.concatenate([plus1, plus], axis=0), 1)
    minus2 = along_lines(jnp.concatenate([minus1, minus], axis=0), -1)
    block = f32(4, CROWS, CCOLS)
    plus, minus = call(pass_on, [VM] * 3, (block, block))(plus2, minus2, across)
    plus3 = along_lines(plus, 1)
    minus3 = along_lines(minus, -1)

    rows = f32(Y2_ROWS, CCOLS)
    up, down, dom, edge = call(
        pack_y2, [VM] * 10, (rows, rows, f32(26, CROWS, CCOLS), f32(8, CROWS, CCOLS))
    )(ab, u, plus1, minus1, across, plus2, minus2, plus3, minus3, far)
    ylo = rotated(up, "pen", 1)
    yhi = rotated(down, "pen", -1)

    return post_call(masks, *window_call(u, dom, edge), t, a, b, ct, ylo, yhi)[2]


def solution(mesh):
    return jax.shard_map(
        on_device,
        mesh=mesh,
        in_specs=(
            P("slab", "pen", None),
            P("slab", "pen", None),
            P("slab", "pen", None),
            P("slab", "pen", None),
            P("slab", "pen", None),
            P(),
        ),
        out_specs=P("slab", "pen", None),
        check_vma=False,
    )
```

```python
import jax
import jax.numpy as jnp
from jax import lax
from jax.experimental import pallas as pl
from jax.experimental.pallas import tpu as pltpu
from jax.sharding import PartitionSpec as P

OMEGA = 0.7
KEEP = 1.0 - OMEGA
COARSE_SWEEPS = 6

FR = 40
ROWS = 32
COLS = 256
CR = 32
CROWS = 16
CCOLS = 128


LINE = 16


def along_lines(x, by):
    slabs, pens = lax.axis_size("slab"), lax.axis_size("pen")
    pairs = []
    for slab in range(slabs):
        for pen in range(pens):
            line, z = divmod(slab, LINE)
            core = pen % 2
            step = (2 * LINE - 1 - z if core else z) + by
            step %= 2 * LINE
            core, z = (0, step) if step < LINE else (1, 2 * LINE - 1 - step)
            pairs.append((slab * pens + pen, (line * LINE + z) * pens + pen // 2 * 2 + core))
    return lax.ppermute(x, ("slab", "pen"), pairs)


def between_lines(x, apart):
    slabs, pens = lax.axis_size("slab"), lax.axis_size("pen")
    pairs = []
    for low in range(slabs - apart):
        if low // LINE != (low + apart) // LINE:
            for pen in range(pens):
                here, there = low * pens + pen, (low + apart) * pens + pen
                pairs += [(here, there), (there, here)]
    return lax.ppermute(x, ("slab", "pen"), pairs)


def place():
    return lax.axis_index("pen") % 2 == 0, lax.axis_index("slab") % LINE


class Picked:
    def __init__(self, first, one, other, end, across):
        self.parts = (first, one, other, end, across)

    def __getitem__(self, index):
        first, one, other, end, across = self.parts
        value = jnp.where(first, one[index], other[index])
        return jnp.where(end, across[index], value)


def below_above(plus, minus, across):
    first, z = place()
    return (
        Picked(first, plus, minus, z == 0, across),
        Picked(first, minus, plus, z == LINE - 1, across),
    )


def rotated(x, axis, by):
    devices = lax.axis_size(axis)
    return lax.ppermute(x, axis, [(i, (i + by) % devices) for i in range(devices)])


def smooth_xy(v):
    rows, cols = v.shape
    col = lax.broadcasted_iota(jnp.int32, v.shape, 1)
    left = jnp.where(col == 0, 0.0, pltpu.roll(v, 1, 1))
    right = jnp.where(col == cols - 1, 0.0, pltpu.roll(v, cols - 1, 1))
    h = v + 0.5 * (left + right)
    return h + 0.5 * (pltpu.roll(h, 1, 0) + pltpu.roll(h, rows - 1, 0))


def to_wide(x):
    return jnp.concatenate([x[0:8], x[8:16]], axis=1)


def from_wide(x):
    return jnp.concatenate([x[:, 0:CCOLS], x[:, CCOLS:COLS]], axis=0)


Z1_RHS = 96
Z1_ACC = 160
Z1_CO = 224
Z1_ROWS = 232


def pack_z1(rhs, perm, acc, cperm, plus, minus, across, held, sems):
    first, z = place()
    upward = (first, jnp.logical_not(first), z == LINE - 1)
    copies = [pltpu.make_async_copy(cperm, held, sems.at[0])]
    for out, up in zip((plus, minus, across), upward):
        for base, ref, start, count in (
            (0, perm, jnp.where(up, ROWS, 0), 3),
            (Z1_RHS, rhs, jnp.where(up, 2 * ROWS, 0), 2),
            (Z1_ACC, acc, jnp.where(up, 2 * ROWS, 0), 2),
        ):
            copies.append(
                pltpu.make_async_copy(
                    ref.at[pl.ds(pl.multiple_of(start, ROWS), ROWS * count)],
                    out.at[pl.ds(base, ROWS * count)],
                    sems.at[len(copies)],
                )
            )
    for copy in copies:
        copy.start()
    for copy in copies:
        copy.wait()
    for out, up in zip((plus, minus, across), upward):
        out[Z1_CO : Z1_CO + 8, :] = to_wide(held[jnp.where(up, 1, 0)])


def fine_rows(own, lo, hi, base, depth, z, first, count):
    if z < 0:
        at = base + 32 * (z + depth)
        return lo[at + first : at + first + count, :]
    if z > 3:
        at = base + 32 * (z - 4)
        return hi[at + first : at + first + count, :]
    return own[z, first : first + count, :]


def coarse_plane(cperm, lo, hi, c):
    if c < 0:
        return from_wide(lo[Z1_CO : Z1_CO + 8, :])
    if c > 1:
        return from_wide(hi[Z1_CO : Z1_CO + 8, :])
    return cperm[c]


Y1_RHS = 30
Y1_ACC = 46
Y1_CO = 62
Y1_ROWS = 72


def pack_y1(rhs, perm, acc, cperm, plus, minus, across, up, down):
    lo, hi = below_above(plus, minus, across)
    for out, top in ((up, True), (down, False)):
        r3 = ROWS - 3 if top else 0
        r2 = ROWS - 2 if top else 0
        for k in range(10):
            out[3 * k : 3 * k + 3, :] = fine_rows(perm, lo, hi, 0, 3, k - 3, r3, 3)
        for k in range(8):
            at = Y1_RHS + 2 * k
            out[at : at + 2, :] = fine_rows(rhs, lo, hi, Z1_RHS, 2, k - 2, r2, 2)
            at = Y1_ACC + 2 * k
            out[at : at + 2, :] = fine_rows(acc, lo, hi, Z1_ACC, 2, k - 2, r2, 2)
        rc = CROWS - 1 if top else 0
        for k in range(4):
            plane = coarse_plane(cperm, lo, hi, k - 1)
            at = Y1_CO + k // 2
            lane = CCOLS * (k % 2)
            out[at : at + 1, lane : lane + CCOLS] = plane[rc : rc + 1, :]


def frame_kernel(rhs, perm, acc, cperm, plus, minus, across, ts, rs, cs, ct):
    lo, hi = below_above(plus, minus, across)
    zeros = jnp.zeros((FR, COLS), jnp.float32)
    for k in range(10):
        ts[k] = zeros
        ts[k, 4:36, :] = jnp.sqrt(fine_rows(perm, lo, hi, 0, 3, k - 3, 0, ROWS))
    for k in range(8):
        for ref, own, base in ((rs, rhs, Z1_RHS), (cs, acc, Z1_ACC)):
            ref[k] = zeros
            ref[k, 4:36, :] = fine_rows(own, lo, hi, base, 2, k - 2, 0, ROWS)
    for k in range(4):
        ct[k] = jnp.zeros((CR, CCOLS), jnp.float32)
        ct[k, 8:24, :] = jnp.sqrt(coarse_plane(cperm, lo, hi, k - 1))


def pre_kernel(
    masks, ts_in, rs_in, cs_in, ct_in, cacc, ylo, yhi,
    ts, rs, cs, ct_out, a_out, b_out, u_out, ab_out, plus_out, minus_out, across_out,
    xs, us, ds, fs,
):
    del ts_in, rs_in, cs_in, ct_in
    first, place_z = place()
    mlo = masks[0]
    mhi = masks[1]
    for k in range(10):
        ts[k, 1:4, :] = jnp.sqrt(ylo[3 * k : 3 * k + 3, :] * mlo)
        ts[k, 36:39, :] = jnp.sqrt(yhi[3 * k : 3 * k + 3, :] * mhi)
    for k in range(8):
        for ref, ybase in ((rs, Y1_RHS), (cs, Y1_ACC)):
            ref[k, 2:4, :] = ylo[ybase + 2 * k : ybase + 2 * k + 2, :] * mlo
            ref[k, 36:38, :] = yhi[ybase + 2 * k : ybase + 2 * k + 2, :] * mhi
    for k in range(10):
        xs[k] = smooth_xy(ts[k])
    for k in range(8):
        t = ts[k + 1]
        w = 2.0 * (xs[k + 1] + 0.5 * (xs[k] + xs[k + 2]) - t)
        d = t * w + cs[k]
        d = jnp.where(d > 0.0, d, 1.0)
        q = OMEGA * t / d
        if 2 <= k < 6:
            ds[k - 2] = d
        rs_k = rs[k]
        us[k] = q * rs_k
        cs[k] = q * t
    for k in range(8):
        xs[k] = smooth_xy(us[k])
    for k in range(6):
        a = us[k + 1]
        b = cs[k + 1]
        w = 2.0 * (xs[k + 1] + 0.5 * (xs[k] + xs[k + 2]) - a)
        a_out[k] = a
        b_out[k] = b
        u_out[k] = (1.0 + KEEP) * a + b * w
    for k in range(6):
        xs[k] = smooth_xy(u_out[k])
    sums = []
    for k in range(4):
        u = u_out[k + 1]
        t = ts[k + 3]
        w = 2.0 * (xs[k + 1] + 0.5 * (xs[k] + xs[k + 2]) - u)
        r = rs[k + 2] + t * w - ds[k] * (u / t)
        sums.append(r)
    pairs = []
    for k in range(2):
        both = sums[2 * k] + sums[2 * k + 1]
        halves = []
        for half in range(2):
            at = 2 * k + half
            fs[at] = both[:, CCOLS * half : CCOLS * half + CCOLS]
            halves.append(fs[at, pl.ds(4, CROWS, 2), :] + fs[at, pl.ds(5, CROWS, 2), :])
        pairs.append(jnp.concatenate(halves, axis=1))
    stacked = jnp.concatenate(pairs, axis=0)
    src = lax.broadcasted_iota(jnp.int32, (COLS, CCOLS), 0)
    dst = lax.broadcasted_iota(jnp.int32, (COLS, CCOLS), 1)
    fold = jnp.where(src // 2 == dst, 1.0, 0.0)
    res = jnp.dot(
        stacked, fold, precision=lax.Precision.HIGHEST, preferred_element_type=jnp.float32
    )
    for k in range(4):
        at = Y1_CO + k // 2
        lane = CCOLS * (k % 2)
        ct_out[k, 7:8, :] = jnp.sqrt(ylo[at : at + 1, lane : lane + CCOLS] * mlo)
        ct_out[k, 24:25, :] = jnp.sqrt(yhi[at : at + 1, lane : lane + CCOLS] * mhi)
    cx = [smooth_xy(ct_out[k]) for k in range(4)]
    for k in range(2):
        t = ct_out[k + 1]
        w = 2.0 * (cx[k + 1] + 0.5 * (cx[k] + cx[k + 2]) - t)
        t = t[8:24]
        d = t * w[8:24] + cacc[k]
        q = OMEGA * t / d
        a = q * res[CROWS * k : CROWS * k + CROWS]
        b = q * t
        for out in (ab_out, across_out):
            out[k] = a
            out[2 + k] = b
    for out, up, at in (
        (plus_out, first, 0),
        (minus_out, jnp.logical_not(first), 0),
        (across_out, place_z == LINE - 1, 4),
    ):
        plane = jnp.where(up, 3, 2)
        for k in range(4):
            row = 4 + 16 * (k // 2)
            lane = CCOLS * (k % 2)
            out[at + k] = u_out[plane, row : row + 16, lane : lane + CCOLS]


def pack_far(ab, plus1, minus1, out):
    first, z = place()
    near_start = z < LINE // 2
    out[0:2] = ab[0:2]
    out[2] = ab[jnp.where(near_start, 2, 3)]
    out[3:7] = jnp.where(first == near_start, plus1[0:4], minus1[0:4])


Y2_B = 84
Y2_U = 156
Y2_ROWS = 200


def pack_y2(
    ab, u, plus1, minus1, across, plus2, minus2, plus3, minus3, far, up, down, dom, edge
):
    first, z = place()

    def below(plus, minus, k, places, other):
        return jnp.where(z < places, other, jnp.where(first, plus[k], minus[k]))

    def above(plus, minus, k, places, other):
        return jnp.where(z >= LINE - places, other, jnp.where(first, minus[k], plus[k]))

    for k in range(4):
        a = k < 2
        dom[6 + k if a else 17 + k] = ab[k]
        dom[4 + k if a else 15 + k] = below(plus1, minus1, k, 1, across[k])
        dom[8 + k if a else 19 + k] = above(plus1, minus1, k, 1, across[k])
        dom[2 + k if a else 13 + k] = below(plus2, minus2, k, 2, far[3 + k])
        dom[10 + k if a else 21 + k] = above(plus2, minus2, k, 2, far[3 + k])
        edge[k] = below(plus2, minus2, 4 + k, 1, across[4 + k])
        edge[4 + k] = above(plus2, minus2, 4 + k, 1, across[4 + k])
    for k in range(3):
        low = 3 if k == 2 else k
        dom[14 if k == 2 else k] = below(plus3, minus3, low, 3, far[k])
        dom[25 if k == 2 else 12 + k] = above(plus3, minus3, k, 3, far[k])
    for out, top_rows in ((up, True), (down, False)):
        row = CROWS - 6 if top_rows else 0
        for k in range(26):
            out[6 * k : 6 * k + 6, :] = dom[k, row : row + 6, :]
        for k in range(8):
            at = Y2_U + 4 * k
            for half in range(2):
                if 0 < k < 7:
                    row = 34 if top_rows else 4
                    rows = u[k - 1, row : row + 2, CCOLS * half : CCOLS * half + CCOLS]
                else:
                    piece = (0 if k == 0 else 4) + half
                    if top_rows:
                        rows = edge[piece + 2, 14:16, :]
                    else:
                        rows = edge[piece, 0:2, :]
                out[at + 2 * half : at + 2 * half + 2, :] = rows


def window_kernel(u_in, dom, edge, ff, uf):
    for k in range(26):
        ff[k] = jnp.zeros((CR, CCOLS), jnp.float32)
        ff[k, 8:24, :] = dom[k]
    for k in range(8):
        if 0 < k < 7:
            uf[k] = u_in[k - 1]
        else:
            uf[k] = jnp.zeros((FR, COLS), jnp.float32)
            piece = 0 if k == 0 else 4
            for j in range(4):
                row = 4 + 16 * (j // 2)
                lane = CCOLS * (j % 2)
                uf[k, row : row + 16, lane : lane + CCOLS] = edge[piece + j]


def post_kernel(
    masks, ff_in, uf_in, t_in, a_in, b_in, ct, ylo, yhi,
    ff, uf, out, cf, xs,
):
    del ff_in, uf_in
    mlo = masks[0]
    mhi = masks[1]
    a = []
    b = [None]
    for k in range(26):
        ff[k, 2:8, :] = ylo[6 * k : 6 * k + 6, :] * mlo
        ff[k, 24:30, :] = yhi[6 * k : 6 * k + 6, :] * mhi
        (a if k < 14 else b).append(ff[k])
    link = [0.5] * 13
    for j in range(6):
        link[2 * j + 1] = 0.5 * masks[2 + j]
    u = list(a)
    for sweep in range(1, COARSE_SWEEPS):
        first, last = sweep, 13 - sweep
        smooth = {k: smooth_xy(u[k]) for k in range(first - 1, last + 2)}
        fresh = list(u)
        for k in range(first, last + 1):
            w = 2.0 * (
                smooth[k] + link[k - 1] * smooth[k - 1] + link[k] * smooth[k + 1] - u[k]
            )
            fresh[k] = KEEP * u[k] + a[k] + b[k] * w
        u = fresh
    corr = []
    for k in range(4):
        t = ct[k]
        inside = t > 0.0
        corr.append(jnp.where(inside, u[5 + k] / jnp.where(inside, t, 1.0), 0.0))
    stacked = jnp.concatenate(corr, axis=0)
    dst = lax.broadcasted_iota(jnp.int32, (CCOLS, COLS), 1)
    src = lax.broadcasted_iota(jnp.int32, (CCOLS, COLS), 0)
    spread = jnp.where(dst // 2 == src, 1.0, 0.0)
    wide = jnp.dot(
        stacked, spread, precision=lax.Precision.HIGHEST, preferred_element_type=jnp.float32
    )
    for k in range(4):
        for half in range(2):
            rows = wide[CR * k + 6 : CR * k + 26, CCOLS * half : CCOLS * half + CCOLS]
            cf[2 * k + half, pl.ds(0, 20, 2), :] = rows
            cf[2 * k + half, pl.ds(1, 20, 2), :] = rows
    for k in range(8):
        at = Y2_U + 4 * k
        for half in range(2):
            lane = CCOLS * half
            uf[k, 2:4, lane : lane + CCOLS] = ylo[at + 2 * half : at + 2 * half + 2, :] * mlo
            uf[k, 36:38, lane : lane + CCOLS] = yhi[at + 2 * half : at + 2 * half + 2, :] * mhi
        both = 2 * (k // 2)
        uf[k] = uf[k] + t_in[k + 1] * jnp.concatenate([cf[both, 0:FR], cf[both + 1, 0:FR]], axis=1)
    for k in range(8):
        xs[k] = smooth_xy(uf[k])
    for k in range(6):
        v = uf[k + 1]
        w = 2.0 * (xs[k + 1] + 0.5 * (xs[k] + xs[k + 2]) - v)
        uf[k + 1] = KEEP * v + a_in[k] + b_in[k] * w
    for k in range(6):
        xs[k] = smooth_xy(uf[k + 1])
    for k in range(4):
        v = uf[k + 2]
        w = 2.0 * (xs[k + 1] + 0.5 * (xs[k] + xs[k + 2]) - v)
        new = KEEP * v + a_in[k + 1] + b_in[k + 1] * w
        uf[k + 2] = new / t_in[k + 3]
        out[k] = uf[k + 2, 4:36, :]


VM = pl.BlockSpec(memory_space=pltpu.VMEM)
SM = pl.BlockSpec(memory_space=pltpu.SMEM)
HBM = pl.BlockSpec(memory_space=pltpu.HBM)


def f32(*shape):
    return jax.ShapeDtypeStruct(shape, jnp.float32)


def call(kernel, specs, outs, scratch=(), in_place=0):
    return pl.pallas_call(
        kernel,
        input_output_aliases={k + 1: k for k in range(in_place)},
        in_specs=specs,
        out_specs=jax.tree.map(lambda _: VM, outs),
        out_shape=outs,
        scratch_shapes=[
            pltpu.VMEM(shape, jnp.float32) if isinstance(shape, tuple) else shape
            for shape in scratch
        ],
        compiler_params=pltpu.CompilerParams(vmem_limit_bytes=8 * 1024 * 1024),
    )


def frame_call(*operands):
    return call(
        frame_kernel,
        [VM] * 7,
        (f32(10, FR, COLS), f32(8, FR, COLS), f32(8, FR, COLS), f32(4, CR, CCOLS)),
    )(*operands)


def pre_call(*operands):
    return call(
        pre_kernel,
        [SM] + [VM] * 7,
        (
            f32(10, FR, COLS), f32(8, FR, COLS), f32(8, FR, COLS), f32(4, CR, CCOLS),
            f32(6, FR, COLS), f32(6, FR, COLS), f32(6, FR, COLS), f32(4, CROWS, CCOLS),
            f32(4, CROWS, CCOLS), f32(4, CROWS, CCOLS), f32(8, CROWS, CCOLS),
        ),
        ((10, FR, COLS), (8, FR, COLS), (4, FR, COLS), (4, FR, CCOLS)),
        in_place=4,
    )(*operands)


def window_call(*operands):
    return call(
        window_kernel, [VM] * 3, (f32(26, CR, CCOLS), f32(8, FR, COLS))
    )(*operands)


def post_call(*operands):
    return call(
        post_kernel,
        [SM] + [VM] * 8,
        (f32(26, CR, CCOLS), f32(8, FR, COLS), f32(4, ROWS, COLS)),
        ((8, FR + 8, CCOLS), (8, FR, COLS)),
        in_place=2,
    )(*operands)


def on_device(pressure_rhs, permeability, accumulation, coarse_perm, coarse_accum, run_lengths):
    message = f32(Z1_ROWS, COLS)
    plus, minus, across = call(
        pack_z1,
        [HBM] * 4,
        (message, message, message),
        (pltpu.VMEM((2, CROWS, CCOLS), jnp.float32), pltpu.SemaphoreType.DMA((10,))),
    )(
        *(
            pltpu.with_memory_space_constraint(x, pltpu.HBM)
            for x in (
                pressure_rhs.reshape(-1, COLS),
                permeability.reshape(-1, COLS),
                accumulation.reshape(-1, COLS),
                coarse_perm,
            )
        )
    )
    across = between_lines(across, 1)
    plus = along_lines(plus, 1)
    minus = along_lines(minus, -1)

    slab = lax.axis_index("slab")
    pen = lax.axis_index("pen")
    starts = jnp.cumsum(run_lengths) - run_lengths
    blocks = slab - 2 + jnp.arange(6, dtype=jnp.int32)
    begins = jnp.any(starts[None, :] == blocks[:, None], axis=1)
    masks = jnp.concatenate(
        [
            jnp.stack([pen > 0, pen < lax.axis_size("pen") - 1]).astype(jnp.float32),
            1.0 - begins.astype(jnp.float32),
        ]
    )

    rows = f32(Y1_ROWS, COLS)
    up, down = call(pack_y1, [VM] * 7, (rows, rows))(
        pressure_rhs, permeability, accumulation, coarse_perm, plus, minus, across
    )
    ylo = rotated(up, "pen", 1)
    yhi = rotated(down, "pen", -1)

    frames = frame_call(
        pressure_rhs, permeability, accumulation, coarse_perm, plus, minus, across
    )
    t, _, _, ct, a, b, u, ab, plus, minus, across = pre_call(
        masks, *frames, coarse_accum, ylo, yhi
    )
    across = between_lines(across, 1)
    plus1 = along_lines(ab, 1)
    minus1 = along_lines(ab, -1)
    far = between_lines(
        call(pack_far, [VM] * 3, f32(7, CROWS, CCOLS))(ab, plus1, minus1), 3
    )
    plus2 = along_lines(jnp.concatenate([plus1, plus], axis=0), 1)
    minus2 = along_lines(jnp.concatenate([minus1, minus], axis=0), -1)
    plus3 = along_lines(plus2[0:4], 1)
    minus3 = along_lines(minus2[0:4], -1)

    rows = f32(Y2_ROWS, CCOLS)
    up, down, dom, edge = call(
        pack_y2, [VM] * 10, (rows, rows, f32(26, CROWS, CCOLS), f32(8, CROWS, CCOLS))
    )(ab, u, plus1, minus1, across, plus2, minus2, plus3, minus3, far)
    ylo = rotated(up, "pen", 1)
    yhi = rotated(down, "pen", -1)

    return post_call(masks, *window_call(u, dom, edge), t, a, b, ct, ylo, yhi)[2]


def solution(mesh):
    return jax.shard_map(
        on_device,
        mesh=mesh,
        in_specs=(
            P("slab", "pen", None),
            P("slab", "pen", None),
            P("slab", "pen", None),
            P("slab", "pen", None),
            P("slab", "pen", None),
            P(),
        ),
        out_specs=P("slab", "pen", None),
        check_vma=False,
    )
```

```python
import jax
import jax.numpy as jnp
from jax import lax
from jax.experimental import pallas as pl
from jax.experimental.pallas import tpu as pltpu
from jax.sharding import PartitionSpec as P

OMEGA = 0.7
KEEP = 1.0 - OMEGA
COARSE_SWEEPS = 6

FR = 40
ROWS = 32
COLS = 256
CR = 32
CROWS = 16
CCOLS = 128


LINE = 16


def along_lines(x, by):
    slabs, pens = lax.axis_size("slab"), lax.axis_size("pen")
    pairs = []
    for slab in range(slabs):
        for pen in range(pens):
            line, z = divmod(slab, LINE)
            core = pen % 2
            step = (2 * LINE - 1 - z if core else z) + by
            step %= 2 * LINE
            core, z = (0, step) if step < LINE else (1, 2 * LINE - 1 - step)
            pairs.append((slab * pens + pen, (line * LINE + z) * pens + pen // 2 * 2 + core))
    return lax.ppermute(x, ("slab", "pen"), pairs)


def between_lines(x, apart):
    slabs, pens = lax.axis_size("slab"), lax.axis_size("pen")
    pairs = []
    for low in range(slabs - apart):
        if low // LINE != (low + apart) // LINE:
            for pen in range(pens):
                here, there = low * pens + pen, (low + apart) * pens + pen
                pairs += [(here, there), (there, here)]
    return lax.ppermute(x, ("slab", "pen"), pairs)


def place():
    return lax.axis_index("pen") % 2 == 0, lax.axis_index("slab") % LINE


class Picked:
    def __init__(self, first, one, other, end, across):
        self.parts = (first, one, other, end, across)

    def __getitem__(self, index):
        first, one, other, end, across = self.parts
        value = jnp.where(first, one[index], other[index])
        return jnp.where(end, across[index], value)


def below_above(plus, minus, across):
    first, z = place()
    return (
        Picked(first, plus, minus, z == 0, across),
        Picked(first, minus, plus, z == LINE - 1, across),
    )


def rotated(x, axis, by):
    devices = lax.axis_size(axis)
    return lax.ppermute(x, axis, [(i, (i + by) % devices) for i in range(devices)])


def smooth_x(v):
    cols = v.shape[1]
    col = lax.broadcasted_iota(jnp.int32, v.shape, 1)
    left = jnp.where(col == 0, 0.0, pltpu.roll(v, 1, 1))
    right = jnp.where(col == cols - 1, 0.0, pltpu.roll(v, cols - 1, 1))
    return v + 0.5 * (left + right)


def smooth_y(h):
    rows = h.shape[0]
    return h + 0.5 * (pltpu.roll(h, 1, 0) + pltpu.roll(h, rows - 1, 0))


def smooth_xy(v):
    return smooth_y(smooth_x(v))


def to_wide(x):
    return jnp.concatenate([x[0:8], x[8:16]], axis=1)


def from_wide(x):
    return jnp.concatenate([x[:, 0:CCOLS], x[:, CCOLS:COLS]], axis=0)


Z1_RHS = 96
Z1_ACC = 160
Z1_CO = 224
Z1_ROWS = 232


def pack_z1(rhs, perm, acc, cperm, plus, minus, across, held, sems):
    first, z = place()
    upward = (first, jnp.logical_not(first), z == LINE - 1)
    copies = [pltpu.make_async_copy(cperm, held, sems.at[0])]
    for out, up in zip((plus, minus, across), upward):
        for base, ref, start, count in (
            (0, perm, jnp.where(up, ROWS, 0), 3),
            (Z1_RHS, rhs, jnp.where(up, 2 * ROWS, 0), 2),
            (Z1_ACC, acc, jnp.where(up, 2 * ROWS, 0), 2),
        ):
            copies.append(
                pltpu.make_async_copy(
                    ref.at[pl.ds(pl.multiple_of(start, ROWS), ROWS * count)],
                    out.at[pl.ds(base, ROWS * count)],
                    sems.at[len(copies)],
                )
            )
    for copy in copies:
        copy.start()
    for copy in copies:
        copy.wait()
    for out, up in zip((plus, minus, across), upward):
        out[Z1_CO : Z1_CO + 8, :] = to_wide(held[jnp.where(up, 1, 0)])


def fine_rows(own, lo, hi, base, depth, z, first, count):
    if z < 0:
        at = base + 32 * (z + depth)
        return lo[at + first : at + first + count, :]
    if z > 3:
        at = base + 32 * (z - 4)
        return hi[at + first : at + first + count, :]
    return own[z, first : first + count, :]


def coarse_plane(cperm, lo, hi, c):
    if c < 0:
        return from_wide(lo[Z1_CO : Z1_CO + 8, :])
    if c > 1:
        return from_wide(hi[Z1_CO : Z1_CO + 8, :])
    return cperm[c]


Y1_RHS = 30
Y1_ACC = 46
Y1_CO = 62
Y1_ROWS = 72


def pack_y1(rhs, perm, acc, cperm, plus, minus, across, up, down):
    lo, hi = below_above(plus, minus, across)
    for out, top in ((up, True), (down, False)):
        r3 = ROWS - 3 if top else 0
        r2 = ROWS - 2 if top else 0
        for k in range(10):
            out[3 * k : 3 * k + 3, :] = fine_rows(perm, lo, hi, 0, 3, k - 3, r3, 3)
        for k in range(8):
            at = Y1_RHS + 2 * k
            out[at : at + 2, :] = fine_rows(rhs, lo, hi, Z1_RHS, 2, k - 2, r2, 2)
            at = Y1_ACC + 2 * k
            out[at : at + 2, :] = fine_rows(acc, lo, hi, Z1_ACC, 2, k - 2, r2, 2)
        rc = CROWS - 1 if top else 0
        for k in range(4):
            plane = coarse_plane(cperm, lo, hi, k - 1)
            at = Y1_CO + k // 2
            lane = CCOLS * (k % 2)
            out[at : at + 1, lane : lane + CCOLS] = plane[rc : rc + 1, :]


def frame_kernel(rhs, perm, acc, cperm, plus, minus, across, ts, rs, cs, ct, hs):
    lo, hi = below_above(plus, minus, across)
    zeros = jnp.zeros((FR, COLS), jnp.float32)
    for k in range(10):
        ts[k] = zeros
        ts[k, 4:36, :] = jnp.sqrt(fine_rows(perm, lo, hi, 0, 3, k - 3, 0, ROWS))
        hs[k] = smooth_x(ts[k])
    for k in range(8):
        for ref, own, base in ((rs, rhs, Z1_RHS), (cs, acc, Z1_ACC)):
            ref[k] = zeros
            ref[k, 4:36, :] = fine_rows(own, lo, hi, base, 2, k - 2, 0, ROWS)
    for k in range(4):
        ct[k] = jnp.zeros((CR, CCOLS), jnp.float32)
        ct[k, 8:24, :] = jnp.sqrt(coarse_plane(cperm, lo, hi, k - 1))


def pre_kernel(
    masks, ts_in, rs_in, cs_in, ct_in, hs_in, cacc, ylo, yhi,
    ts, rs, cs, ct_out, hs, a_out, b_out, u_out, ab_out, plus_out, minus_out, across_out,
    xs, us, ds, fs,
):
    del ts_in, rs_in, cs_in, ct_in, hs_in
    first, place_z = place()
    mlo = masks[0]
    mhi = masks[1]
    for k in range(10):
        ts[k, 1:4, :] = jnp.sqrt(ylo[3 * k : 3 * k + 3, :] * mlo)
        ts[k, 36:39, :] = jnp.sqrt(yhi[3 * k : 3 * k + 3, :] * mhi)
    for k in range(8):
        for ref, ybase in ((rs, Y1_RHS), (cs, Y1_ACC)):
            ref[k, 2:4, :] = ylo[ybase + 2 * k : ybase + 2 * k + 2, :] * mlo
            ref[k, 36:38, :] = yhi[ybase + 2 * k : ybase + 2 * k + 2, :] * mhi
    for k in range(10):
        for tile in (0, 32):
            hs[k, tile : tile + 8, :] = smooth_x(ts[k, tile : tile + 8, :])
        xs[k] = smooth_y(hs[k])
    for k in range(8):
        t = ts[k + 1]
        w = 2.0 * (xs[k + 1] + 0.5 * (xs[k] + xs[k + 2]) - t)
        d = t * w + cs[k]
        d = jnp.where(d > 0.0, d, 1.0)
        q = OMEGA * t / d
        if 2 <= k < 6:
            ds[k - 2] = d
        rs_k = rs[k]
        us[k] = q * rs_k
        cs[k] = q * t
    for k in range(8):
        xs[k] = smooth_xy(us[k])
    for k in range(6):
        a = us[k + 1]
        b = cs[k + 1]
        w = 2.0 * (xs[k + 1] + 0.5 * (xs[k] + xs[k + 2]) - a)
        a_out[k] = a
        b_out[k] = b
        u_out[k] = (1.0 + KEEP) * a + b * w
    for k in range(6):
        xs[k] = smooth_xy(u_out[k])
    sums = []
    for k in range(4):
        u = u_out[k + 1]
        t = ts[k + 3]
        w = 2.0 * (xs[k + 1] + 0.5 * (xs[k] + xs[k + 2]) - u)
        r = rs[k + 2] + t * w - ds[k] * (u / t)
        sums.append(r)
    pairs = []
    for k in range(2):
        both = sums[2 * k] + sums[2 * k + 1]
        halves = []
        for half in range(2):
            at = 2 * k + half
            fs[at] = both[:, CCOLS * half : CCOLS * half + CCOLS]
            halves.append(fs[at, pl.ds(4, CROWS, 2), :] + fs[at, pl.ds(5, CROWS, 2), :])
        pairs.append(jnp.concatenate(halves, axis=1))
    stacked = jnp.concatenate(pairs, axis=0)
    src = lax.broadcasted_iota(jnp.int32, (COLS, CCOLS), 0)
    dst = lax.broadcasted_iota(jnp.int32, (COLS, CCOLS), 1)
    fold = jnp.where(src // 2 == dst, 1.0, 0.0)
    res = jnp.dot(
        stacked, fold, precision=lax.Precision.HIGHEST, preferred_element_type=jnp.float32
    )
    for k in range(4):
        at = Y1_CO + k // 2
        lane = CCOLS * (k % 2)
        ct_out[k, 7:8, :] = jnp.sqrt(ylo[at : at + 1, lane : lane + CCOLS] * mlo)
        ct_out[k, 24:25, :] = jnp.sqrt(yhi[at : at + 1, lane : lane + CCOLS] * mhi)
    cx = [smooth_xy(ct_out[k]) for k in range(4)]
    for k in range(2):
        t = ct_out[k + 1]
        w = 2.0 * (cx[k + 1] + 0.5 * (cx[k] + cx[k + 2]) - t)
        t = t[8:24]
        d = t * w[8:24] + cacc[k]
        q = OMEGA * t / d
        a = q * res[CROWS * k : CROWS * k + CROWS]
        b = q * t
        for out in (ab_out, across_out):
            out[k] = a
            out[2 + k] = b
    for out, up, at in (
        (plus_out, first, 0),
        (minus_out, jnp.logical_not(first), 0),
        (across_out, place_z == LINE - 1, 4),
    ):
        plane = jnp.where(up, 3, 2)
        for k in range(4):
            row = 4 + 16 * (k // 2)
            lane = CCOLS * (k % 2)
            out[at + k] = u_out[plane, row : row + 16, lane : lane + CCOLS]


def pass_on(plus2, minus2, across, plus_out, minus_out):
    del across
    plus_out[...] = plus2[0:4]
    minus_out[...] = minus2[0:4]


def pack_far(ab, plus1, minus1, out):
    first, z = place()
    near_start = z < LINE // 2
    out[0:2] = ab[0:2]
    out[2] = ab[jnp.where(near_start, 2, 3)]
    out[3:7] = jnp.where(first == near_start, plus1[0:4], minus1[0:4])


Y2_B = 84
Y2_U = 156
Y2_ROWS = 200


def pack_y2(
    ab, u, plus1, minus1, across, plus2, minus2, plus3, minus3, far, up, down, dom, edge
):
    first, z = place()

    def below(plus, minus, k, places, other):
        return jnp.where(z < places, other, jnp.where(first, plus[k], minus[k]))

    def above(plus, minus, k, places, other):
        return jnp.where(z >= LINE - places, other, jnp.where(first, minus[k], plus[k]))

    for k in range(4):
        a = k < 2
        dom[6 + k if a else 17 + k] = ab[k]
        dom[4 + k if a else 15 + k] = below(plus1, minus1, k, 1, across[k])
        dom[8 + k if a else 19 + k] = above(plus1, minus1, k, 1, across[k])
        dom[2 + k if a else 13 + k] = below(plus2, minus2, k, 2, far[3 + k])
        dom[10 + k if a else 21 + k] = above(plus2, minus2, k, 2, far[3 + k])
        edge[k] = below(plus2, minus2, 4 + k, 1, across[4 + k])
        edge[4 + k] = above(plus2, minus2, 4 + k, 1, across[4 + k])
    for k in range(3):
        low = 3 if k == 2 else k
        dom[14 if k == 2 else k] = below(plus3, minus3, low, 3, far[k])
        dom[25 if k == 2 else 12 + k] = above(plus3, minus3, k, 3, far[k])
    for out, top_rows in ((up, True), (down, False)):
        row = CROWS - 6 if top_rows else 0
        for k in range(26):
            out[6 * k : 6 * k + 6, :] = dom[k, row : row + 6, :]
        for k in range(8):
            at = Y2_U + 4 * k
            for half in range(2):
                if 0 < k < 7:
                    row = 34 if top_rows else 4
                    rows = u[k - 1, row : row + 2, CCOLS * half : CCOLS * half + CCOLS]
                else:
                    piece = (0 if k == 0 else 4) + half
                    if top_rows:
                        rows = edge[piece + 2, 14:16, :]
                    else:
                        rows = edge[piece, 0:2, :]
                out[at + 2 * half : at + 2 * half + 2, :] = rows


def window_kernel(u_in, dom, edge, ff, uf):
    for k in range(26):
        ff[k] = jnp.zeros((CR, CCOLS), jnp.float32)
        ff[k, 8:24, :] = dom[k]
    for k in range(8):
        if 0 < k < 7:
            uf[k] = u_in[k - 1]
        else:
            uf[k] = jnp.zeros((FR, COLS), jnp.float32)
            piece = 0 if k == 0 else 4
            for j in range(4):
                row = 4 + 16 * (j // 2)
                lane = CCOLS * (j % 2)
                uf[k, row : row + 16, lane : lane + CCOLS] = edge[piece + j]


def post_kernel(
    masks, ff_in, uf_in, t_in, a_in, b_in, ct, ylo, yhi,
    ff, uf, out, cf, xs,
):
    del ff_in, uf_in
    mlo = masks[0]
    mhi = masks[1]
    a = []
    b = [None]
    for k in range(26):
        ff[k, 2:8, :] = ylo[6 * k : 6 * k + 6, :] * mlo
        ff[k, 24:30, :] = yhi[6 * k : 6 * k + 6, :] * mhi
        (a if k < 14 else b).append(ff[k])
    link = [0.5] * 13
    for j in range(6):
        link[2 * j + 1] = 0.5 * masks[2 + j]
    u = list(a)
    for sweep in range(1, COARSE_SWEEPS):
        first, last = sweep, 13 - sweep
        smooth = {k: smooth_xy(u[k]) for k in range(first - 1, last + 2)}
        fresh = list(u)
        for k in range(first, last + 1):
            w = 2.0 * (
                smooth[k] + link[k - 1] * smooth[k - 1] + link[k] * smooth[k + 1] - u[k]
            )
            fresh[k] = KEEP * u[k] + a[k] + b[k] * w
        u = fresh
    corr = []
    for k in range(4):
        t = ct[k]
        inside = t > 0.0
        corr.append(jnp.where(inside, u[5 + k] / jnp.where(inside, t, 1.0), 0.0))
    stacked = jnp.concatenate(corr, axis=0)
    dst = lax.broadcasted_iota(jnp.int32, (CCOLS, COLS), 1)
    src = lax.broadcasted_iota(jnp.int32, (CCOLS, COLS), 0)
    spread = jnp.where(dst // 2 == src, 1.0, 0.0)
    wide = jnp.dot(
        stacked, spread, precision=lax.Precision.HIGHEST, preferred_element_type=jnp.float32
    )
    for k in range(4):
        for half in range(2):
            rows = wide[CR * k + 6 : CR * k + 26, CCOLS * half : CCOLS * half + CCOLS]
            cf[2 * k + half, pl.ds(0, 20, 2), :] = rows
            cf[2 * k + half, pl.ds(1, 20, 2), :] = rows
    for k in range(8):
        at = Y2_U + 4 * k
        for half in range(2):
            lane = CCOLS * half
            uf[k, 2:4, lane : lane + CCOLS] = ylo[at + 2 * half : at + 2 * half + 2, :] * mlo
            uf[k, 36:38, lane : lane + CCOLS] = yhi[at + 2 * half : at + 2 * half + 2, :] * mhi
        both = 2 * (k // 2)
        uf[k] = uf[k] + t_in[k + 1] * jnp.concatenate([cf[both, 0:FR], cf[both + 1, 0:FR]], axis=1)
    for k in range(8):
        xs[k] = smooth_xy(uf[k])
    for k in range(6):
        v = uf[k + 1]
        w = 2.0 * (xs[k + 1] + 0.5 * (xs[k] + xs[k + 2]) - v)
        uf[k + 1] = KEEP * v + a_in[k] + b_in[k] * w
    for k in range(6):
        xs[k] = smooth_xy(uf[k + 1])
    for k in range(4):
        v = uf[k + 2]
        w = 2.0 * (xs[k + 1] + 0.5 * (xs[k] + xs[k + 2]) - v)
        new = KEEP * v + a_in[k + 1] + b_in[k + 1] * w
        uf[k + 2] = new / t_in[k + 3]
        out[k] = uf[k + 2, 4:36, :]


VM = pl.BlockSpec(memory_space=pltpu.VMEM)
SM = pl.BlockSpec(memory_space=pltpu.SMEM)
HBM = pl.BlockSpec(memory_space=pltpu.HBM)


def f32(*shape):
    return jax.ShapeDtypeStruct(shape, jnp.float32)


def call(kernel, specs, outs, scratch=(), in_place=0):
    return pl.pallas_call(
        kernel,
        input_output_aliases={k + 1: k for k in range(in_place)},
        in_specs=specs,
        out_specs=jax.tree.map(lambda _: VM, outs),
        out_shape=outs,
        scratch_shapes=[
            pltpu.VMEM(shape, jnp.float32) if isinstance(shape, tuple) else shape
            for shape in scratch
        ],
        compiler_params=pltpu.CompilerParams(vmem_limit_bytes=8 * 1024 * 1024),
    )


def frame_call(*operands):
    return call(
        frame_kernel,
        [VM] * 7,
        (
            f32(10, FR, COLS), f32(8, FR, COLS), f32(8, FR, COLS), f32(4, CR, CCOLS),
            f32(10, FR, COLS),
        ),
    )(*operands)


def pre_call(*operands):
    return call(
        pre_kernel,
        [SM] + [VM] * 8,
        (
            f32(10, FR, COLS), f32(8, FR, COLS), f32(8, FR, COLS), f32(4, CR, CCOLS),
            f32(10, FR, COLS), f32(6, FR, COLS), f32(6, FR, COLS), f32(6, FR, COLS), f32(4, CROWS, CCOLS),
            f32(4, CROWS, CCOLS), f32(4, CROWS, CCOLS), f32(8, CROWS, CCOLS),
        ),
        ((10, FR, COLS), (8, FR, COLS), (4, FR, COLS), (4, FR, CCOLS)),
        in_place=5,
    )(*operands)


def window_call(*operands):
    return call(
        window_kernel, [VM] * 3, (f32(26, CR, CCOLS), f32(8, FR, COLS))
    )(*operands)


def post_call(*operands):
    return call(
        post_kernel,
        [SM] + [VM] * 8,
        (f32(26, CR, CCOLS), f32(8, FR, COLS), f32(4, ROWS, COLS)),
        ((8, FR + 8, CCOLS), (8, FR, COLS)),
        in_place=2,
    )(*operands)


def on_device(pressure_rhs, permeability, accumulation, coarse_perm, coarse_accum, run_lengths):
    message = f32(Z1_ROWS, COLS)
    plus, minus, across = call(
        pack_z1,
        [HBM] * 4,
        (message, message, message),
        (pltpu.VMEM((2, CROWS, CCOLS), jnp.float32), pltpu.SemaphoreType.DMA((10,))),
    )(
        *(
            pltpu.with_memory_space_constraint(x, pltpu.HBM)
            for x in (
                pressure_rhs.reshape(-1, COLS),
                permeability.reshape(-1, COLS),
                accumulation.reshape(-1, COLS),
                coarse_perm,
            )
        )
    )
    across = between_lines(across, 1)
    plus = along_lines(plus, 1)
    minus = along_lines(minus, -1)

    slab = lax.axis_index("slab")
    pen = lax.axis_index("pen")
    starts = jnp.cumsum(run_lengths) - run_lengths
    blocks = slab - 2 + jnp.arange(6, dtype=jnp.int32)
    begins = jnp.any(starts[None, :] == blocks[:, None], axis=1)
    masks = jnp.concatenate(
        [
            jnp.stack([pen > 0, pen < lax.axis_size("pen") - 1]).astype(jnp.float32),
            1.0 - begins.astype(jnp.float32),
        ]
    )

    rows = f32(Y1_ROWS, COLS)
    up, down = call(pack_y1, [VM] * 7, (rows, rows))(
        pressure_rhs, permeability, accumulation, coarse_perm, plus, minus, across
    )
    ylo = rotated(up, "pen", 1)
    yhi = rotated(down, "pen", -1)

    frames = frame_call(
        pressure_rhs, permeability, accumulation, coarse_perm, plus, minus, across
    )
    t, _, _, ct, _, a, b, u, ab, plus, minus, across = pre_call(
        masks, *frames, coarse_accum, ylo, yhi
    )
    across = between_lines(across, 1)
    plus1 = along_lines(ab, 1)
    minus1 = along_lines(ab, -1)
    far = between_lines(
        call(pack_far, [VM] * 3, f32(7, CROWS, CCOLS))(ab, plus1, minus1), 3
    )
    plus2 = along_lines(jnp.concatenate([plus1, plus], axis=0), 1)
    minus2 = along_lines(jnp.concatenate([minus1, minus], axis=0), -1)
    block = f32(4, CROWS, CCOLS)
    plus, minus = call(pass_on, [VM] * 3, (block, block))(plus2, minus2, across)
    plus3 = along_lines(plus, 1)
    minus3 = along_lines(minus, -1)

    rows = f32(Y2_ROWS, CCOLS)
    up, down, dom, edge = call(
        pack_y2, [VM] * 10, (rows, rows, f32(26, CROWS, CCOLS), f32(8, CROWS, CCOLS))
    )(ab, u, plus1, minus1, across, plus2, minus2, plus3, minus3, far)
    ylo = rotated(up, "pen", 1)
    yhi = rotated(down, "pen", -1)

    return post_call(masks, *window_call(u, dom, edge), t, a, b, ct, ylo, yhi)[2]


def solution(mesh):
    return jax.shard_map(
        on_device,
        mesh=mesh,
        in_specs=(
            P("slab", "pen", None),
            P("slab", "pen", None),
            P("slab", "pen", None),
            P("slab", "pen", None),
            P("slab", "pen", None),
            P(),
        ),
        out_specs=P("slab", "pen", None),
        check_vma=False,
    )
```

```python
import jax
import jax.numpy as jnp
from jax import lax
from jax.experimental import pallas as pl
from jax.experimental.pallas import tpu as pltpu
from jax.sharding import PartitionSpec as P

OMEGA = 0.7
KEEP = 1.0 - OMEGA
COARSE_SWEEPS = 6

FR = 40
ROWS = 32
COLS = 256
CR = 32
CROWS = 16
CCOLS = 128


LINE = 16


def along_lines(x, by):
    slabs, pens = lax.axis_size("slab"), lax.axis_size("pen")
    pairs = []
    for slab in range(slabs):
        for pen in range(pens):
            line, z = divmod(slab, LINE)
            core = pen % 2
            step = (2 * LINE - 1 - z if core else z) + by
            step %= 2 * LINE
            core, z = (0, step) if step < LINE else (1, 2 * LINE - 1 - step)
            pairs.append((slab * pens + pen, (line * LINE + z) * pens + pen // 2 * 2 + core))
    return lax.ppermute(x, ("slab", "pen"), pairs)


def between_lines(x, apart):
    slabs, pens = lax.axis_size("slab"), lax.axis_size("pen")
    pairs = []
    for low in range(slabs - apart):
        if low // LINE != (low + apart) // LINE:
            for pen in range(pens):
                here, there = low * pens + pen, (low + apart) * pens + pen
                pairs += [(here, there), (there, here)]
    return lax.ppermute(x, ("slab", "pen"), pairs)


def place():
    return lax.axis_index("pen") % 2 == 0, lax.axis_index("slab") % LINE


class Picked:
    def __init__(self, first, one, other, end, across):
        self.parts = (first, one, other, end, across)

    def __getitem__(self, index):
        first, one, other, end, across = self.parts
        value = jnp.where(first, one[index], other[index])
        return jnp.where(end, across[index], value)


def below_above(plus, minus, across):
    first, z = place()
    return (
        Picked(first, plus, minus, z == 0, across),
        Picked(first, minus, plus, z == LINE - 1, across),
    )


def rotated(x, axis, by):
    devices = lax.axis_size(axis)
    return lax.ppermute(x, axis, [(i, (i + by) % devices) for i in range(devices)])


def smooth_x(v):
    cols = v.shape[1]
    col = lax.broadcasted_iota(jnp.int32, v.shape, 1)
    left = jnp.where(col == 0, 0.0, pltpu.roll(v, 1, 1))
    right = jnp.where(col == cols - 1, 0.0, pltpu.roll(v, cols - 1, 1))
    return v + 0.5 * (left + right)


def smooth_y(h):
    rows = h.shape[0]
    return h + 0.5 * (pltpu.roll(h, 1, 0) + pltpu.roll(h, rows - 1, 0))


def smooth_xy(v):
    return smooth_y(smooth_x(v))


def to_wide(x):
    return jnp.concatenate([x[0:8], x[8:16]], axis=1)


def from_wide(x):
    return jnp.concatenate([x[:, 0:CCOLS], x[:, CCOLS:COLS]], axis=0)


Z1_RHS = 96
Z1_ACC = 160
Z1_CO = 224
Z1_ROWS = 232


def pack_z1(rhs, perm, acc, cperm, plus, minus, across, held, sems):
    first, z = place()
    upward = (first, jnp.logical_not(first), z == LINE - 1)
    copies = [pltpu.make_async_copy(cperm, held, sems.at[0])]
    for out, up in zip((plus, minus, across), upward):
        for base, ref, start, count in (
            (0, perm, jnp.where(up, ROWS, 0), 3),
            (Z1_RHS, rhs, jnp.where(up, 2 * ROWS, 0), 2),
            (Z1_ACC, acc, jnp.where(up, 2 * ROWS, 0), 2),
        ):
            copies.append(
                pltpu.make_async_copy(
                    ref.at[pl.ds(pl.multiple_of(start, ROWS), ROWS * count)],
                    out.at[pl.ds(base, ROWS * count)],
                    sems.at[len(copies)],
                )
            )
    for copy in copies:
        copy.start()
    for copy in copies:
        copy.wait()
    for out, up in zip((plus, minus, across), upward):
        out[Z1_CO : Z1_CO + 8, :] = to_wide(held[jnp.where(up, 1, 0)])


def fine_rows(own, lo, hi, base, depth, z, first, count):
    if z < 0:
        at = base + 32 * (z + depth)
        return lo[at + first : at + first + count, :]
    if z > 3:
        at = base + 32 * (z - 4)
        return hi[at + first : at + first + count, :]
    return own[z, first : first + count, :]


def coarse_plane(cperm, lo, hi, c):
    if c < 0:
        return from_wide(lo[Z1_CO : Z1_CO + 8, :])
    if c > 1:
        return from_wide(hi[Z1_CO : Z1_CO + 8, :])
    return cperm[c]


Y1_RHS = 30
Y1_ACC = 46
Y1_CO = 62
Y1_ROWS = 72


def pack_y1(rhs, perm, acc, cperm, plus, minus, across, up, down):
    lo, hi = below_above(plus, minus, across)
    for out, top in ((up, True), (down, False)):
        r3 = ROWS - 3 if top else 0
        r2 = ROWS - 2 if top else 0
        for k in range(10):
            out[3 * k : 3 * k + 3, :] = fine_rows(perm, lo, hi, 0, 3, k - 3, r3, 3)
        for k in range(8):
            at = Y1_RHS + 2 * k
            out[at : at + 2, :] = fine_rows(rhs, lo, hi, Z1_RHS, 2, k - 2, r2, 2)
            at = Y1_ACC + 2 * k
            out[at : at + 2, :] = fine_rows(acc, lo, hi, Z1_ACC, 2, k - 2, r2, 2)
        rc = CROWS - 1 if top else 0
        for k in range(4):
            plane = coarse_plane(cperm, lo, hi, k - 1)
            at = Y1_CO + k // 2
            lane = CCOLS * (k % 2)
            out[at : at + 1, lane : lane + CCOLS] = plane[rc : rc + 1, :]


def frame_kernel(rhs, perm, acc, cperm, plus, minus, across, ts, rs, cs, ct, hs):
    lo, hi = below_above(plus, minus, across)
    zeros = jnp.zeros((FR, COLS), jnp.float32)
    for k in range(10):
        ts[k] = zeros
        ts[k, 4:36, :] = jnp.sqrt(fine_rows(perm, lo, hi, 0, 3, k - 3, 0, ROWS))
        hs[k] = smooth_x(ts[k])
    for k in range(8):
        for ref, own, base in ((rs, rhs, Z1_RHS), (cs, acc, Z1_ACC)):
            ref[k] = zeros
            ref[k, 4:36, :] = fine_rows(own, lo, hi, base, 2, k - 2, 0, ROWS)
    for k in range(4):
        ct[k] = jnp.zeros((CR, CCOLS), jnp.float32)
        ct[k, 8:24, :] = jnp.sqrt(coarse_plane(cperm, lo, hi, k - 1))


def pre_kernel(
    masks, ts_in, rs_in, cs_in, ct_in, hs_in, cacc, ylo, yhi,
    ts, rs, cs, ct_out, hs, a_out, b_out, u_out, ab_out, plus_out, minus_out, across_out,
    xs, us, ds, fs,
):
    del ts_in, rs_in, cs_in, ct_in, hs_in
    first, place_z = place()
    mlo = masks[0]
    mhi = masks[1]
    for k in range(10):
        ts[k, 1:4, :] = jnp.sqrt(ylo[3 * k : 3 * k + 3, :] * mlo)
        ts[k, 36:39, :] = jnp.sqrt(yhi[3 * k : 3 * k + 3, :] * mhi)
    for k in range(8):
        for ref, ybase in ((rs, Y1_RHS), (cs, Y1_ACC)):
            ref[k, 2:4, :] = ylo[ybase + 2 * k : ybase + 2 * k + 2, :] * mlo
            ref[k, 36:38, :] = yhi[ybase + 2 * k : ybase + 2 * k + 2, :] * mhi
    for k in range(10):
        for tile in (0, 32):
            hs[k, tile : tile + 8, :] = smooth_x(ts[k, tile : tile + 8, :])
        xs[k] = smooth_y(hs[k])
    for k in range(8):
        t = ts[k + 1]
        w = 2.0 * (xs[k + 1] + 0.5 * (xs[k] + xs[k + 2]) - t)
        d = t * w + cs[k]
        d = jnp.where(d > 0.0, d, 1.0)
        q = OMEGA * t / d
        if 2 <= k < 6:
            ds[k - 2] = d
        rs_k = rs[k]
        us[k] = q * rs_k
        cs[k] = q * t
    for k in range(8):
        xs[k] = smooth_xy(us[k])
    for k in range(6):
        a = us[k + 1]
        b = cs[k + 1]
        w = 2.0 * (xs[k + 1] + 0.5 * (xs[k] + xs[k + 2]) - a)
        a_out[k] = a
        b_out[k] = b
        u_out[k] = (1.0 + KEEP) * a + b * w
    for k in range(6):
        xs[k] = smooth_xy(u_out[k])
    sums = []
    for k in range(4):
        u = u_out[k + 1]
        t = ts[k + 3]
        w = 2.0 * (xs[k + 1] + 0.5 * (xs[k] + xs[k + 2]) - u)
        r = rs[k + 2] + t * w - ds[k] * (u / t)
        sums.append(r)
    pairs = []
    for k in range(2):
        both = sums[2 * k] + sums[2 * k + 1]
        halves = []
        for half in range(2):
            at = 2 * k + half
            fs[at] = both[:, CCOLS * half : CCOLS * half + CCOLS]
            halves.append(fs[at, pl.ds(4, CROWS, 2), :] + fs[at, pl.ds(5, CROWS, 2), :])
        pairs.append(jnp.concatenate(halves, axis=1))
    stacked = jnp.concatenate(pairs, axis=0)
    src = lax.broadcasted_iota(jnp.int32, (COLS, CCOLS), 0)
    dst = lax.broadcasted_iota(jnp.int32, (COLS, CCOLS), 1)
    fold = jnp.where(src // 2 == dst, 1.0, 0.0)
    res = jnp.dot(
        stacked, fold, precision=lax.Precision.HIGHEST, preferred_element_type=jnp.float32
    )
    for k in range(4):
        at = Y1_CO + k // 2
        lane = CCOLS * (k % 2)
        ct_out[k, 7:8, :] = jnp.sqrt(ylo[at : at + 1, lane : lane + CCOLS] * mlo)
        ct_out[k, 24:25, :] = jnp.sqrt(yhi[at : at + 1, lane : lane + CCOLS] * mhi)
    cx = [smooth_xy(ct_out[k]) for k in range(4)]
    for k in range(2):
        t = ct_out[k + 1]
        w = 2.0 * (cx[k + 1] + 0.5 * (cx[k] + cx[k + 2]) - t)
        t = t[8:24]
        d = t * w[8:24] + cacc[k]
        q = OMEGA * t / d
        a = q * res[CROWS * k : CROWS * k + CROWS]
        b = q * t
        for out in (ab_out, across_out):
            out[k] = a
            out[2 + k] = b
    for out, up, at in (
        (plus_out, first, 0),
        (minus_out, jnp.logical_not(first), 0),
        (across_out, place_z == LINE - 1, 4),
    ):
        plane = jnp.where(up, 3, 2)
        for k in range(4):
            row = 4 + 16 * (k // 2)
            lane = CCOLS * (k % 2)
            out[at + k] = u_out[plane, row : row + 16, lane : lane + CCOLS]


def pass_on(plus2, minus2, plus, minus, across, plus_out, minus_out):
    del across
    plus_out[0:4] = plus2[...]
    plus_out[4:8] = plus[...]
    minus_out[0:4] = minus2[...]
    minus_out[4:8] = minus[...]


def pack_far(ab, plus1, minus1, out):
    first, z = place()
    near_start = z < LINE // 2
    out[0:2] = ab[0:2]
    out[2] = ab[jnp.where(near_start, 2, 3)]
    out[3:7] = jnp.where(first == near_start, plus1[0:4], minus1[0:4])


Y2_B = 84
Y2_U = 156
Y2_ROWS = 200


def pack_y2(
    ab, u, plus1, minus1, across, plus2, minus2, plus3, minus3, far, up, down, dom, edge
):
    first, z = place()

    def below(plus, minus, k, places, other):
        return jnp.where(z < places, other, jnp.where(first, plus[k], minus[k]))

    def above(plus, minus, k, places, other):
        return jnp.where(z >= LINE - places, other, jnp.where(first, minus[k], plus[k]))

    for k in range(4):
        a = k < 2
        dom[6 + k if a else 17 + k] = ab[k]
        dom[4 + k if a else 15 + k] = below(plus1, minus1, k, 1, across[k])
        dom[8 + k if a else 19 + k] = above(plus1, minus1, k, 1, across[k])
        dom[2 + k if a else 13 + k] = below(plus2, minus2, k, 2, far[3 + k])
        dom[10 + k if a else 21 + k] = above(plus2, minus2, k, 2, far[3 + k])
        edge[k] = below(plus3, minus3, 4 + k, 1, across[4 + k])
        edge[4 + k] = above(plus3, minus3, 4 + k, 1, across[4 + k])
    for k in range(3):
        low = 3 if k == 2 else k
        dom[14 if k == 2 else k] = below(plus3, minus3, low, 3, far[k])
        dom[25 if k == 2 else 12 + k] = above(plus3, minus3, k, 3, far[k])
    for out, top_rows in ((up, True), (down, False)):
        row = CROWS - 6 if top_rows else 0
        for k in range(26):
            out[6 * k : 6 * k + 6, :] = dom[k, row : row + 6, :]
        for k in range(8):
            at = Y2_U + 4 * k
            for half in range(2):
                if 0 < k < 7:
                    row = 34 if top_rows else 4
                    rows = u[k - 1, row : row + 2, CCOLS * half : CCOLS * half + CCOLS]
                else:
                    piece = (0 if k == 0 else 4) + half
                    if top_rows:
                        rows = edge[piece + 2, 14:16, :]
                    else:
                        rows = edge[piece, 0:2, :]
                out[at + 2 * half : at + 2 * half + 2, :] = rows


def window_kernel(u_in, dom, edge, ff, uf):
    for k in range(26):
        ff[k] = jnp.zeros((CR, CCOLS), jnp.float32)
        ff[k, 8:24, :] = dom[k]
    for k in range(8):
        if 0 < k < 7:
            uf[k] = u_in[k - 1]
        else:
            uf[k] = jnp.zeros((FR, COLS), jnp.float32)
            piece = 0 if k == 0 else 4
            for j in range(4):
                row = 4 + 16 * (j // 2)
                lane = CCOLS * (j % 2)
                uf[k, row : row + 16, lane : lane + CCOLS] = edge[piece + j]


def post_kernel(
    masks, ff_in, uf_in, t_in, a_in, b_in, ct, ylo, yhi,
    ff, uf, out, cf, xs,
):
    del ff_in, uf_in
    mlo = masks[0]
    mhi = masks[1]
    a = []
    b = [None]
    for k in range(26):
        ff[k, 2:8, :] = ylo[6 * k : 6 * k + 6, :] * mlo
        ff[k, 24:30, :] = yhi[6 * k : 6 * k + 6, :] * mhi
        (a if k < 14 else b).append(ff[k])
    link = [0.5] * 13
    for j in range(6):
        link[2 * j + 1] = 0.5 * masks[2 + j]
    u = list(a)
    for sweep in range(1, COARSE_SWEEPS):
        first, last = sweep, 13 - sweep
        smooth = {k: smooth_xy(u[k]) for k in range(first - 1, last + 2)}
        fresh = list(u)
        for k in range(first, last + 1):
            w = 2.0 * (
                smooth[k] + link[k - 1] * smooth[k - 1] + link[k] * smooth[k + 1] - u[k]
            )
            fresh[k] = KEEP * u[k] + a[k] + b[k] * w
        u = fresh
    corr = []
    for k in range(4):
        t = ct[k]
        inside = t > 0.0
        corr.append(jnp.where(inside, u[5 + k] / jnp.where(inside, t, 1.0), 0.0))
    stacked = jnp.concatenate(corr, axis=0)
    dst = lax.broadcasted_iota(jnp.int32, (CCOLS, COLS), 1)
    src = lax.broadcasted_iota(jnp.int32, (CCOLS, COLS), 0)
    spread = jnp.where(dst // 2 == src, 1.0, 0.0)
    wide = jnp.dot(
        stacked, spread, precision=lax.Precision.HIGHEST, preferred_element_type=jnp.float32
    )
    for k in range(4):
        for half in range(2):
            rows = wide[CR * k + 6 : CR * k + 26, CCOLS * half : CCOLS * half + CCOLS]
            cf[2 * k + half, pl.ds(0, 20, 2), :] = rows
            cf[2 * k + half, pl.ds(1, 20, 2), :] = rows
    for k in range(8):
        at = Y2_U + 4 * k
        for half in range(2):
            lane = CCOLS * half
            uf[k, 2:4, lane : lane + CCOLS] = ylo[at + 2 * half : at + 2 * half + 2, :] * mlo
            uf[k, 36:38, lane : lane + CCOLS] = yhi[at + 2 * half : at + 2 * half + 2, :] * mhi
        both = 2 * (k // 2)
        uf[k] = uf[k] + t_in[k + 1] * jnp.concatenate([cf[both, 0:FR], cf[both + 1, 0:FR]], axis=1)
    for k in range(8):
        xs[k] = smooth_xy(uf[k])
    for k in range(6):
        v = uf[k + 1]
        w = 2.0 * (xs[k + 1] + 0.5 * (xs[k] + xs[k + 2]) - v)
        uf[k + 1] = KEEP * v + a_in[k] + b_in[k] * w
    for k in range(6):
        xs[k] = smooth_xy(uf[k + 1])
    for k in range(4):
        v = uf[k + 2]
        w = 2.0 * (xs[k + 1] + 0.5 * (xs[k] + xs[k + 2]) - v)
        new = KEEP * v + a_in[k + 1] + b_in[k + 1] * w
        uf[k + 2] = new / t_in[k + 3]
        out[k] = uf[k + 2, 4:36, :]


VM = pl.BlockSpec(memory_space=pltpu.VMEM)
SM = pl.BlockSpec(memory_space=pltpu.SMEM)
HBM = pl.BlockSpec(memory_space=pltpu.HBM)


def f32(*shape):
    return jax.ShapeDtypeStruct(shape, jnp.float32)


def call(kernel, specs, outs, scratch=(), in_place=0):
    return pl.pallas_call(
        kernel,
        input_output_aliases={k + 1: k for k in range(in_place)},
        in_specs=specs,
        out_specs=jax.tree.map(lambda _: VM, outs),
        out_shape=outs,
        scratch_shapes=[
            pltpu.VMEM(shape, jnp.float32) if isinstance(shape, tuple) else shape
            for shape in scratch
        ],
        compiler_params=pltpu.CompilerParams(vmem_limit_bytes=8 * 1024 * 1024),
    )


def frame_call(*operands):
    return call(
        frame_kernel,
        [VM] * 7,
        (
            f32(10, FR, COLS), f32(8, FR, COLS), f32(8, FR, COLS), f32(4, CR, CCOLS),
            f32(10, FR, COLS),
        ),
    )(*operands)


def pre_call(*operands):
    return call(
        pre_kernel,
        [SM] + [VM] * 8,
        (
            f32(10, FR, COLS), f32(8, FR, COLS), f32(8, FR, COLS), f32(4, CR, CCOLS),
            f32(10, FR, COLS), f32(6, FR, COLS), f32(6, FR, COLS), f32(6, FR, COLS), f32(4, CROWS, CCOLS),
            f32(4, CROWS, CCOLS), f32(4, CROWS, CCOLS), f32(8, CROWS, CCOLS),
        ),
        ((10, FR, COLS), (8, FR, COLS), (4, FR, COLS), (4, FR, CCOLS)),
        in_place=5,
    )(*operands)


def window_call(*operands):
    return call(
        window_kernel, [VM] * 3, (f32(26, CR, CCOLS), f32(8, FR, COLS))
    )(*operands)


def post_call(*operands):
    return call(
        post_kernel,
        [SM] + [VM] * 8,
        (f32(26, CR, CCOLS), f32(8, FR, COLS), f32(4, ROWS, COLS)),
        ((8, FR + 8, CCOLS), (8, FR, COLS)),
        in_place=2,
    )(*operands)


def on_device(pressure_rhs, permeability, accumulation, coarse_perm, coarse_accum, run_lengths):
    message = f32(Z1_ROWS, COLS)
    plus, minus, across = call(
        pack_z1,
        [HBM] * 4,
        (message, message, message),
        (pltpu.VMEM((2, CROWS, CCOLS), jnp.float32), pltpu.SemaphoreType.DMA((10,))),
    )(
        *(
            pltpu.with_memory_space_constraint(x, pltpu.HBM)
            for x in (
                pressure_rhs.reshape(-1, COLS),
                permeability.reshape(-1, COLS),
                accumulation.reshape(-1, COLS),
                coarse_perm,
            )
        )
    )
    across = between_lines(across, 1)
    plus = along_lines(plus, 1)
    minus = along_lines(minus, -1)

    slab = lax.axis_index("slab")
    pen = lax.axis_index("pen")
    starts = jnp.cumsum(run_lengths) - run_lengths
    blocks = slab - 2 + jnp.arange(6, dtype=jnp.int32)
    begins = jnp.any(starts[None, :] == blocks[:, None], axis=1)
    masks = jnp.concatenate(
        [
            jnp.stack([pen > 0, pen < lax.axis_size("pen") - 1]).astype(jnp.float32),
            1.0 - begins.astype(jnp.float32),
        ]
    )

    rows = f32(Y1_ROWS, COLS)
    up, down = call(pack_y1, [VM] * 7, (rows, rows))(
        pressure_rhs, permeability, accumulation, coarse_perm, plus, minus, across
    )
    ylo = rotated(up, "pen", 1)
    yhi = rotated(down, "pen", -1)

    frames = frame_call(
        pressure_rhs, permeability, accumulation, coarse_perm, plus, minus, across
    )
    t, _, _, ct, _, a, b, u, ab, plus, minus, across = pre_call(
        masks, *frames, coarse_accum, ylo, yhi
    )
    across = between_lines(across, 1)
    plus1 = along_lines(ab, 1)
    minus1 = along_lines(ab, -1)
    far = between_lines(
        call(pack_far, [VM] * 3, f32(7, CROWS, CCOLS))(ab, plus1, minus1), 3
    )
    plus2 = along_lines(plus1, 1)
    minus2 = along_lines(minus1, -1)
    block = f32(8, CROWS, CCOLS)
    plus, minus = call(pass_on, [VM] * 5, (block, block))(plus2, minus2, plus, minus, across)
    plus3 = along_lines(plus, 1)
    minus3 = along_lines(minus, -1)

    rows = f32(Y2_ROWS, CCOLS)
    up, down, dom, edge = call(
        pack_y2, [VM] * 10, (rows, rows, f32(26, CROWS, CCOLS), f32(8, CROWS, CCOLS))
    )(ab, u, plus1, minus1, across, plus2, minus2, plus3, minus3, far)
    ylo = rotated(up, "pen", 1)
    yhi = rotated(down, "pen", -1)

    return post_call(masks, *window_call(u, dom, edge), t, a, b, ct, ylo, yhi)[2]


def solution(mesh):
    return jax.shard_map(
        on_device,
        mesh=mesh,
        in_specs=(
            P("slab", "pen", None),
            P("slab", "pen", None),
            P("slab", "pen", None),
            P("slab", "pen", None),
            P("slab", "pen", None),
            P(),
        ),
        out_specs=P("slab", "pen", None),
        check_vma=False,
    )
```
